32 devices in a mesh: member: 2 (over core), slab: 16 (over z, y, x).
Axes of the slice: x: 2, y: 2, z: 4, core: 2. Of those that a mesh axis runs over, the one named last changes fastest.
Arguments:
- base_field: bfloat16 [32, 512, 2, 512], P(None, 'slab'), may hold values from -6 to 6
- forcing: bfloat16 [512, 2, 512], P('slab'), may hold values from -6 to 6
- load: float32 [32], replicated, may hold values from 0.25 to 1.75
- amplitudes: float32 [16], replicated, may hold values from 0.25 to 2
- amp_index: int32 [2], P('member'), may hold values from 0 to 15
- mode_count: int32 [2], P('member'), may hold values from 32 to 64, as said below
- point_weight: bfloat16 [32, 32], replicated, may hold values from -1 to 1
- point_bias: float32 [32], replicated, may hold values from -3 to 3
- spectral_weight: bfloat16 [64, 64, 2, 32, 32], P('slab'), may hold values from -6 to 6
Outputs:
- dependence: bfloat16 [32, 512, 2, 512], P('member', 'slab')
The draws below stay inside these ranges and needn't reach their ends.
Inputs may be any that keep to these rules, and one draw needn't show every extreme that they name: `mode_count`: each member keeps the second-dimension modes below its count; some member keeps all 64.
All inputs are finite; a program needn't handle non-finite values.
Results may differ from the reference program's by a relative error of at most 0.015.
Values may be sent and summed in bfloat16 or wider, within the bound.
No kernel may reach another device: no remote copies, remote signals or barrier semaphores. Data moves between devices by JAX's collectives and lax.ppermute only.
A program may use at most 64 MiB of HBM per device.

```python
import math
import jax
import jax.numpy as jnp
from jax import lax

C = 32
NX = 512
NY = 512
KX = 64
KY = 64
ZP = 2
LEVELS = 16
MEMBERS = 2


def draw_mode_count(key, part):
    count_key = jax.random.fold_in(key, 11)
    order_key = jax.random.fold_in(key, 23)
    counts = jax.random.randint(count_key, (MEMBERS,), KY // 2, KY + 1)
    order = jax.random.permutation(order_key, MEMBERS)
    counts = counts.at[order[0]].set(KY)
    if MEMBERS > 2:
        counts = counts.at[order[1]].set(KY // 2)
    return counts.astype(jnp.int32)


def block_levels(key, extent, cuts, least, largest):
    def one(dim, shards_of):
        heights = jax.random.uniform(jax.random.fold_in(jax.random.fold_in(key, 6), dim), (shards_of,), jnp.float32, least / len(cuts), largest / len(cuts))
        return jnp.repeat(jnp.exp(heights), extent[dim] // shards_of).reshape((-1,) + (1,) * (len(extent) - dim - 1))

    factor_of = one(*cuts[0])
    for cut in cuts[1:]:
        factor_of = factor_of * one(*cut)
    return factor_of


def centred(stream_key, extent, deviation, reach, pieces=(), held_as=jnp.bfloat16):
    level = block_levels(stream_key, extent, pieces, -0.22, 0.18) if pieces else 1.0
    drawn = jax.random.normal(stream_key, extent, jnp.float32) * deviation * level
    return jnp.minimum(jnp.maximum(drawn, -reach), reach).astype(held_as)


def setup_inputs(seed: int = 0) -> dict:
    key_of = jax.random.split(jax.random.key(seed), 10)
    return {
        "base_field": centred(key_of[0], (C, NX, ZP, NY), 1.0, 6.0, ((1, 16),)),
        "forcing": centred(key_of[1], (NX, ZP, NY), 1.0, 6.0, ((0, 16),)),
        "load": jnp.clip(1.0 + 0.15 * jax.random.normal(key_of[2], (C,), jnp.float32), 0.25, 1.75),
        "amplitudes": jnp.clip(jnp.exp(jax.random.uniform(key_of[3], (LEVELS,), jnp.float32, math.log(0.25), math.log(2.0))), 0.25, 2.0),
        "amp_index": jax.random.randint(key_of[4], (MEMBERS,), 0, LEVELS).astype(jnp.int32),
        "mode_count": draw_mode_count(jax.random.fold_in(key_of[9], 71), 0),
        "point_weight": centred(key_of[6], (C, C), C ** -0.5, 1.0),
        "point_bias": centred(key_of[7], (C,), 0.5, 3.0, (), jnp.float32),
        "spectral_weight": centred(key_of[8], (KY, KX, 2, C, C), (max(1, NX * NY // (2 * C * KX * KY))) ** -0.5, 6.0, ((0, 16),)),
    }


TWO_PI = 2.0 * math.pi


def phases(frequency, positions, length):
    product = (frequency[:, None] * positions[None, :]) % length
    angles = product.astype(jnp.float32) * (TWO_PI / length)
    return jnp.cos(angles), jnp.sin(angles)


def rounded(values):
    return lax.optimization_barrier(values.astype(jnp.bfloat16)).astype(jnp.float32)


def reference(base_field, forcing, load, amplitudes, amp_index, mode_count, point_weight, point_bias, spectral_weight):
    y_cos, y_sin = phases(jnp.arange(KY, dtype=jnp.int32), jnp.arange(NY, dtype=jnp.int32), NY)
    fwd_cos_y = y_cos.astype(jnp.bfloat16).astype(jnp.float32)
    fwd_sin_y = y_sin.astype(jnp.bfloat16).astype(jnp.float32)
    scale_y = jnp.where(jnp.arange(KY) == 0, 1.0, 2.0).astype(jnp.float32) / (NX * NY)
    inv_cos_y = (scale_y[:, None] * y_cos).astype(jnp.bfloat16).astype(jnp.float32)
    inv_sin_y = (scale_y[:, None] * y_sin).astype(jnp.bfloat16).astype(jnp.float32)
    frequency_x = jnp.concatenate([jnp.arange(KX // 2, dtype=jnp.int32), jnp.arange(NX - KX // 2, NX, dtype=jnp.int32)])
    x_cos, x_sin = phases(frequency_x, jnp.arange(NX, dtype=jnp.int32), NX)
    x_cos = x_cos.astype(jnp.bfloat16).astype(jnp.float32)
    x_sin = x_sin.astype(jnp.bfloat16).astype(jnp.float32)
    weight_f = point_weight.astype(jnp.float32)
    spec_f = spectral_weight.astype(jnp.float32)
    weight_real = spec_f[:, :, 0]
    weight_imag = spec_f[:, :, 1]
    base_f = base_field.astype(jnp.float32)
    forcing_f = forcing.astype(jnp.float32)
    levels = amplitudes[amp_index]

    def mixing(weights, values):
        return jnp.einsum("kmoi,kmiz->kmoz", weights, values)

    def member_step(total, member_data):
        amplitude, keep_count = member_data
        driven = base_f + amplitude * load[:, None, None, None] * forcing_f[None]
        field_now = (2.0 * jnp.tanh(0.5 * driven)).astype(jnp.bfloat16)
        field_f = field_now.astype(jnp.float32)
        y_real = jnp.einsum("cxzy,ky->kxcz", field_f, fwd_cos_y)
        y_imag = -jnp.einsum("cxzy,ky->kxcz", field_f, fwd_sin_y)
        packed = rounded(jnp.stack([y_real, y_imag], axis=2))
        with_cos = jnp.einsum("kxrcz,mx->kmrcz", packed, x_cos)
        with_sin = jnp.einsum("kxrcz,mx->kmrcz", packed, x_sin)
        spec_real = rounded(with_cos[:, :, 0] + with_sin[:, :, 1])
        spec_imag = rounded(with_cos[:, :, 1] - with_sin[:, :, 0])
        mix_real = mixing(weight_real, spec_real) - mixing(weight_imag, spec_imag)
        mix_imag = mixing(weight_real, spec_imag) + mixing(weight_imag, spec_real)
        keep = (jnp.arange(KY, dtype=jnp.int32) < keep_count).astype(jnp.float32)[:, None, None, None]
        mix_real = rounded(mix_real * keep)
        mix_imag = rounded(mix_imag * keep)
        back_real = rounded(jnp.einsum("kmoz,mx->kxoz", mix_real, x_cos) - jnp.einsum("kmoz,mx->kxoz", mix_imag, x_sin))
        back_imag = rounded(jnp.einsum("kmoz,mx->kxoz", mix_imag, x_cos) + jnp.einsum("kmoz,mx->kxoz", mix_real, x_sin))
        spectral = jnp.einsum("kxcz,ky->cxzy", back_real, inv_cos_y) - jnp.einsum("kxcz,ky->cxzy", back_imag, inv_sin_y)
        pointwise = jnp.einsum("oc,cxzy->oxzy", weight_f, field_f) + point_bias[:, None, None, None]
        layer = rounded(jax.nn.gelu(pointwise + spectral, approximate=True))
        return total + layer, None

    total, _ = lax.scan(member_step, jnp.zeros((C, NX, ZP, NY), jnp.float32), (levels, mode_count))
    return (total / MEMBERS).astype(jnp.bfloat16)
```

```python
import math

import jax
import jax.numpy as jnp
from jax import lax
from jax.sharding import PartitionSpec as P

TWO_PI = 2.0 * math.pi


def phases(frequency, positions, length):
    product = frequency[:, None] * positions[None, :] % length
    angles = product.astype(jnp.float32) * (TWO_PI / length)
    return (jnp.cos(angles), jnp.sin(angles))


def forward_x(pencil, cos_table, sin_table):
    row_total = pencil.shape[0]
    modes = cos_table.shape[0]
    with_cos = jnp.einsum(
        "kxf,mx->kmf", pencil, cos_table, preferred_element_type=jnp.float32
    ).reshape(row_total, modes, 2, -1)
    with_sin = jnp.einsum(
        "kxf,mx->kmf", pencil, sin_table, preferred_element_type=jnp.float32
    ).reshape(row_total, modes, 2, -1)
    real_part = with_cos[:, :, 0] + with_sin[:, :, 1]
    imag_part = with_cos[:, :, 1] - with_sin[:, :, 0]
    return jnp.stack([real_part, imag_part], axis=2).reshape(row_total, modes, -1)


def inverse_x(spectra, cos_table, sin_table):
    row_total = spectra.shape[0]
    points = cos_table.shape[1]
    with_cos = jnp.einsum(
        "kmf,mx->kxf", spectra, cos_table, preferred_element_type=jnp.float32
    ).reshape(row_total, points, 2, -1)
    with_sin = jnp.einsum(
        "kmf,mx->kxf", spectra, sin_table, preferred_element_type=jnp.float32
    ).reshape(row_total, points, 2, -1)
    real_part = with_cos[:, :, 0] - with_sin[:, :, 1]
    imag_part = with_cos[:, :, 1] + with_sin[:, :, 0]
    return jnp.stack([real_part, imag_part], axis=2).reshape(row_total, points, -1)


def mixing(weights, values):
    return jnp.einsum("kmoi,kmiz->kmoz", weights, values, preferred_element_type=jnp.float32)


def local(
    base_field,
    forcing,
    load,
    amplitudes,
    amp_index,
    mode_count,
    point_weight,
    point_bias,
    spectral_weight,
):
    channels, slab_rows, plane_count, length_y = base_field.shape
    slab_count = lax.axis_size("slab")
    local_modes = spectral_weight.shape[0]
    modes_y = local_modes * slab_count
    modes_x = spectral_weight.shape[1]
    length_x = slab_rows * slab_count
    packed_width = 2 * channels * plane_count
    slab_index = lax.axis_index("slab")
    level_ids = jnp.arange(amplitudes.shape[0], dtype=jnp.int32)
    amplitude = jnp.sum(jnp.where(level_ids == amp_index[0], amplitudes, 0.0))
    driven = base_field.astype(jnp.float32) + amplitude * load[:, None, None, None] * forcing[
        None
    ].astype(jnp.float32)
    field_now = (2.0 * jnp.tanh(0.5 * driven)).astype(jnp.bfloat16)
    y_cos, y_sin = phases(
        jnp.arange(modes_y, dtype=jnp.int32), jnp.arange(length_y, dtype=jnp.int32), length_y
    )
    y_real = jnp.einsum(
        "cxzy,ky->kxcz", field_now, y_cos.astype(jnp.bfloat16), preferred_element_type=jnp.float32
    )
    y_imag = -jnp.einsum(
        "cxzy,ky->kxcz", field_now, y_sin.astype(jnp.bfloat16), preferred_element_type=jnp.float32
    )
    packed = (
        jnp.stack([y_real, y_imag], axis=2)
        .astype(jnp.bfloat16)
        .reshape(modes_y, slab_rows, packed_width)
    )
    frequency_x = jnp.concatenate(
        [
            jnp.arange(modes_x // 2, dtype=jnp.int32),
            jnp.arange(length_x - modes_x // 2, length_x, dtype=jnp.int32),
        ]
    )
    full_cos, full_sin = phases(frequency_x, jnp.arange(length_x, dtype=jnp.int32), length_x)
    full_cos = full_cos.astype(jnp.bfloat16)
    full_sin = full_sin.astype(jnp.bfloat16)
    pencil = lax.all_to_all(packed, "slab", split_axis=0, concat_axis=1, tiled=True)
    spectrum = forward_x(pencil, full_cos, full_sin)
    spectrum = spectrum.astype(jnp.bfloat16).reshape(local_modes, modes_x, 2, channels, plane_count)
    weight_real = spectral_weight[:, :, 0]
    weight_imag = spectral_weight[:, :, 1]
    spec_real = spectrum[:, :, 0]
    spec_imag = spectrum[:, :, 1]
    mix_real = mixing(weight_real, spec_real) - mixing(weight_imag, spec_imag)
    mix_imag = mixing(weight_real, spec_imag) + mixing(weight_imag, spec_real)
    global_modes = slab_index * local_modes + jnp.arange(local_modes, dtype=jnp.int32)
    keep = (global_modes < mode_count[0]).astype(jnp.float32)[:, None, None, None, None]
    mixed = (
        (jnp.stack([mix_real, mix_imag], axis=2) * keep)
        .astype(jnp.bfloat16)
        .reshape(local_modes, modes_x, packed_width)
    )
    back = inverse_x(mixed, full_cos, full_sin).astype(jnp.bfloat16)
    returned = lax.all_to_all(back, "slab", split_axis=1, concat_axis=0, tiled=True)
    returned = returned.reshape(modes_y, slab_rows, 2, channels, plane_count)
    weights_y = jnp.where(jnp.arange(modes_y) == 0, 1.0, 2.0).astype(jnp.float32) / (
        length_x * length_y
    )
    back_cos = (weights_y[:, None] * y_cos).astype(jnp.bfloat16)
    back_sin = (weights_y[:, None] * y_sin).astype(jnp.bfloat16)
    spectral = jnp.einsum(
        "kxcz,ky->cxzy", returned[:, :, 0], back_cos, preferred_element_type=jnp.float32
    )
    spectral = spectral - jnp.einsum(
        "kxcz,ky->cxzy", returned[:, :, 1], back_sin, preferred_element_type=jnp.float32
    )
    pointwise = (
        jnp.einsum("oc,cxzy->oxzy", point_weight, field_now, preferred_element_type=jnp.float32)
        + point_bias[:, None, None, None]
    )
    layer = jax.nn.gelu(pointwise + spectral, approximate=True).astype(jnp.bfloat16)
    layer = lax.optimization_barrier(layer).astype(jnp.float32)
    total = lax.psum_scatter(
        layer.astype(jnp.bfloat16), "member", scatter_dimension=0, tiled=True
    ).astype(jnp.float32)
    return (total / lax.axis_size("member")).astype(jnp.bfloat16)


def solution(mesh):
    in_specs = (
        P(None, "slab", None, None),
        P("slab", None, None),
        P(),
        P(),
        P("member"),
        P("member"),
        P(),
        P(),
        P("slab", None, None, None, None),
    )
    out_specs = P("member", "slab", None, None)
    return jax.shard_map(local, mesh=mesh, in_specs=in_specs, out_specs=out_specs, check_vma=False)
```

```python
import math

import jax
import jax.numpy as jnp
import numpy as np
from jax import lax
from jax.experimental import pallas as pl
from jax.experimental.pallas import tpu as pltpu
from jax.sharding import PartitionSpec as P

TWO_PI = 2.0 * math.pi
LANES = 128
SUBLANES = 8
SMEM = pltpu.SMEM
F32 = jnp.float32
BF16 = jnp.bfloat16


def host_phases(frequency, positions, length):
    product = frequency[:, None] * positions[None, :] % length
    angles = product.astype(np.float32) * np.float32(TWO_PI / length)
    return np.cos(angles), np.sin(angles)


def first_frequencies(modes_x, length_x):
    return np.concatenate([np.arange(modes_x // 2), np.arange(length_x - modes_x // 2, length_x)])


def as_bf16(table):
    return jnp.asarray(table.astype(BF16))


def forward_y_table(modes_y, length_y):
    cos, sin = host_phases(np.arange(modes_y), np.arange(length_y), length_y)
    return as_bf16(np.concatenate([cos, -sin], axis=0))


def inverse_y_table(modes_y, length_y, length_x, slabs):
    cos, sin = host_phases(np.arange(modes_y), np.arange(length_y), length_y)
    scale = np.where(np.arange(modes_y) == 0, 1.0, 2.0).astype(np.float32)
    scale = (scale / np.float32(length_x * length_y))[:, None]
    parts = np.stack([scale * cos, -(scale * sin)], axis=0)
    parts = parts.reshape(2, slabs, modes_y // slabs, length_y).transpose(1, 0, 2, 3)
    return as_bf16(parts.reshape(2 * modes_y, length_y))


def forward_x_table(modes_x, length_x, slabs, planes):
    cos, sin = host_phases(first_frequencies(modes_x, length_x), np.arange(length_x), length_x)
    whole = np.array([[cos, -sin], [sin, cos]])
    whole = whole.reshape(2, 2, modes_x, slabs, length_x // slabs)
    table = np.einsum("abqsx,zw->sazxwbq", whole, np.eye(planes, dtype=np.float32))
    return as_bf16(table.reshape(2 * planes * length_x, planes * 2 * modes_x))


def inverse_x_table(modes_x, length_x, slabs, planes):
    cos, sin = host_phases(first_frequencies(modes_x, length_x), np.arange(length_x), length_x)
    whole = np.array([cos, -sin]).reshape(2, modes_x, slabs, length_x // slabs)
    table = np.einsum("aqsx,zw->zaqswx", whole, np.eye(planes, dtype=np.float32))
    return as_bf16(table.reshape(planes * 2 * modes_x, planes * length_x))


def low_half(shape):
    return lax.broadcasted_iota(jnp.int32, shape, len(shape) - 1) < shape[-1] // 2


def half_turn(values):
    return pltpu.roll(values, values.shape[-1] // 2, values.ndim - 1)


def pair_halves(first, second):
    low = low_half(first.shape)
    return (
        jnp.where(low, first, half_turn(second)),
        jnp.where(low, half_turn(first), second),
    )


def driven_field(base, forcing, strength):
    return 2.0 * jnp.tanh(0.5 * (base.astype(F32) + strength * forcing))


def y_modes_kernel(
    index_ref, amplitude_ref, load_ref, base_ref, forcing_ref, table_ref, out_ref, cells, rows, modes
):
    group = pl.program_id(0)
    width, cell_rows, _ = base_ref.shape
    planes, y_blocks, slab_rows = Y_LAYOUT(cell_rows, table_ref.shape[1])
    channels = load_ref.shape[0]
    modes_y = table_ref.shape[0] // 2
    amplitude = amplitude_ref[index_ref[0]]
    forcing = forcing_ref[...].astype(F32)
    span = planes * slab_rows
    for c in range(width):
        cells[c] = driven_field(base_ref[c], forcing, amplitude * load_ref[group * width + c])
        for z in range(planes):
            for j in range(y_blocks):
                picked = cells[c, pl.ds(j * planes + z, slab_rows, stride=planes * y_blocks), :]
                rows[
                    pl.ds(c * span + z * slab_rows, slab_rows), pl.ds(j * LANES, LANES)
                ] = picked.astype(BF16)
    result = lax.dot_general(
        table_ref[...], rows[...], (((1,), (1,)), ((), ())), preferred_element_type=F32
    )
    for t in range(width // 2):
        tile = slice(t * LANES, (t + 1) * LANES)
        pair = pair_halves(result[:modes_y, tile], result[modes_y:, tile])
        for n in range(2):
            modes[pl.ds(group * width + 2 * t + n, modes_y, stride=channels), :] = pair[n]

    @pl.when(group == pl.num_programs(0) - 1)
    def _():
        block_rows = out_ref.shape[1]
        for d in range(out_ref.shape[0]):
            out_ref[d] = modes[pl.ds(d * block_rows, block_rows), :].astype(BF16)


def Y_LAYOUT(cell_rows, length_y):
    y_blocks = length_y // LANES
    planes = SUBLANES // y_blocks
    return planes, y_blocks, cell_rows // SUBLANES


def y_modes(amp_index, amplitudes, load, cells, forcing, slabs, modes_y, length_y):
    channels, cell_rows, _ = cells.shape
    width = 4
    block_rows = modes_y // slabs * channels
    table = forward_y_table(modes_y, length_y)
    planes, y_blocks, slab_rows = Y_LAYOUT(cell_rows, length_y)
    smem = pl.BlockSpec(memory_space=SMEM)
    return pl.pallas_call(
        y_modes_kernel,
        grid=(channels // width,),
        in_specs=[
            smem,
            smem,
            smem,
            pl.BlockSpec((width, cell_rows, LANES), lambda g: (g, 0, 0)),
            pl.BlockSpec((cell_rows, LANES), lambda g: (0, 0)),
            pl.BlockSpec(table.shape, lambda g: (0, 0)),
        ],
        out_specs=pl.BlockSpec((slabs, block_rows, LANES), lambda g: (0, 0, 0)),
        out_shape=jax.ShapeDtypeStruct((slabs, block_rows, LANES), BF16),
        scratch_shapes=[
            pltpu.VMEM((width, cell_rows, LANES), F32),
            pltpu.VMEM((width * planes * slab_rows, length_y), BF16),
            pltpu.VMEM((modes_y * channels, LANES), F32),
        ],
        compiler_params=pltpu.CompilerParams(vmem_limit_bytes=32 * 1024 * 1024),
        cost_estimate=pl.CostEstimate(
            flops=4 * modes_y * cells.size, bytes_accessed=4 * cells.size, transcendentals=cells.size
        ),
        name="y_modes",
    )(amp_index, amplitudes, load, cells, forcing, table)


def mix_kernel(
    limit_ref, pencil_ref, forward_ref, straight_ref, crossed_ref, inverse_ref, out_ref, spectrum, turned, mixed
):
    slabs, block_rows, _ = pencil_ref.shape
    local_modes, channels, _, width = straight_ref.shape
    planes = forward_ref.shape[1] // width
    groups = channels // SUBLANES
    pencil = jnp.concatenate([pencil_ref[s] for s in range(slabs)], axis=1)
    result = jnp.dot(pencil, forward_ref[...], preferred_element_type=F32)
    for z in range(planes):
        part = result[:, z * width : (z + 1) * width]
        spectrum[z] = part
        turned[z] = half_turn(part)
    low = low_half((SUBLANES, width))
    block = SUBLANES * 2 * local_modes
    for k in range(local_modes):
        keep = jnp.where(limit_ref[0] > k, 1.0, 0.0).astype(F32)
        sums = [[jnp.zeros((SUBLANES, width), F32) for _ in range(groups)] for _ in range(planes)]
        for i in range(channels):
            row = pl.ds(k * channels + i, 1)
            plain = [jnp.broadcast_to(spectrum[z, row, :], (SUBLANES, width)) for z in range(planes)]
            other = [jnp.broadcast_to(turned[z, row, :], (SUBLANES, width)) for z in range(planes)]
            for g in range(groups):
                straight = straight_ref[k, i, pl.ds(g * SUBLANES, SUBLANES), :]
                crossed = crossed_ref[k, i, pl.ds(g * SUBLANES, SUBLANES), :]
                for z in range(planes):
                    sums[z][g] = sums[z][g] + (straight * plain[z] + crossed * other[z])
        for z in range(planes):
            for g in range(groups):
                kept = sums[z][g] * keep
                swapped = half_turn(kept)
                start = g * block + k
                mixed[z, pl.ds(start, SUBLANES, stride=2 * local_modes), :] = kept
                mixed[z, pl.ds(start + local_modes, SUBLANES, stride=2 * local_modes), :] = jnp.where(
                    low, swapped, -swapped
                )
    left = jnp.concatenate([mixed[z].astype(BF16) for z in range(planes)], axis=1)
    back = jnp.dot(left, inverse_ref[...], preferred_element_type=F32)
    members = out_ref.shape[0] // slabs
    for h in range(members):
        for t in range(slabs // 2):
            tile = slice(t * LANES, (t + 1) * LANES)
            start = 2 * h * block
            pair = pair_halves(back[start : start + block, tile], back[start + block : start + 2 * block, tile])
            for n in range(2):
                out_ref[h * slabs + 2 * t + n] = pair[n].astype(BF16)


def mix(limit, pencil, straight, crossed, length_x, planes, members):
    slabs, block_rows, _ = pencil.shape
    local_modes, channels, _, width = straight.shape
    modes_x = width // 2
    forward = forward_x_table(modes_x, length_x, slabs, planes)
    inverse = inverse_x_table(modes_x, length_x, slabs, planes)
    vmem = pl.BlockSpec(memory_space=pltpu.VMEM)
    block = SUBLANES * 2 * local_modes
    return pl.pallas_call(
        mix_kernel,
        in_specs=[pl.BlockSpec(memory_space=SMEM)] + [vmem] * 5,
        out_specs=vmem,
        out_shape=jax.ShapeDtypeStruct((members * slabs, block, LANES), BF16),
        scratch_shapes=[
            pltpu.VMEM((planes, block_rows, width), F32),
            pltpu.VMEM((planes, block_rows, width), F32),
            pltpu.VMEM((planes, channels // SUBLANES * block, width), F32),
        ],
        compiler_params=pltpu.CompilerParams(vmem_limit_bytes=40 * 1024 * 1024),
        cost_estimate=pl.CostEstimate(
            flops=2 * block_rows * forward.size, bytes_accessed=8 * straight.size, transcendentals=0
        ),
        name="mix",
    )(limit, pencil, forward, straight, crossed, inverse)


def pointwise_kernel(
    place_ref, index_ref, amplitude_ref, load_ref, bias_ref, base_ref, forcing_ref, weight_ref, out_ref
):
    channels, depth, _ = base_ref.shape
    members = index_ref.shape[0]
    me = place_ref[0]
    forcing = forcing_ref[...].astype(F32)
    fields = []
    for m in range(members):
        amplitude = amplitude_ref[index_ref[lax.rem(me - m + members, members)]]
        parts = [
            driven_field(base_ref[c], forcing, amplitude * load_ref[c]).astype(BF16) for c in range(channels)
        ]
        fields.append(jnp.concatenate(parts, axis=0))
    result = jnp.dot(weight_ref[...], jnp.concatenate(fields, axis=1), preferred_element_type=F32)
    _, outer, inner, _, _ = out_ref.shape
    for a in range(outer):
        for b in range(inner):
            o = a * inner + b
            bias = bias_ref[me * outer * inner + o]
            for m in range(members):
                out_ref[m, a, b] = result[o * depth : (o + 1) * depth, m * LANES : (m + 1) * LANES] + bias


def pointwise(place, indices, amplitudes, load, bias, cells, forcing, weight):
    channels, cell_rows, _ = cells.shape
    members = indices.shape[0]
    depth = 2 * SUBLANES
    inner = SUBLANES
    outer = channels // members // inner
    spread = (weight[:, None, :, None] * jnp.eye(depth, dtype=BF16)[None, :, None, :]).reshape(
        weight.shape[0] * depth, channels * depth
    )
    smem = pl.BlockSpec(memory_space=SMEM)
    return pl.pallas_call(
        pointwise_kernel,
        grid=(cell_rows // depth,),
        in_specs=[smem] * 5
        + [
            pl.BlockSpec((channels, depth, LANES), lambda r: (0, r, 0)),
            pl.BlockSpec((depth, LANES), lambda r: (r, 0)),
            pl.BlockSpec(spread.shape, lambda r: (0, 0)),
        ],
        out_specs=pl.BlockSpec((members, outer, inner, depth, LANES), lambda r: (0, 0, 0, r, 0)),
        out_shape=jax.ShapeDtypeStruct((members, outer, inner, cell_rows, LANES), F32),
        compiler_params=pltpu.CompilerParams(vmem_limit_bytes=32 * 1024 * 1024),
        cost_estimate=pl.CostEstimate(
            flops=4 * spread.size * members * cell_rows // depth * LANES,
            bytes_accessed=8 * cells.size,
            transcendentals=members * cells.size,
        ),
        name="pointwise",
    )(place, indices, amplitudes, load, bias, cells, forcing, spread)


def layer_kernel(back_ref, table_ref, point_ref, out_ref, columns, spectral):
    step = pl.program_id(0)
    members, outer, _, cell_rows, _ = point_ref.shape
    sources, block_rows, _ = back_ref.shape
    slabs = sources // members
    inner = columns.shape[0]
    depth = block_rows // inner
    planes, y_blocks, slab_rows = Y_LAYOUT(cell_rows, table_ref.shape[1])

    @pl.when(step == 0)
    def _():
        for m in range(members):
            for s in range(slabs):
                block = back_ref[m * slabs + s].astype(F32)
                for b in range(inner):
                    columns[b, m, pl.ds(s * depth, depth), :] = block[b * depth : (b + 1) * depth]

    for m in range(members):
        left = columns[step, m].astype(BF16)
        values = lax.dot_general(
            left, table_ref[...], (((0,), (0,)), ((), ())), preferred_element_type=F32
        )
        for a in range(outer):
            for z in range(planes):
                start = (a * planes + z) * slab_rows
                for j in range(y_blocks):
                    spectral[m, a, pl.ds(j * planes + z, slab_rows, stride=planes * y_blocks), :] = values[
                        start : start + slab_rows, j * LANES : (j + 1) * LANES
                    ]
    for a in range(outer):
        total = None
        for m in range(members):
            value = jax.nn.gelu(point_ref[m, a, 0] + spectral[m, a], approximate=True)
            total = value if total is None else total + value
        out_ref[a, 0] = (total * (1.0 / members)).astype(BF16)


def layer(back, points, length_x, length_y, modes_y):
    members, outer, inner, cell_rows, _ = points.shape
    slabs = back.shape[0] // members
    table = inverse_y_table(modes_y, length_y, length_x, slabs)
    return pl.pallas_call(
        layer_kernel,
        grid=(inner,),
        in_specs=[
            pl.BlockSpec(back.shape, lambda b: (0, 0, 0)),
            pl.BlockSpec(table.shape, lambda b: (0, 0)),
            pl.BlockSpec((members, outer, 1, cell_rows, LANES), lambda b: (0, 0, b, 0, 0)),
        ],
        out_specs=pl.BlockSpec((outer, 1, cell_rows, LANES), lambda b: (0, b, 0, 0)),
        out_shape=jax.ShapeDtypeStruct((outer, inner, cell_rows, LANES), BF16),
        scratch_shapes=[
            pltpu.VMEM((inner, members, 2 * modes_y, LANES), F32),
            pltpu.VMEM((members, outer, cell_rows, LANES), F32),
        ],
        compiler_params=pltpu.CompilerParams(vmem_limit_bytes=32 * 1024 * 1024),
        cost_estimate=pl.CostEstimate(
            flops=4 * modes_y * points.size, bytes_accessed=5 * points.size, transcendentals=points.size
        ),
        name="layer",
    )(back, table, points)


def fast_local(
    base_field,
    forcing,
    load,
    amplitudes,
    amp_index,
    mode_count,
    point_weight,
    point_bias,
    spectral_weight,
):
    channels, slab_rows, planes, length_y = base_field.shape
    slabs, members = lax.axis_size("slab"), lax.axis_size("member")
    local_modes, modes_x = spectral_weight.shape[:2]
    modes_y = local_modes * slabs
    length_x = slab_rows * slabs
    y_blocks = length_y // LANES
    cells = base_field.reshape(channels, slab_rows, planes, y_blocks, LANES).transpose(0, 1, 3, 2, 4)
    cells = cells.reshape(channels, slab_rows * SUBLANES, LANES)
    force = forcing.reshape(slab_rows, planes, y_blocks, LANES).transpose(0, 2, 1, 3)
    force = force.reshape(slab_rows * SUBLANES, LANES)
    me = lax.axis_index("member")
    indices = jnp.concatenate(
        [amp_index]
        + [
            lax.ppermute(amp_index, "member", [(s, (s + r) % members) for s in range(members)])
            for r in range(1, members)
        ]
    )
    out_channels = channels // members
    packed = y_modes(amp_index, amplitudes, load, cells, force, slabs, modes_y, length_y)
    pencil = lax.all_to_all(packed, "slab", split_axis=0, concat_axis=0, tiled=True)
    weights = spectral_weight.transpose(0, 2, 4, 3, 1).astype(F32)
    straight = jnp.concatenate([weights[:, 0], weights[:, 0]], axis=-1)
    crossed = jnp.concatenate([-weights[:, 1], weights[:, 1]], axis=-1)
    limit = mode_count - lax.axis_index("slab") * local_modes
    back = mix(limit, pencil, straight, crossed, length_x, planes, members)
    back = lax.all_to_all(back, ("member", "slab"), split_axis=0, concat_axis=0, tiled=True)
    weight = lax.dynamic_slice_in_dim(point_weight, me * out_channels, out_channels, 0)
    points = pointwise(me.reshape(1), indices, amplitudes, load, point_bias, cells, force, weight)
    result = layer(back, points, length_x, length_y, modes_y)
    result = result.reshape(out_channels, slab_rows, y_blocks, planes, LANES).transpose(0, 1, 3, 2, 4)
    return result.reshape(out_channels, slab_rows, planes, length_y)


def tiles_fit(base_shape, weight_shape, slabs, members):
    channels, slab_rows, planes, length_y = base_shape
    local_modes, modes_x = weight_shape[:2]
    return (
        2 * planes * slab_rows == LANES
        and 2 * modes_x == LANES
        and planes * length_y == SUBLANES * LANES
        and 2 * local_modes == SUBLANES
        and 2 * SUBLANES * members == channels
        and slabs % 2 == 0
    )


def phases(frequency, positions, length):
    product = frequency[:, None] * positions[None, :] % length
    angles = product.astype(jnp.float32) * (TWO_PI / length)
    return (jnp.cos(angles), jnp.sin(angles))


def forward_x(pencil, cos_table, sin_table):
    row_total = pencil.shape[0]
    modes = cos_table.shape[0]
    with_cos = jnp.einsum(
        "kxf,mx->kmf", pencil, cos_table, preferred_element_type=jnp.float32
    ).reshape(row_total, modes, 2, -1)
    with_sin = jnp.einsum(
        "kxf,mx->kmf", pencil, sin_table, preferred_element_type=jnp.float32
    ).reshape(row_total, modes, 2, -1)
    real_part = with_cos[:, :, 0] + with_sin[:, :, 1]
    imag_part = with_cos[:, :, 1] - with_sin[:, :, 0]
    return jnp.stack([real_part, imag_part], axis=2).reshape(row_total, modes, -1)


def inverse_x(spectra, cos_table, sin_table):
    row_total = spectra.shape[0]
    points = cos_table.shape[1]
    with_cos = jnp.einsum(
        "kmf,mx->kxf", spectra, cos_table, preferred_element_type=jnp.float32
    ).reshape(row_total, points, 2, -1)
    with_sin = jnp.einsum(
        "kmf,mx->kxf", spectra, sin_table, preferred_element_type=jnp.float32
    ).reshape(row_total, points, 2, -1)
    real_part = with_cos[:, :, 0] - with_sin[:, :, 1]
    imag_part = with_cos[:, :, 1] + with_sin[:, :, 0]
    return jnp.stack([real_part, imag_part], axis=2).reshape(row_total, points, -1)


def mixing(weights, values):
    return jnp.einsum("kmoi,kmiz->kmoz", weights, values, preferred_element_type=jnp.float32)


def general_local(
    base_field,
    forcing,
    load,
    amplitudes,
    amp_index,
    mode_count,
    point_weight,
    point_bias,
    spectral_weight,
):
    channels, slab_rows, plane_count, length_y = base_field.shape
    slab_count = lax.axis_size("slab")
    local_modes = spectral_weight.shape[0]
    modes_y = local_modes * slab_count
    modes_x = spectral_weight.shape[1]
    length_x = slab_rows * slab_count
    packed_width = 2 * channels * plane_count
    slab_index = lax.axis_index("slab")
    level_ids = jnp.arange(amplitudes.shape[0], dtype=jnp.int32)
    amplitude = jnp.sum(jnp.where(level_ids == amp_index[0], amplitudes, 0.0))
    driven = base_field.astype(jnp.float32) + amplitude * load[:, None, None, None] * forcing[
        None
    ].astype(jnp.float32)
    field_now = (2.0 * jnp.tanh(0.5 * driven)).astype(jnp.bfloat16)
    y_cos, y_sin = phases(
        jnp.arange(modes_y, dtype=jnp.int32), jnp.arange(length_y, dtype=jnp.int32), length_y
    )
    y_real = jnp.einsum(
        "cxzy,ky->kxcz", field_now, y_cos.astype(jnp.bfloat16), preferred_element_type=jnp.float32
    )
    y_imag = -jnp.einsum(
        "cxzy,ky->kxcz", field_now, y_sin.astype(jnp.bfloat16), preferred_element_type=jnp.float32
    )
    packed = (
        jnp.stack([y_real, y_imag], axis=2)
        .astype(jnp.bfloat16)
        .reshape(modes_y, slab_rows, packed_width)
    )
    frequency_x = jnp.concatenate(
        [
            jnp.arange(modes_x // 2, dtype=jnp.int32),
            jnp.arange(length_x - modes_x // 2, length_x, dtype=jnp.int32),
        ]
    )
    full_cos, full_sin = phases(frequency_x, jnp.arange(length_x, dtype=jnp.int32), length_x)
    full_cos = full_cos.astype(jnp.bfloat16)
    full_sin = full_sin.astype(jnp.bfloat16)
    pencil = lax.all_to_all(packed, "slab", split_axis=0, concat_axis=1, tiled=True)
    spectrum = forward_x(pencil, full_cos, full_sin)
    spectrum = spectrum.astype(jnp.bfloat16).reshape(local_modes, modes_x, 2, channels, plane_count)
    weight_real = spectral_weight[:, :, 0]
    weight_imag = spectral_weight[:, :, 1]
    spec_real = spectrum[:, :, 0]
    spec_imag = spectrum[:, :, 1]
    mix_real = mixing(weight_real, spec_real) - mixing(weight_imag, spec_imag)
    mix_imag = mixing(weight_real, spec_imag) + mixing(weight_imag, spec_real)
    global_modes = slab_index * local_modes + jnp.arange(local_modes, dtype=jnp.int32)
    keep = (global_modes < mode_count[0]).astype(jnp.float32)[:, None, None, None, None]
    mixed = (
        (jnp.stack([mix_real, mix_imag], axis=2) * keep)
        .astype(jnp.bfloat16)
        .reshape(local_modes, modes_x, packed_width)
    )
    back = inverse_x(mixed, full_cos, full_sin).astype(jnp.bfloat16)
    returned = lax.all_to_all(back, "slab", split_axis=1, concat_axis=0, tiled=True)
    returned = returned.reshape(modes_y, slab_rows, 2, channels, plane_count)
    weights_y = jnp.where(jnp.arange(modes_y) == 0, 1.0, 2.0).astype(jnp.float32) / (
        length_x * length_y
    )
    back_cos = (weights_y[:, None] * y_cos).astype(jnp.bfloat16)
    back_sin = (weights_y[:, None] * y_sin).astype(jnp.bfloat16)
    spectral = jnp.einsum(
        "kxcz,ky->cxzy", returned[:, :, 0], back_cos, preferred_element_type=jnp.float32
    )
    spectral = spectral - jnp.einsum(
        "kxcz,ky->cxzy", returned[:, :, 1], back_sin, preferred_element_type=jnp.float32
    )
    pointwise = (
        jnp.einsum("oc,cxzy->oxzy", point_weight, field_now, preferred_element_type=jnp.float32)
        + point_bias[:, None, None, None]
    )
    layer = jax.nn.gelu(pointwise + spectral, approximate=True).astype(jnp.bfloat16)
    layer = lax.optimization_barrier(layer).astype(jnp.float32)
    total = lax.psum_scatter(
        layer.astype(jnp.bfloat16), "member", scatter_dimension=0, tiled=True
    ).astype(jnp.float32)
    return (total / lax.axis_size("member")).astype(jnp.bfloat16)


def local(base_field, forcing, load, amplitudes, amp_index, mode_count, point_weight, point_bias, spectral_weight):
    fits = tiles_fit(
        base_field.shape, spectral_weight.shape, lax.axis_size("slab"), lax.axis_size("member")
    )
    return (fast_local if fits else general_local)(
        base_field,
        forcing,
        load,
        amplitudes,
        amp_index,
        mode_count,
        point_weight,
        point_bias,
        spectral_weight,
    )


def solution(mesh):
    in_specs = (
        P(None, "slab", None, None),
        P("slab", None, None),
        P(),
        P(),
        P("member"),
        P("member"),
        P(),
        P(),
        P("slab", None, None, None, None),
    )
    out_specs = P("member", "slab", None, None)
    return jax.shard_map(local, mesh=mesh, in_specs=in_specs, out_specs=out_specs, check_vma=False)
```

```python
import math

import jax
import jax.numpy as jnp
import numpy as np
from jax import lax
from jax.experimental import pallas as pl
from jax.experimental.pallas import tpu as pltpu
from jax.sharding import PartitionSpec as P

TWO_PI = 2.0 * math.pi
LANES = 128
SUBLANES = 8
SMEM = pltpu.SMEM
F32 = jnp.float32
BF16 = jnp.bfloat16


def host_phases(frequency, positions, length):
    product = frequency[:, None] * positions[None, :] % length
    angles = product.astype(np.float32) * np.float32(TWO_PI / length)
    return np.cos(angles), np.sin(angles)


def first_frequencies(modes_x, length_x):
    return np.concatenate([np.arange(modes_x // 2), np.arange(length_x - modes_x // 2, length_x)])


def as_bf16(table):
    return jnp.asarray(table.astype(BF16))


def forward_y_table(modes_y, length_y):
    cos, sin = host_phases(np.arange(modes_y), np.arange(length_y), length_y)
    return as_bf16(2.0 * np.concatenate([cos, -sin], axis=0).astype(BF16).astype(np.float32))


def inverse_y_table(modes_y, length_y, length_x, slabs):
    cos, sin = host_phases(np.arange(modes_y), np.arange(length_y), length_y)
    scale = np.where(np.arange(modes_y) == 0, 1.0, 2.0).astype(np.float32)
    scale = (scale / np.float32(length_x * length_y))[:, None]
    parts = np.stack([scale * cos, -(scale * sin)], axis=0)
    parts = parts.reshape(2, slabs, modes_y // slabs, length_y).transpose(1, 0, 2, 3)
    return as_bf16(parts.reshape(2 * modes_y, length_y))


def forward_x_table(modes_x, length_x, slabs, planes):
    cos, sin = host_phases(first_frequencies(modes_x, length_x), np.arange(length_x), length_x)
    whole = np.array([[cos, -sin], [sin, cos]])
    whole = whole.reshape(2, 2, modes_x, slabs, length_x // slabs)
    table = np.einsum("abqsx,zw->sazxwbq", whole, np.eye(planes, dtype=np.float32))
    return as_bf16(table.reshape(2 * planes * length_x, planes * 2 * modes_x))


def inverse_x_table(modes_x, length_x, slabs, planes):
    cos, sin = host_phases(first_frequencies(modes_x, length_x), np.arange(length_x), length_x)
    whole = np.array([cos, -sin]).reshape(2, modes_x, slabs, length_x // slabs)
    table = np.einsum("aqsx,zw->zaqswx", whole, np.eye(planes, dtype=np.float32))
    return as_bf16(table.reshape(planes * 2 * modes_x, planes * length_x))


def low_half(shape):
    return lax.broadcasted_iota(jnp.int32, shape, len(shape) - 1) < shape[-1] // 2


def half_turn(values):
    return pltpu.roll(values, values.shape[-1] // 2, values.ndim - 1)


def pair_halves(first, second):
    low = low_half(first.shape)
    return (
        jnp.where(low, first, half_turn(second)),
        jnp.where(low, half_turn(first), second),
    )


def half_field(base, forcing, strength):
    return jnp.tanh(0.5 * (base.astype(F32) + strength * forcing))


def cell_layout(cell_rows, length_y):
    y_blocks = length_y // LANES
    planes = SUBLANES // y_blocks
    return planes, y_blocks, cell_rows // SUBLANES


def in_hbm(*arrays):
    return [pltpu.with_memory_space_constraint(a, pltpu.HBM) for a in arrays]


def y_modes_kernel(
    index,
    amplitude_hbm,
    load_hbm,
    cells_hbm,
    forcing_hbm,
    table_hbm,
    out_hbm,
    amplitudes,
    load,
    cells,
    forcing,
    forcing_wide,
    table,
    field,
    rows,
    modes,
    packed,
    arrived,
    sent,
):
    channels, cell_rows, _ = cells.shape
    width = field.shape[1]
    groups = channels // width
    planes, y_blocks, slab_rows = cell_layout(cell_rows, table.shape[1])
    modes_y = table.shape[0] // 2
    span = planes * slab_rows
    halves, slabs, half_rows, _ = packed.shape
    half_channels = channels // halves
    small = [
        pltpu.make_async_copy(source, target, arrived.at[n])
        for n, (source, target) in enumerate(
            [
                (amplitude_hbm, amplitudes),
                (load_hbm, load),
                (forcing_hbm, forcing),
                (table_hbm, table),
            ]
        )
    ]
    large = [
        pltpu.make_async_copy(
            cells_hbm.at[pl.ds(g * width, width)], cells.at[pl.ds(g * width, width)], arrived.at[len(small) + g]
        )
        for g in range(groups)
    ]
    for copy in small[:3] + large[:1] + small[3:] + large[1:]:
        copy.start()
    for copy in small[:3]:
        copy.wait()
    amplitude = amplitudes[index[0]]
    forcing_wide[...] = forcing[...].astype(F32)
    small[3].wait()
    leaving = []
    for step in range(groups + 1):
        if step < groups:
            large[step].wait()
            for c in range(width):
                channel = step * width + c
                field[step % 2, c] = half_field(cells[channel], forcing_wide[...], amplitude * load[channel])
                for z in range(planes):
                    for j in range(y_blocks):
                        picked = field[step % 2, c, pl.ds(j * planes + z, slab_rows, stride=planes * y_blocks), :]
                        rows[
                            step % 2, pl.ds(c * span + z * slab_rows, slab_rows), pl.ds(j * LANES, LANES)
                        ] = picked.astype(BF16)
        if step > 0:
            g = step - 1
            result = lax.dot_general(
                table[...], rows[g % 2], (((1,), (1,)), ((), ())), preferred_element_type=F32
            )
            for t in range(width // 2):
                tile = slice(t * LANES, (t + 1) * LANES)
                pair = pair_halves(result[:modes_y, tile], result[modes_y:, tile])
                for n in range(2):
                    half, c = divmod(g * width + 2 * t + n, half_channels)
                    modes[half, pl.ds(c, modes_y, stride=half_channels), :] = pair[n]
            if step * width % half_channels == 0:
                half = g * width // half_channels
                for d in range(slabs):
                    packed[half, d] = modes[half, pl.ds(d * half_rows, half_rows), :].astype(BF16)
                copy = pltpu.make_async_copy(
                    packed.at[half], out_hbm.at[:, pl.ds(half * half_rows, half_rows), :], sent.at[half]
                )
                copy.start()
                leaving.append(copy)
    for copy in leaving:
        copy.wait()


def y_modes(amp_index, amplitudes, load, cells, forcing, slabs, modes_y, length_y):
    channels, cell_rows, _ = cells.shape
    width, halves = 4, 2
    block_rows = modes_y // slabs * channels
    table = forward_y_table(modes_y, length_y)
    planes, _, slab_rows = cell_layout(cell_rows, length_y)
    operands = in_hbm(amplitudes, load, cells, forcing, table)
    anywhere = pl.BlockSpec(memory_space=pl.ANY)
    return pl.pallas_call(
        y_modes_kernel,
        in_specs=[pl.BlockSpec(memory_space=SMEM)] + [anywhere] * len(operands),
        out_specs=anywhere,
        out_shape=jax.ShapeDtypeStruct((slabs, block_rows, LANES), BF16),
        scratch_shapes=[
            SMEM(amplitudes.shape, F32),
            SMEM(load.shape, F32),
            pltpu.VMEM(cells.shape, BF16),
            pltpu.VMEM(forcing.shape, BF16),
            pltpu.VMEM(forcing.shape, F32),
            pltpu.VMEM(table.shape, BF16),
            pltpu.VMEM((2, width, cell_rows, LANES), F32),
            pltpu.VMEM((2, width * planes * slab_rows, length_y), BF16),
            pltpu.VMEM((halves, modes_y * channels // halves, LANES), F32),
            pltpu.VMEM((halves, slabs, block_rows // halves, LANES), BF16),
            pltpu.SemaphoreType.DMA((4 + channels // width,)),
            pltpu.SemaphoreType.DMA((halves,)),
        ],
        compiler_params=pltpu.CompilerParams(vmem_limit_bytes=12 * 1024 * 1024),
        cost_estimate=pl.CostEstimate(
            flops=4 * modes_y * cells.size, bytes_accessed=4 * cells.size, transcendentals=cells.size
        ),
        name="y_modes",
    )(amp_index, *operands)


def prepare_kernel(weight_ref, forward_ref, inverse_ref, weights, forward_out, inverse_out, wide):
    forward_out[...] = forward_ref[...]
    inverse_out[...] = inverse_ref[...]
    local_modes, parts, channels, _, _ = weight_ref.shape
    for k in range(local_modes // 2):
        for r in range(parts):
            for o in range(channels):
                pair = [weight_ref[2 * k + n, r, o].astype(F32) for n in range(2)]
                wide[k, r, pl.ds(o, channels, stride=channels), :] = jnp.concatenate(pair, axis=1)
    weights[...] = wide[...].astype(BF16)


def prepare(spectral_weight, length_x, slabs, planes):
    local_modes, parts, channels, _, modes_x = spectral_weight.shape
    forward = forward_x_table(modes_x, length_x, slabs, planes)
    inverse = inverse_x_table(modes_x, length_x, slabs, planes)
    wide = (local_modes // 2, parts, channels * channels, 2 * modes_x)
    vmem = pl.BlockSpec(memory_space=pltpu.VMEM)
    return pl.pallas_call(
        prepare_kernel,
        in_specs=[vmem] * 3,
        out_specs=[vmem] * 3,
        out_shape=[
            pltpu.VMEM(wide, BF16),
            pltpu.VMEM(forward.shape, BF16),
            pltpu.VMEM(inverse.shape, BF16),
        ],
        scratch_shapes=[pltpu.VMEM(wide, F32)],
        compiler_params=pltpu.CompilerParams(vmem_limit_bytes=16 * 1024 * 1024),
        cost_estimate=pl.CostEstimate(
            flops=4 * spectral_weight.size, bytes_accessed=10 * spectral_weight.size, transcendentals=0
        ),
        name="prepare",
    )(*in_hbm(spectral_weight, forward, inverse))


def mix_kernel(limit_ref, pencil_ref, forward_ref, weight_ref, inverse_ref, out_ref, spectrum, mixed):
    slabs, block_rows, _ = pencil_ref.shape
    pairs, _, rows, width = weight_ref.shape
    local_modes = 2 * pairs
    channels = block_rows // local_modes
    planes = forward_ref.shape[1] // width
    groups = channels // SUBLANES
    half_channels = channels // 2
    block = SUBLANES * 2 * local_modes
    pencil = jnp.concatenate([pencil_ref[s] for s in range(slabs)], axis=1)
    result = jnp.dot(pencil, forward_ref[...], preferred_element_type=F32)
    for z in range(planes):
        for half in range(2):
            for k in range(pairs):
                start = (half * local_modes + 2 * k) * half_channels
                both = [
                    result[start + n * half_channels : start + (n + 1) * half_channels, z * width : (z + 1) * width]
                    for n in range(2)
                ]
                parts = pair_halves(*both)
                for r in range(2):
                    spectrum[k, z, r, pl.ds(half * half_channels, half_channels), :] = parts[r]
    low = low_half((SUBLANES, width))
    for k in range(pairs):
        keep = [jnp.where(limit_ref[0] > 2 * k + n, 1.0, 0.0).astype(F32) for n in range(2)]
        sums = [[[None, None] for _ in range(groups)] for _ in range(planes)]
        for i in range(channels):
            values = [
                [jnp.broadcast_to(spectrum[k, z, r, pl.ds(i, 1), :], (SUBLANES, width)) for r in range(2)]
                for z in range(planes)
            ]
            weights = [weight_ref[k, r, pl.ds(i * channels, channels), :].astype(F32) for r in range(2)]
            for g in range(groups):
                real, imag = (w[g * SUBLANES : (g + 1) * SUBLANES] for w in weights)
                for z in range(planes):
                    terms = (
                        real * values[z][0] - imag * values[z][1],
                        real * values[z][1] + imag * values[z][0],
                    )
                    for r in range(2):
                        old = sums[z][g][r]
                        sums[z][g][r] = terms[r] if old is None else old + terms[r]
        for z in range(planes):
            for g in range(groups):
                modes = pair_halves(*sums[z][g])
                for n in range(2):
                    kept = modes[n] * keep[n]
                    swapped = half_turn(kept)
                    start = g * block + 2 * k + n
                    mixed[z, pl.ds(start, SUBLANES, stride=2 * local_modes), :] = kept
                    mixed[z, pl.ds(start + local_modes, SUBLANES, stride=2 * local_modes), :] = jnp.where(
                        low, swapped, -swapped
                    )
    left = jnp.concatenate([mixed[z].astype(BF16) for z in range(planes)], axis=1)
    back = jnp.dot(left, inverse_ref[...], preferred_element_type=F32)
    members = out_ref.shape[0] // slabs
    for h in range(members):
        for t in range(slabs // 2):
            tile = slice(t * LANES, (t + 1) * LANES)
            start = 2 * h * block
            pair = pair_halves(back[start : start + block, tile], back[start + block : start + 2 * block, tile])
            for n in range(2):
                out_ref[(2 * t + n) * members + h] = pair[n].astype(BF16)


def mix(limit, pencil, weights, forward, inverse, members):
    slabs, block_rows, _ = pencil.shape
    pairs, _, _, width = weights.shape
    channels = block_rows // (2 * pairs)
    planes = forward.shape[1] // width
    vmem = pl.BlockSpec(memory_space=pltpu.VMEM)
    block = SUBLANES * 4 * pairs
    return pl.pallas_call(
        mix_kernel,
        in_specs=[pl.BlockSpec(memory_space=SMEM)] + [vmem] * 4,
        out_specs=vmem,
        out_shape=jax.ShapeDtypeStruct((members * slabs, block, LANES), BF16),
        scratch_shapes=[
            pltpu.VMEM((pairs, planes, 2, channels, width), F32),
            pltpu.VMEM((planes, channels // SUBLANES * block, width), F32),
        ],
        compiler_params=pltpu.CompilerParams(vmem_limit_bytes=12 * 1024 * 1024),
        cost_estimate=pl.CostEstimate(
            flops=2 * block_rows * forward.size, bytes_accessed=8 * weights.size, transcendentals=0
        ),
        name="mix",
    )(limit, pencil, forward, weights, inverse)


def pointwise_kernel(
    place_ref, index_ref, amplitude_ref, load_ref, bias_ref, weight_ref, base_ref, forcing_ref, out_ref, spread
):
    channels, depth, _ = base_ref.shape
    members = index_ref.shape[0]
    out_channels = channels // members
    me = place_ref[0]

    @pl.when(pl.program_id(0) == 0)
    def _():
        tall = (out_channels * depth, channels)
        wide = (channels, channels * depth)
        row_of = lax.broadcasted_iota(jnp.int32, tall, 0) // depth + me * out_channels
        pick_rows = (row_of == lax.broadcasted_iota(jnp.int32, tall, 1)).astype(BF16)
        column_of = lax.broadcasted_iota(jnp.int32, wide, 1) // depth
        pick_columns = (column_of == lax.broadcasted_iota(jnp.int32, wide, 0)).astype(BF16)
        picked = jnp.dot(pick_rows, weight_ref[...], preferred_element_type=F32).astype(BF16)
        full = jnp.dot(picked, pick_columns, preferred_element_type=F32)
        same = lax.broadcasted_iota(jnp.int32, full.shape, 0) % depth == (
            lax.broadcasted_iota(jnp.int32, full.shape, 1) % depth
        )
        spread[...] = jnp.where(same, 2.0 * full, 0.0).astype(BF16)

    forcing = forcing_ref[...].astype(F32)
    fields = []
    for m in range(members):
        amplitude = amplitude_ref[index_ref[lax.rem(me - m + members, members)]]
        parts = [half_field(base_ref[c], forcing, amplitude * load_ref[c]).astype(BF16) for c in range(channels)]
        fields.append(jnp.concatenate(parts, axis=0))
    result = jnp.dot(spread[...], jnp.concatenate(fields, axis=1), preferred_element_type=F32)
    _, outer, inner, _, _ = out_ref.shape
    start = pl.program_id(0) * depth
    for a in range(outer):
        for b in range(inner):
            o = a * inner + b
            bias = bias_ref[me * out_channels + o]
            for m in range(members):
                cells = result[o * depth : (o + 1) * depth, m * LANES : (m + 1) * LANES] + bias
                out_ref[m, a, b, pl.ds(pl.multiple_of(start, depth), depth), :] = cells.astype(BF16)


def pointwise(place, indices, amplitudes, load, bias, weight, cells, forcing):
    channels, cell_rows, _ = cells.shape
    members = indices.shape[0]
    depth = 2 * SUBLANES
    inner = SUBLANES
    outer = channels // members // inner
    spread = (channels // members * depth, channels * depth)
    smem = pl.BlockSpec(memory_space=SMEM)
    return pl.pallas_call(
        pointwise_kernel,
        grid=(cell_rows // depth,),
        in_specs=[smem] * 5
        + [
            pl.BlockSpec(weight.shape, lambda r: (0, 0)),
            pl.BlockSpec((channels, depth, LANES), lambda r: (0, r, 0)),
            pl.BlockSpec((depth, LANES), lambda r: (r, 0)),
        ],
        out_specs=pl.BlockSpec(memory_space=pltpu.VMEM),
        out_shape=pltpu.VMEM((members, outer, inner, cell_rows, LANES), BF16),
        scratch_shapes=[pltpu.VMEM(spread, BF16)],
        compiler_params=pltpu.CompilerParams(vmem_limit_bytes=12 * 1024 * 1024),
        cost_estimate=pl.CostEstimate(
            flops=4 * spread[0] * spread[1] * members * cell_rows // depth * LANES,
            bytes_accessed=8 * cells.size,
            transcendentals=members * cells.size,
        ),
        name="pointwise",
    )(place, indices, amplitudes, load, bias, weight, *in_hbm(cells, forcing))


def layer_kernel(back_ref, table_ref, points, out_hbm, columns, spectral, result, sent):
    members, outer, inner, cell_rows, _ = points.shape
    sources, block_rows, _ = back_ref.shape
    slabs = sources // members
    depth = block_rows // inner
    planes, y_blocks, slab_rows = cell_layout(cell_rows, table_ref.shape[1])
    leaving = [pltpu.make_async_copy(result.at[:, b], out_hbm.at[:, b], sent.at[b]) for b in range(inner)]
    for m in range(members):
        for s in range(slabs):
            block = back_ref[s * members + m].astype(F32)
            for b in range(inner):
                columns[b, m, pl.ds(s * depth, depth), :] = block[b * depth : (b + 1) * depth]
    for b in range(inner):
        turn = b % 2
        for m in range(members):
            values = lax.dot_general(
                columns[b, m].astype(BF16), table_ref[...], (((0,), (0,)), ((), ())), preferred_element_type=F32
            )
            for a in range(outer):
                for z in range(planes):
                    start = (a * planes + z) * slab_rows
                    for j in range(y_blocks):
                        spectral[
                            turn, m, a, pl.ds(j * planes + z, slab_rows, stride=planes * y_blocks), :
                        ] = values[start : start + slab_rows, j * LANES : (j + 1) * LANES]
        for a in range(outer):
            total = None
            for m in range(members):
                value = jax.nn.gelu(points[m, a, b].astype(F32) + spectral[turn, m, a], approximate=True)
                total = value if total is None else total + value
            result[a, b] = (total * (1.0 / members)).astype(BF16)
        leaving[b].start()
    for copy in leaving:
        copy.wait()


def layer(back, points, length_x, length_y, modes_y):
    members, outer, inner, cell_rows, _ = points.shape
    slabs = back.shape[0] // members
    table = inverse_y_table(modes_y, length_y, length_x, slabs)
    vmem = pl.BlockSpec(memory_space=pltpu.VMEM)
    anywhere = pl.BlockSpec(memory_space=pl.ANY)
    return pl.pallas_call(
        layer_kernel,
        in_specs=[vmem, vmem, vmem],
        out_specs=anywhere,
        out_shape=pltpu.HBM((outer, inner, cell_rows, LANES), BF16),
        scratch_shapes=[
            pltpu.VMEM((inner, members, 2 * modes_y, LANES), F32),
            pltpu.VMEM((2, members, outer, cell_rows, LANES), F32),
            pltpu.VMEM((outer, inner, cell_rows, LANES), BF16),
            pltpu.SemaphoreType.DMA((inner,)),
        ],
        compiler_params=pltpu.CompilerParams(vmem_limit_bytes=16 * 1024 * 1024),
        cost_estimate=pl.CostEstimate(
            flops=4 * modes_y * points.size, bytes_accessed=5 * points.size, transcendentals=points.size
        ),
        name="layer",
    )(back, table, points)


def fast_local(
    base_field,
    forcing,
    load,
    amplitudes,
    amp_index,
    mode_count,
    point_weight,
    point_bias,
    spectral_weight,
):
    channels, slab_rows, planes, length_y = base_field.shape
    slabs, members = lax.axis_size("slab"), lax.axis_size("member")
    local_modes, modes_x = spectral_weight.shape[:2]
    modes_y = local_modes * slabs
    length_x = slab_rows * slabs
    y_blocks = length_y // LANES
    cells = base_field.reshape(channels, slab_rows, planes, y_blocks, LANES).transpose(0, 1, 3, 2, 4)
    cells = cells.reshape(channels, slab_rows * SUBLANES, LANES)
    force = forcing.reshape(slab_rows, planes, y_blocks, LANES).transpose(0, 2, 1, 3)
    force = force.reshape(slab_rows * SUBLANES, LANES)
    me = lax.axis_index("member")
    indices = jnp.concatenate(
        [amp_index]
        + [
            lax.ppermute(amp_index, "member", [(s, (s + r) % members) for s in range(members)])
            for r in range(1, members)
        ]
    )
    out_channels = channels // members
    packed = y_modes(amp_index, amplitudes, load, cells, force, slabs, modes_y, length_y)
    pencil = lax.all_to_all(packed, "slab", split_axis=0, concat_axis=0, tiled=True)
    weights, forward, inverse = prepare(spectral_weight.transpose(0, 2, 3, 4, 1), length_x, slabs, planes)
    limit = mode_count - lax.axis_index("slab") * local_modes
    back = mix(limit, pencil, weights, forward, inverse, members)
    back = lax.all_to_all(back, ("slab", "member"), split_axis=0, concat_axis=0, tiled=True)
    points = pointwise(me.reshape(1), indices, amplitudes, load, point_bias, point_weight, cells, force)
    result = layer(back, points, length_x, length_y, modes_y)
    result = result.reshape(out_channels, slab_rows, y_blocks, planes, LANES).transpose(0, 1, 3, 2, 4)
    return result.reshape(out_channels, slab_rows, planes, length_y)


def tiles_fit(base_shape, weight_shape, slabs, members):
    channels, slab_rows, planes, length_y = base_shape
    local_modes, modes_x = weight_shape[:2]
    return (
        2 * planes * slab_rows == LANES
        and 2 * modes_x == LANES
        and planes * length_y == SUBLANES * LANES
        and 2 * local_modes == SUBLANES
        and 2 * SUBLANES * members == channels
        and slabs % 2 == 0
    )


def phases(frequency, positions, length):
    product = frequency[:, None] * positions[None, :] % length
    angles = product.astype(jnp.float32) * (TWO_PI / length)
    return (jnp.cos(angles), jnp.sin(angles))


def forward_x(pencil, cos_table, sin_table):
    row_total = pencil.shape[0]
    modes = cos_table.shape[0]
    with_cos = jnp.einsum(
        "kxf,mx->kmf", pencil, cos_table, preferred_element_type=jnp.float32
    ).reshape(row_total, modes, 2, -1)
    with_sin = jnp.einsum(
        "kxf,mx->kmf", pencil, sin_table, preferred_element_type=jnp.float32
    ).reshape(row_total, modes, 2, -1)
    real_part = with_cos[:, :, 0] + with_sin[:, :, 1]
    imag_part = with_cos[:, :, 1] - with_sin[:, :, 0]
    return jnp.stack([real_part, imag_part], axis=2).reshape(row_total, modes, -1)


def inverse_x(spectra, cos_table, sin_table):
    row_total = spectra.shape[0]
    points = cos_table.shape[1]
    with_cos = jnp.einsum(
        "kmf,mx->kxf", spectra, cos_table, preferred_element_type=jnp.float32
    ).reshape(row_total, points, 2, -1)
    with_sin = jnp.einsum(
        "kmf,mx->kxf", spectra, sin_table, preferred_element_type=jnp.float32
    ).reshape(row_total, points, 2, -1)
    real_part = with_cos[:, :, 0] - with_sin[:, :, 1]
    imag_part = with_cos[:, :, 1] + with_sin[:, :, 0]
    return jnp.stack([real_part, imag_part], axis=2).reshape(row_total, points, -1)


def mixing(weights, values):
    return jnp.einsum("kmoi,kmiz->kmoz", weights, values, preferred_element_type=jnp.float32)


def general_local(
    base_field,
    forcing,
    load,
    amplitudes,
    amp_index,
    mode_count,
    point_weight,
    point_bias,
    spectral_weight,
):
    channels, slab_rows, plane_count, length_y = base_field.shape
    slab_count = lax.axis_size("slab")
    local_modes = spectral_weight.shape[0]
    modes_y = local_modes * slab_count
    modes_x = spectral_weight.shape[1]
    length_x = slab_rows * slab_count
    packed_width = 2 * channels * plane_count
    slab_index = lax.axis_index("slab")
    level_ids = jnp.arange(amplitudes.shape[0], dtype=jnp.int32)
    amplitude = jnp.sum(jnp.where(level_ids == amp_index[0], amplitudes, 0.0))
    driven = base_field.astype(jnp.float32) + amplitude * load[:, None, None, None] * forcing[
        None
    ].astype(jnp.float32)
    field_now = (2.0 * jnp.tanh(0.5 * driven)).astype(jnp.bfloat16)
    y_cos, y_sin = phases(
        jnp.arange(modes_y, dtype=jnp.int32), jnp.arange(length_y, dtype=jnp.int32), length_y
    )
    y_real = jnp.einsum(
        "cxzy,ky->kxcz", field_now, y_cos.astype(jnp.bfloat16), preferred_element_type=jnp.float32
    )
    y_imag = -jnp.einsum(
        "cxzy,ky->kxcz", field_now, y_sin.astype(jnp.bfloat16), preferred_element_type=jnp.float32
    )
    packed = (
        jnp.stack([y_real, y_imag], axis=2)
        .astype(jnp.bfloat16)
        .reshape(modes_y, slab_rows, packed_width)
    )
    frequency_x = jnp.concatenate(
        [
            jnp.arange(modes_x // 2, dtype=jnp.int32),
            jnp.arange(length_x - modes_x // 2, length_x, dtype=jnp.int32),
        ]
    )
    full_cos, full_sin = phases(frequency_x, jnp.arange(length_x, dtype=jnp.int32), length_x)
    full_cos = full_cos.astype(jnp.bfloat16)
    full_sin = full_sin.astype(jnp.bfloat16)
    pencil = lax.all_to_all(packed, "slab", split_axis=0, concat_axis=1, tiled=True)
    spectrum = forward_x(pencil, full_cos, full_sin)
    spectrum = spectrum.astype(jnp.bfloat16).reshape(local_modes, modes_x, 2, channels, plane_count)
    weight_real = spectral_weight[:, :, 0]
    weight_imag = spectral_weight[:, :, 1]
    spec_real = spectrum[:, :, 0]
    spec_imag = spectrum[:, :, 1]
    mix_real = mixing(weight_real, spec_real) - mixing(weight_imag, spec_imag)
    mix_imag = mixing(weight_real, spec_imag) + mixing(weight_imag, spec_real)
    global_modes = slab_index * local_modes + jnp.arange(local_modes, dtype=jnp.int32)
    keep = (global_modes < mode_count[0]).astype(jnp.float32)[:, None, None, None, None]
    mixed = (
        (jnp.stack([mix_real, mix_imag], axis=2) * keep)
        .astype(jnp.bfloat16)
        .reshape(local_modes, modes_x, packed_width)
    )
    back = inverse_x(mixed, full_cos, full_sin).astype(jnp.bfloat16)
    returned = lax.all_to_all(back, "slab", split_axis=1, concat_axis=0, tiled=True)
    returned = returned.reshape(modes_y, slab_rows, 2, channels, plane_count)
    weights_y = jnp.where(jnp.arange(modes_y) == 0, 1.0, 2.0).astype(jnp.float32) / (
        length_x * length_y
    )
    back_cos = (weights_y[:, None] * y_cos).astype(jnp.bfloat16)
    back_sin = (weights_y[:, None] * y_sin).astype(jnp.bfloat16)
    spectral = jnp.einsum(
        "kxcz,ky->cxzy", returned[:, :, 0], back_cos, preferred_element_type=jnp.float32
    )
    spectral = spectral - jnp.einsum(
        "kxcz,ky->cxzy", returned[:, :, 1], back_sin, preferred_element_type=jnp.float32
    )
    pointwise = (
        jnp.einsum("oc,cxzy->oxzy", point_weight, field_now, preferred_element_type=jnp.float32)
        + point_bias[:, None, None, None]
    )
    layer = jax.nn.gelu(pointwise + spectral, approximate=True).astype(jnp.bfloat16)
    layer = lax.optimization_barrier(layer).astype(jnp.float32)
    total = lax.psum_scatter(
        layer.astype(jnp.bfloat16), "member", scatter_dimension=0, tiled=True
    ).astype(jnp.float32)
    return (total / lax.axis_size("member")).astype(jnp.bfloat16)


def local(base_field, forcing, load, amplitudes, amp_index, mode_count, point_weight, point_bias, spectral_weight):
    fits = tiles_fit(
        base_field.shape, spectral_weight.shape, lax.axis_size("slab"), lax.axis_size("member")
    )
    return (fast_local if fits else general_local)(
        base_field,
        forcing,
        load,
        amplitudes,
        amp_index,
        mode_count,
        point_weight,
        point_bias,
        spectral_weight,
    )


def solution(mesh):
    in_specs = (
        P(None, "slab", None, None),
        P("slab", None, None),
        P(),
        P(),
        P("member"),
        P("member"),
        P(),
        P(),
        P("slab", None, None, None, None),
    )
    out_specs = P("member", "slab", None, None)
    return jax.shard_map(local, mesh=mesh, in_specs=in_specs, out_specs=out_specs, check_vma=False)
```

```python
import math

import jax
import jax.numpy as jnp
import numpy as np
from jax import lax
from jax.experimental import pallas as pl
from jax.experimental.pallas import tpu as pltpu
from jax.sharding import PartitionSpec as P

TWO_PI = 2.0 * math.pi
LANES = 128
SUBLANES = 8
FORCING_ROWS = 64
PART_ROWS = SUBLANES * SUBLANES // 2
SMEM = pltpu.SMEM
F32 = jnp.float32
BF16 = jnp.bfloat16


def host_phases(frequency, positions, length):
    product = frequency[:, None] * positions[None, :] % length
    angles = product.astype(np.float32) * np.float32(TWO_PI / length)
    return np.cos(angles), np.sin(angles)


def first_frequencies(modes_x, length_x):
    return np.concatenate([np.arange(modes_x // 2), np.arange(length_x - modes_x // 2, length_x)])


def as_bf16(table):
    return jnp.asarray(table.astype(BF16))


def by_owner(table, slabs):
    modes, length = table.shape
    local = modes // slabs
    return table.reshape(2, slabs // 2, local, length).transpose(1, 0, 2, 3)


def forward_y_table(modes_y, length_y, slabs):
    cos, sin = host_phases(np.arange(modes_y), np.arange(length_y), length_y)
    table = np.stack([by_owner(cos, slabs), by_owner(-sin, slabs)], axis=0)
    return as_bf16(2.0 * table.astype(BF16).astype(np.float32).reshape(2 * modes_y, length_y))


def inverse_y_table(modes_y, length_y, length_x, slabs):
    cos, sin = host_phases(np.arange(modes_y), np.arange(length_y), length_y)
    scale = np.where(np.arange(modes_y) == 0, 1.0, 2.0).astype(np.float32)
    scale = (scale / np.float32(length_x * length_y))[:, None]
    parts = np.stack([scale * cos, -(scale * sin)], axis=0)
    parts = parts.reshape(2, slabs, modes_y // slabs, length_y).transpose(1, 0, 2, 3)
    return as_bf16(parts.reshape(2 * modes_y, length_y))


def forward_x_table(modes_x, length_x, slabs, planes):
    cos, sin = host_phases(first_frequencies(modes_x, length_x), np.arange(length_x), length_x)
    whole = np.array([[cos, -sin], [sin, cos]])
    whole = whole.reshape(2, 2, modes_x, 2, slabs // 2, length_x // slabs)
    table = np.einsum("abqhsx,zw->hsazxwbq", whole, np.eye(planes, dtype=np.float32))
    return as_bf16(table.reshape(2, planes * length_x, planes * 2 * modes_x))


def inverse_x_table(modes_x, length_x, slabs, planes):
    cos, sin = host_phases(first_frequencies(modes_x, length_x), np.arange(length_x), length_x)
    whole = np.array([cos, -sin]).reshape(2, modes_x, slabs, length_x // slabs)
    table = np.einsum("aqsx,zw->zaqswx", whole, np.eye(planes, dtype=np.float32))
    return as_bf16(table.reshape(planes * 2 * modes_x, planes * length_x))


def low_half(shape):
    return lax.broadcasted_iota(jnp.int32, shape, len(shape) - 1) < shape[-1] // 2


def half_turn(values):
    return pltpu.roll(values, values.shape[-1] // 2, values.ndim - 1)


def pair_halves(first, second):
    low = low_half(first.shape)
    return (
        jnp.where(low, first, half_turn(second)),
        jnp.where(low, half_turn(first), second),
    )


def half_field(base, forcing, strength):
    return jnp.tanh(0.5 * (base.astype(F32) + strength * forcing))


def cell_layout(cell_rows, length_y):
    y_blocks = length_y // LANES
    planes = SUBLANES // y_blocks
    return planes, y_blocks, cell_rows // SUBLANES


def in_hbm(*arrays):
    return [pltpu.with_memory_space_constraint(a, pltpu.HBM) for a in arrays]


def y_modes_kernel(
    index_any,
    amplitude_hbm,
    load_hbm,
    cells_hbm,
    forcing_hbm,
    table_hbm,
    out_hbm,
    index,
    amplitudes,
    load,
    cells,
    forcing,
    forcing_wide,
    table,
    field,
    rows,
    modes,
    packed,
    arrived,
    sent,
):
    channels, cell_rows, _ = cells.shape
    width = field.shape[1]
    groups = channels // width
    planes, y_blocks, slab_rows = cell_layout(cell_rows, table.shape[1])
    modes_y = table.shape[0] // 2
    span = planes * slab_rows
    owners, block_rows, _ = out_hbm.shape
    part_rows = block_rows // groups
    small = [
        pltpu.make_async_copy(source, target, arrived.at[n])
        for n, (source, target) in enumerate(
            [
                (index_any, index),
                (amplitude_hbm, amplitudes),
                (load_hbm, load),
                (forcing_hbm, forcing),
                (table_hbm, table),
            ]
        )
    ]
    large = [
        pltpu.make_async_copy(
            cells_hbm.at[pl.ds(g * width, width)], cells.at[pl.ds(g * width, width)], arrived.at[len(small) + g]
        )
        for g in range(groups)
    ]
    for copy in small[:4] + large[:1] + small[4:] + large[1:]:
        copy.start()
    for copy in small[:4]:
        copy.wait()
    amplitude = amplitudes[index[0, 0]]
    forcing_wide[...] = forcing[...].astype(F32)
    small[4].wait()
    leaving = [
        pltpu.make_async_copy(packed.at[g], out_hbm.at[:, pl.ds(g * part_rows, part_rows), :], sent.at[g])
        for g in range(groups)
    ]
    for step in range(groups + 1):
        if step < groups:
            large[step].wait()
            strengths = [amplitude * load[step * width + c] for c in range(width)]
            for start in range(0, cell_rows, FORCING_ROWS):
                some = pl.ds(start, FORCING_ROWS)
                force = forcing_wide[some, :]
                for c in range(width):
                    field[step % 2, c, some, :] = half_field(cells[step * width + c, some, :], force, strengths[c])
            for c in range(width):
                for z in range(planes):
                    for j in range(y_blocks):
                        picked = field[step % 2, c, pl.ds(j * planes + z, slab_rows, stride=planes * y_blocks), :]
                        rows[
                            step % 2, pl.ds(c * span + z * slab_rows, slab_rows), pl.ds(j * LANES, LANES)
                        ] = picked.astype(BF16)
        if step > 0:
            g = step - 1
            result = lax.dot_general(
                table[...], rows[g % 2], (((1,), (1,)), ((), ())), preferred_element_type=F32
            )
            for t in range(width // 2):
                tile = slice(t * LANES, (t + 1) * LANES)
                pair = pair_halves(result[:modes_y, tile], result[modes_y:, tile])
                for n in range(2):
                    modes[g % 2, pl.ds(2 * t + n, modes_y, stride=width), :] = pair[n]
            for d in range(owners):
                packed[g, d] = modes[g % 2, pl.ds(d * part_rows, part_rows), :].astype(BF16)
            leaving[g].start()
    for copy in leaving:
        copy.wait()


def y_modes(amp_index, amplitudes, load, cells, forcing, slabs, modes_y, length_y):
    channels, cell_rows, _ = cells.shape
    width = SUBLANES
    parts = channels // width
    owners = slabs // 2
    block_rows = modes_y // owners * channels
    table = forward_y_table(modes_y, length_y, slabs)
    planes, _, slab_rows = cell_layout(cell_rows, length_y)
    operands = in_hbm(amplitudes, load, cells, forcing, table)
    anywhere = pl.BlockSpec(memory_space=pl.ANY)
    return pl.pallas_call(
        y_modes_kernel,
        in_specs=[anywhere] * (1 + len(operands)),
        out_specs=anywhere,
        out_shape=jax.ShapeDtypeStruct((owners, block_rows, LANES), BF16),
        scratch_shapes=[
            SMEM(amp_index.shape, jnp.int32),
            SMEM(amplitudes.shape, F32),
            SMEM(load.shape, F32),
            pltpu.VMEM(cells.shape, BF16),
            pltpu.VMEM(forcing.shape, BF16),
            pltpu.VMEM(forcing.shape, F32),
            pltpu.VMEM(table.shape, BF16),
            pltpu.VMEM((2, width, cell_rows, LANES), F32),
            pltpu.VMEM((2, width * planes * slab_rows, length_y), BF16),
            pltpu.VMEM((2, modes_y * width, LANES), F32),
            pltpu.VMEM((parts, owners, block_rows // parts, LANES), BF16),
            pltpu.SemaphoreType.DMA((5 + parts,)),
            pltpu.SemaphoreType.DMA((parts,)),
        ],
        compiler_params=pltpu.CompilerParams(vmem_limit_bytes=12 * 1024 * 1024),
        cost_estimate=pl.CostEstimate(
            flops=4 * modes_y * cells.size, bytes_accessed=4 * cells.size, transcendentals=cells.size
        ),
        name="y_modes",
    )(amp_index, *operands)


def prepare_kernel(
    half_ref,
    own_any,
    other_any,
    amplitude_ref,
    load_ref,
    weight_ref,
    forward_hbm,
    inverse_hbm,
    strengths,
    weights,
    forward,
    inverse,
    wide,
    indices,
    arrived,
):
    half, me = half_ref[0], half_ref[1]
    copies = [
        pltpu.make_async_copy(forward_hbm.at[half], forward, arrived.at[0]),
        pltpu.make_async_copy(inverse_hbm, inverse, arrived.at[1]),
        pltpu.make_async_copy(own_any, indices.at[pl.ds(0, 1)], arrived.at[2]),
        pltpu.make_async_copy(other_any, indices.at[pl.ds(1, 1)], arrived.at[3]),
    ]
    for copy in copies:
        copy.start()
    local_modes, parts, channels, _, _ = weight_ref.shape
    for k in range(local_modes // 2):
        for r in range(parts):
            for o in range(channels):
                pair = [weight_ref[2 * k + n, r, o].astype(F32) for n in range(2)]
                wide[k, r, pl.ds(o, channels, stride=channels), :] = jnp.concatenate(pair, axis=1)
    weights[...] = wide[...].astype(BF16)
    for copy in copies:
        copy.wait()
    for m in range(2):
        amplitude = amplitude_ref[indices[lax.rem(me + m, 2), 0]]
        for c in range(channels):
            strengths[m * channels + c] = amplitude * load_ref[c]


def prepare(place, own, other, amplitudes, load, spectral_weight, length_x, slabs, planes):
    local_modes, parts, channels, _, modes_x = spectral_weight.shape
    forward = forward_x_table(modes_x, length_x, slabs, planes)
    inverse = inverse_x_table(modes_x, length_x, slabs, planes)
    wide = (local_modes // 2, parts, channels * channels, 2 * modes_x)
    vmem = pl.BlockSpec(memory_space=pltpu.VMEM)
    smem = pl.BlockSpec(memory_space=SMEM)
    anywhere = pl.BlockSpec(memory_space=pl.ANY)
    return pl.pallas_call(
        prepare_kernel,
        in_specs=[smem] + [anywhere] * 2 + [smem] * 2 + [vmem] + [anywhere] * 2,
        out_specs=[smem] + [vmem] * 3,
        out_shape=[
            jax.ShapeDtypeStruct((2 * channels,), F32),
            pltpu.VMEM(wide, BF16),
            pltpu.VMEM(forward.shape[1:], BF16),
            pltpu.VMEM(inverse.shape, BF16),
        ],
        scratch_shapes=[pltpu.VMEM(wide, F32), SMEM((2, 1), jnp.int32), pltpu.SemaphoreType.DMA((4,))],
        compiler_params=pltpu.CompilerParams(vmem_limit_bytes=16 * 1024 * 1024),
        cost_estimate=pl.CostEstimate(
            flops=4 * spectral_weight.size, bytes_accessed=10 * spectral_weight.size, transcendentals=0
        ),
        name="prepare",
    )(place, own, other, amplitudes, load, *in_hbm(spectral_weight, forward, inverse))


def spectrum_kernel(half_ref, pencil_ref, forward_ref, out_ref):
    sources, block_rows, _ = pencil_ref.shape
    rows = out_ref.shape[0]
    parts = rows // PART_ROWS
    picked = []
    for part in range(parts):
        start = pl.multiple_of((2 * part + half_ref[0]) * PART_ROWS, PART_ROWS)
        picked.append(
            jnp.concatenate([pencil_ref[s, pl.ds(start, PART_ROWS), :] for s in range(sources)], axis=1)
        )
    result = jnp.dot(jnp.concatenate(picked, axis=0), forward_ref[...], preferred_element_type=F32)
    out_ref[...] = result.astype(out_ref.dtype)


def partial_spectrum(half, pencil, forward, dtype):
    _, block_rows, _ = pencil.shape
    vmem = pl.BlockSpec(memory_space=pltpu.VMEM)
    return pl.pallas_call(
        spectrum_kernel,
        in_specs=[pl.BlockSpec(memory_space=SMEM), vmem, vmem],
        out_specs=vmem,
        out_shape=jax.ShapeDtypeStruct((block_rows // 2, forward.shape[1]), dtype),
        compiler_params=pltpu.CompilerParams(vmem_limit_bytes=8 * 1024 * 1024),
        cost_estimate=pl.CostEstimate(
            flops=block_rows * forward.size, bytes_accessed=2 * pencil.size, transcendentals=0
        ),
        name="partial_spectrum",
    )(half, pencil, forward)


def mix_kernel(limit_ref, own_ref, other_ref, weight_ref, inverse_ref, out_hbm, spectrum, mixed, packed, sent):
    block_rows, _ = own_ref.shape
    pairs, _, _, width = weight_ref.shape
    local_modes = 2 * pairs
    channels = block_rows // local_modes
    planes = own_ref.shape[1] // width
    groups = channels // SUBLANES
    block = SUBLANES * 2 * local_modes
    low = low_half((SUBLANES, width))
    result = own_ref[...] + other_ref[...].astype(F32)
    for z in range(planes):
        lanes = slice(z * width, (z + 1) * width)
        for part in range(groups):
            for k in range(pairs):
                start = (part * local_modes + 2 * k) * SUBLANES
                real, imag = pair_halves(
                    result[start : start + SUBLANES, lanes], result[start + SUBLANES : start + 2 * SUBLANES, lanes]
                )
                spectrum[k, z, 0, pl.ds(part * SUBLANES, SUBLANES), :] = real
                spectrum[k, z, 1, pl.ds(part * SUBLANES, SUBLANES), :] = imag
    for k in range(pairs):
        keep = [jnp.where(limit_ref[0] > 2 * k + n, 1.0, 0.0).astype(F32) for n in range(2)]
        sums = [[[None, None] for _ in range(groups)] for _ in range(planes)]
        for i in range(channels):
            values = [
                [jnp.broadcast_to(spectrum[k, z, r, pl.ds(i, 1), :], (SUBLANES, width)) for r in range(2)]
                for z in range(planes)
            ]
            weights = [weight_ref[k, r, pl.ds(i * channels, channels), :].astype(F32) for r in range(2)]
            for g in range(groups):
                real, imag = (w[g * SUBLANES : (g + 1) * SUBLANES] for w in weights)
                for z in range(planes):
                    terms = (
                        real * values[z][0] - imag * values[z][1],
                        real * values[z][1] + imag * values[z][0],
                    )
                    for r in range(2):
                        old = sums[z][g][r]
                        sums[z][g][r] = terms[r] if old is None else old + terms[r]
        for z in range(planes):
            for g in range(groups):
                modes = pair_halves(*sums[z][g])
                for n in range(2):
                    kept = modes[n] * keep[n]
                    swapped = half_turn(kept)
                    start = g * block + 2 * k + n
                    mixed[z, pl.ds(start, SUBLANES, stride=2 * local_modes), :] = kept
                    mixed[z, pl.ds(start + local_modes, SUBLANES, stride=2 * local_modes), :] = jnp.where(
                        low, swapped, -swapped
                    )
    left = jnp.concatenate([mixed[z].astype(BF16) for z in range(planes)], axis=1)
    members = groups // 2
    wide = 2 * LANES
    leaving = []
    for t in range(inverse_ref.shape[1] // wide):
        back = jnp.dot(left, inverse_ref[:, t * wide : (t + 1) * wide], preferred_element_type=F32)
        for u in range(2):
            tile = slice(u * LANES, (u + 1) * LANES)
            for h in range(members):
                start = 2 * h * block
                pair = pair_halves(back[start : start + block, tile], back[start + block : start + 2 * block, tile])
                for n in range(2):
                    packed[(4 * t + 2 * u + n) * members + h] = pair[n].astype(BF16)
        blocks = pl.ds(4 * t * members, 4 * members)
        copy = pltpu.make_async_copy(packed.at[blocks], out_hbm.at[blocks], sent.at[t])
        copy.start()
        leaving.append(copy)
    for copy in leaving:
        copy.wait()


def mix(limit, own, other, weights, inverse, slabs, members):
    block_rows, _ = own.shape
    pairs, _, _, width = weights.shape
    channels = block_rows // (2 * pairs)
    planes = own.shape[1] // width
    rows = channels * 4 * pairs
    blocks = (slabs * members, SUBLANES * 4 * pairs, LANES)
    vmem = pl.BlockSpec(memory_space=pltpu.VMEM)
    return pl.pallas_call(
        mix_kernel,
        in_specs=[pl.BlockSpec(memory_space=SMEM)] + [vmem] * 4,
        out_specs=pl.BlockSpec(memory_space=pl.ANY),
        out_shape=jax.ShapeDtypeStruct(blocks, BF16),
        scratch_shapes=[
            pltpu.VMEM((pairs, planes, 2, channels, width), F32),
            pltpu.VMEM((planes, rows, width), F32),
            pltpu.VMEM(blocks, BF16),
            pltpu.SemaphoreType.DMA((slabs // 4,)),
        ],
        compiler_params=pltpu.CompilerParams(vmem_limit_bytes=8 * 1024 * 1024),
        cost_estimate=pl.CostEstimate(
            flops=2 * rows * inverse.size, bytes_accessed=4 * weights.size, transcendentals=0
        ),
        name="mix",
    )(limit, own, other, weights, inverse)


def pointwise_kernel(
    place_ref, strength_ref, bias_ref, weight_ref, base_ref, forcing_ref, out_ref, spread, native
):
    members, inner, out_rows, length_y = out_ref.shape
    channels, cell_rows, _ = base_ref.shape
    outer = channels // (members * inner)
    planes, y_blocks, slab_rows = cell_layout(cell_rows, length_y)
    depth = 2 * SUBLANES
    out_channels = channels // members
    me = place_ref[1]

    def spread_weight():
        tall = (out_channels * depth, channels)
        wide = (channels, channels * depth)
        row_of = lax.broadcasted_iota(jnp.int32, tall, 0) // depth + me * out_channels
        pick_rows = (row_of == lax.broadcasted_iota(jnp.int32, tall, 1)).astype(BF16)
        column_of = lax.broadcasted_iota(jnp.int32, wide, 1) // depth
        pick_columns = (column_of == lax.broadcasted_iota(jnp.int32, wide, 0)).astype(BF16)
        picked = jnp.dot(pick_rows, weight_ref[...], preferred_element_type=F32).astype(BF16)
        full = jnp.dot(picked, pick_columns, preferred_element_type=F32)
        same = lax.broadcasted_iota(jnp.int32, full.shape, 0) % depth == (
            lax.broadcasted_iota(jnp.int32, full.shape, 1) % depth
        )
        spread[...] = jnp.where(same, 2.0 * full, 0.0).astype(BF16)

    spread_weight()

    def body(step, carry):
        rows = pl.ds(pl.multiple_of(step * depth, depth), depth)
        forcing = forcing_ref[rows, :].astype(F32)
        fields = []
        for m in range(members):
            parts = [
                half_field(base_ref[c, rows, :], forcing, strength_ref[m * channels + c]).astype(BF16)
                for c in range(channels)
            ]
            fields.append(jnp.concatenate(parts, axis=0))
        result = jnp.dot(spread[...], jnp.concatenate(fields, axis=1), preferred_element_type=F32)
        for a in range(outer):
            for b in range(inner):
                o = a * inner + b
                bias = bias_ref[me * out_channels + o]
                for m in range(members):
                    cells = result[o * depth : (o + 1) * depth, m * LANES : (m + 1) * LANES] + bias
                    native[m, a, b, rows, :] = cells
        return carry

    lax.fori_loop(0, cell_rows // depth, body, 0)

    def arrange(b, carry):
        for m in range(members):
            for a in range(outer):
                for z in range(planes):
                    rows = pl.ds((a * planes + z) * slab_rows, slab_rows)
                    for j in range(y_blocks):
                        picked = native[m, a, b, pl.ds(j * planes + z, slab_rows, stride=planes * y_blocks), :]
                        out_ref[m, b, rows, pl.ds(j * LANES, LANES)] = picked.astype(BF16)
        return carry

    lax.fori_loop(0, inner, arrange, 0)


def pointwise(place, strengths, bias, weight, cells, forcing, length_y):
    channels, cell_rows, _ = cells.shape
    members = strengths.shape[0] // channels
    depth = 2 * SUBLANES
    inner = SUBLANES
    outer = channels // members // inner
    spread = (channels // members * depth, channels * depth)
    smem = pl.BlockSpec(memory_space=SMEM)
    vmem = pl.BlockSpec(memory_space=pltpu.VMEM)
    return pl.pallas_call(
        pointwise_kernel,
        in_specs=[smem] * 3 + [vmem] * 3,
        out_specs=vmem,
        out_shape=pltpu.VMEM((members, inner, outer * cell_rows * LANES // length_y, length_y), BF16),
        scratch_shapes=[
            pltpu.VMEM(spread, BF16),
            pltpu.VMEM((members, outer, inner, cell_rows, LANES), F32),
        ],
        compiler_params=pltpu.CompilerParams(vmem_limit_bytes=16 * 1024 * 1024),
        cost_estimate=pl.CostEstimate(
            flops=4 * spread[0] * spread[1] * members * cell_rows // depth * LANES,
            bytes_accessed=8 * cells.size,
            transcendentals=members * cells.size,
        ),
        name="pointwise",
    )(place, strengths, bias, weight, *in_hbm(cells, forcing))


def layer_kernel(back_ref, table_ref, point_ref, out_hbm, columns, native, result, sent):
    members, inner, rows, length_y = point_ref.shape
    _, outer, cell_rows, _ = native.shape
    sources, block_rows, _ = back_ref.shape
    slabs = sources // members
    depth = block_rows // inner
    planes, y_blocks, slab_rows = cell_layout(cell_rows, length_y)
    leaving = [pltpu.make_async_copy(result.at[:, b], out_hbm.at[:, b], sent.at[b]) for b in range(inner)]
    for m in range(members):
        for s in range(slabs):
            block = back_ref[s * members + m].astype(F32)
            for b in range(inner):
                columns[b, m, pl.ds(s * depth, depth), :] = block[b * depth : (b + 1) * depth]
    for b in range(inner):
        turn = b % 2
        total = None
        for m in range(members):
            spectral = lax.dot_general(
                columns[b, m].astype(BF16), table_ref[...], (((0,), (0,)), ((), ())), preferred_element_type=F32
            )
            value = jax.nn.gelu(point_ref[m, b].astype(F32) + spectral, approximate=True)
            total = value if total is None else total + value
        total = total * (1.0 / members)
        for a in range(outer):
            for z in range(planes):
                start = (a * planes + z) * slab_rows
                for j in range(y_blocks):
                    native[turn, a, pl.ds(j * planes + z, slab_rows, stride=planes * y_blocks), :] = total[
                        start : start + slab_rows, j * LANES : (j + 1) * LANES
                    ]
        for a in range(outer):
            result[a, b] = native[turn, a].astype(BF16)
        leaving[b].start()
    for copy in leaving:
        copy.wait()


def layer(back, points, outer, length_x, modes_y, slabs):
    members, inner, rows, length_y = points.shape
    cell_rows = rows * length_y // (outer * LANES)
    table = inverse_y_table(modes_y, length_y, length_x, slabs)
    vmem = pl.BlockSpec(memory_space=pltpu.VMEM)
    return pl.pallas_call(
        layer_kernel,
        in_specs=[vmem, vmem, vmem],
        out_specs=pl.BlockSpec(memory_space=pl.ANY),
        out_shape=pltpu.HBM((outer, inner, cell_rows, LANES), BF16),
        scratch_shapes=[
            pltpu.VMEM((inner, members, 2 * modes_y, LANES), F32),
            pltpu.VMEM((2, outer, cell_rows, LANES), F32),
            pltpu.VMEM((outer, inner, cell_rows, LANES), BF16),
            pltpu.SemaphoreType.DMA((inner,)),
        ],
        compiler_params=pltpu.CompilerParams(vmem_limit_bytes=16 * 1024 * 1024),
        cost_estimate=pl.CostEstimate(
            flops=4 * modes_y * points.size, bytes_accessed=5 * points.size, transcendentals=points.size
        ),
        name="layer",
    )(back, table, points)


def fast_local(
    base_field,
    forcing,
    load,
    amplitudes,
    amp_index,
    mode_count,
    point_weight,
    point_bias,
    spectral_weight,
):
    channels, slab_rows, planes, length_y = base_field.shape
    slabs, members = lax.axis_size("slab"), lax.axis_size("member")
    local_modes, modes_x = spectral_weight.shape[:2]
    modes_y = local_modes * slabs
    length_x = slab_rows * slabs
    y_blocks = length_y // LANES
    cells = base_field.reshape(channels, slab_rows, planes, y_blocks, LANES).transpose(0, 1, 3, 2, 4)
    cells = cells.reshape(channels, slab_rows * SUBLANES, LANES)
    force = forcing.reshape(slab_rows, planes, y_blocks, LANES).transpose(0, 2, 1, 3)
    force = force.reshape(slab_rows * SUBLANES, LANES)
    owners = slabs // 2
    slab, me = lax.axis_index("slab"), lax.axis_index("member")
    half = slab // owners
    place = jnp.stack([half, me])
    other_half = jnp.reshape(1 - half, (1,))
    partners = [(n, (n + owners) % slabs) for n in range(slabs)]
    index = amp_index.reshape(1, 1)
    other_index = lax.ppermute(index, "member", [(n, 1 - n) for n in range(2)])
    out_channels = channels // members
    packed = y_modes(index, amplitudes, load, cells, force, slabs, modes_y, length_y)
    pencil = lax.all_to_all(
        packed,
        "slab",
        split_axis=0,
        concat_axis=0,
        tiled=True,
        axis_index_groups=[list(range(h * owners, (h + 1) * owners)) for h in range(2)],
    )
    strengths, weights, forward, inverse = prepare(
        place, index, other_index, amplitudes, load, spectral_weight.transpose(0, 2, 3, 4, 1), length_x, slabs, planes
    )
    leaving = partial_spectrum(other_half, pencil, forward, BF16)
    other = lax.ppermute(leaving, "slab", partners)
    own = partial_spectrum(place, pencil, forward, F32)
    back = mix(mode_count - slab * local_modes, own, other, weights, inverse, slabs, members)
    back = lax.all_to_all(back, ("slab", "member"), split_axis=0, concat_axis=0, tiled=True)
    points = pointwise(place, strengths, point_bias, point_weight, cells, force, length_y)
    result = layer(back, points, out_channels // SUBLANES, length_x, modes_y, slabs)
    result = result.reshape(out_channels, slab_rows, y_blocks, planes, LANES).transpose(0, 1, 3, 2, 4)
    return result.reshape(out_channels, slab_rows, planes, length_y)


def tiles_fit(base_shape, weight_shape, slabs, members):
    channels, slab_rows, planes, length_y = base_shape
    local_modes, modes_x = weight_shape[:2]
    return (
        2 * planes * slab_rows == LANES
        and 2 * modes_x == LANES
        and planes * length_y == SUBLANES * LANES
        and 2 * local_modes == SUBLANES
        and 2 * SUBLANES * members == channels
        and slabs % 4 == 0
    )


def phases(frequency, positions, length):
    product = frequency[:, None] * positions[None, :] % length
    angles = product.astype(jnp.float32) * (TWO_PI / length)
    return (jnp.cos(angles), jnp.sin(angles))


def forward_x(pencil, cos_table, sin_table):
    row_total = pencil.shape[0]
    modes = cos_table.shape[0]
    with_cos = jnp.einsum(
        "kxf,mx->kmf", pencil, cos_table, preferred_element_type=jnp.float32
    ).reshape(row_total, modes, 2, -1)
    with_sin = jnp.einsum(
        "kxf,mx->kmf", pencil, sin_table, preferred_element_type=jnp.float32
    ).reshape(row_total, modes, 2, -1)
    real_part = with_cos[:, :, 0] + with_sin[:, :, 1]
    imag_part = with_cos[:, :, 1] - with_sin[:, :, 0]
    return jnp.stack([real_part, imag_part], axis=2).reshape(row_total, modes, -1)


def inverse_x(spectra, cos_table, sin_table):
    row_total = spectra.shape[0]
    points = cos_table.shape[1]
    with_cos = jnp.einsum(
        "kmf,mx->kxf", spectra, cos_table, preferred_element_type=jnp.float32
    ).reshape(row_total, points, 2, -1)
    with_sin = jnp.einsum(
        "kmf,mx->kxf", spectra, sin_table, preferred_element_type=jnp.float32
    ).reshape(row_total, points, 2, -1)
    real_part = with_cos[:, :, 0] - with_sin[:, :, 1]
    imag_part = with_cos[:, :, 1] + with_sin[:, :, 0]
    return jnp.stack([real_part, imag_part], axis=2).reshape(row_total, points, -1)


def mixing(weights, values):
    return jnp.einsum("kmoi,kmiz->kmoz", weights, values, preferred_element_type=jnp.float32)


def general_local(
    base_field,
    forcing,
    load,
    amplitudes,
    amp_index,
    mode_count,
    point_weight,
    point_bias,
    spectral_weight,
):
    channels, slab_rows, plane_count, length_y = base_field.shape
    slab_count = lax.axis_size("slab")
    local_modes = spectral_weight.shape[0]
    modes_y = local_modes * slab_count
    modes_x = spectral_weight.shape[1]
    length_x = slab_rows * slab_count
    packed_width = 2 * channels * plane_count
    slab_index = lax.axis_index("slab")
    level_ids = jnp.arange(amplitudes.shape[0], dtype=jnp.int32)
    amplitude = jnp.sum(jnp.where(level_ids == amp_index[0], amplitudes, 0.0))
    driven = base_field.astype(jnp.float32) + amplitude * load[:, None, None, None] * forcing[
        None
    ].astype(jnp.float32)
    field_now = (2.0 * jnp.tanh(0.5 * driven)).astype(jnp.bfloat16)
    y_cos, y_sin = phases(
        jnp.arange(modes_y, dtype=jnp.int32), jnp.arange(length_y, dtype=jnp.int32), length_y
    )
    y_real = jnp.einsum(
        "cxzy,ky->kxcz", field_now, y_cos.astype(jnp.bfloat16), preferred_element_type=jnp.float32
    )
    y_imag = -jnp.einsum(
        "cxzy,ky->kxcz", field_now, y_sin.astype(jnp.bfloat16), preferred_element_type=jnp.float32
    )
    packed = (
        jnp.stack([y_real, y_imag], axis=2)
        .astype(jnp.bfloat16)
        .reshape(modes_y, slab_rows, packed_width)
    )
    frequency_x = jnp.concatenate(
        [
            jnp.arange(modes_x // 2, dtype=jnp.int32),
            jnp.arange(length_x - modes_x // 2, length_x, dtype=jnp.int32),
        ]
    )
    full_cos, full_sin = phases(frequency_x, jnp.arange(length_x, dtype=jnp.int32), length_x)
    full_cos = full_cos.astype(jnp.bfloat16)
    full_sin = full_sin.astype(jnp.bfloat16)
    pencil = lax.all_to_all(packed, "slab", split_axis=0, concat_axis=1, tiled=True)
    spectrum = forward_x(pencil, full_cos, full_sin)
    spectrum = spectrum.astype(jnp.bfloat16).reshape(local_modes, modes_x, 2, channels, plane_count)
    weight_real = spectral_weight[:, :, 0]
    weight_imag = spectral_weight[:, :, 1]
    spec_real = spectrum[:, :, 0]
    spec_imag = spectrum[:, :, 1]
    mix_real = mixing(weight_real, spec_real) - mixing(weight_imag, spec_imag)
    mix_imag = mixing(weight_real, spec_imag) + mixing(weight_imag, spec_real)
    global_modes = slab_index * local_modes + jnp.arange(local_modes, dtype=jnp.int32)
    keep = (global_modes < mode_count[0]).astype(jnp.float32)[:, None, None, None, None]
    mixed = (
        (jnp.stack([mix_real, mix_imag], axis=2) * keep)
        .astype(jnp.bfloat16)
        .reshape(local_modes, modes_x, packed_width)
    )
    back = inverse_x(mixed, full_cos, full_sin).astype(jnp.bfloat16)
    returned = lax.all_to_all(back, "slab", split_axis=1, concat_axis=0, tiled=True)
    returned = returned.reshape(modes_y, slab_rows, 2, channels, plane_count)
    weights_y = jnp.where(jnp.arange(modes_y) == 0, 1.0, 2.0).astype(jnp.float32) / (
        length_x * length_y
    )
    back_cos = (weights_y[:, None] * y_cos).astype(jnp.bfloat16)
    back_sin = (weights_y[:, None] * y_sin).astype(jnp.bfloat16)
    spectral = jnp.einsum(
        "kxcz,ky->cxzy", returned[:, :, 0], back_cos, preferred_element_type=jnp.float32
    )
    spectral = spectral - jnp.einsum(
        "kxcz,ky->cxzy", returned[:, :, 1], back_sin, preferred_element_type=jnp.float32
    )
    pointwise = (
        jnp.einsum("oc,cxzy->oxzy", point_weight, field_now, preferred_element_type=jnp.float32)
        + point_bias[:, None, None, None]
    )
    layer = jax.nn.gelu(pointwise + spectral, approximate=True).astype(jnp.bfloat16)
    layer = lax.optimization_barrier(layer).astype(jnp.float32)
    total = lax.psum_scatter(
        layer.astype(jnp.bfloat16), "member", scatter_dimension=0, tiled=True
    ).astype(jnp.float32)
    return (total / lax.axis_size("member")).astype(jnp.bfloat16)


def local(base_field, forcing, load, amplitudes, amp_index, mode_count, point_weight, point_bias, spectral_weight):
    fits = tiles_fit(
        base_field.shape, spectral_weight.shape, lax.axis_size("slab"), lax.axis_size("member")
    )
    return (fast_local if fits else general_local)(
        base_field,
        forcing,
        load,
        amplitudes,
        amp_index,
        mode_count,
        point_weight,
        point_bias,
        spectral_weight,
    )


def solution(mesh):
    in_specs = (
        P(None, "slab", None, None),
        P("slab", None, None),
        P(),
        P(),
        P("member"),
        P("member"),
        P(),
        P(),
        P("slab", None, None, None, None),
    )
    out_specs = P("member", "slab", None, None)
    return jax.shard_map(local, mesh=mesh, in_specs=in_specs, out_specs=out_specs, check_vma=False)
```

```python
import math

import jax
import jax.numpy as jnp
import numpy as np
from jax import lax
from jax.experimental import pallas as pl
from jax.experimental.pallas import tpu as pltpu
from jax.sharding import PartitionSpec as P

TWO_PI = 2.0 * math.pi
LANES = 128
SUBLANES = 8
FORCING_ROWS = 64
PART_ROWS = SUBLANES * SUBLANES // 2
SMEM = pltpu.SMEM
F32 = jnp.float32
BF16 = jnp.bfloat16


def host_phases(frequency, positions, length):
    product = frequency[:, None] * positions[None, :] % length
    angles = product.astype(np.float32) * np.float32(TWO_PI / length)
    return np.cos(angles), np.sin(angles)


def first_frequencies(modes_x, length_x):
    return np.concatenate([np.arange(modes_x // 2), np.arange(length_x - modes_x // 2, length_x)])


def as_bf16(table):
    return jnp.asarray(table.astype(BF16))


def by_owner(table, slabs):
    modes, length = table.shape
    local = modes // slabs
    return table.reshape(2, slabs // 2, local, length).transpose(1, 0, 2, 3)


def forward_y_table(modes_y, length_y, slabs):
    cos, sin = host_phases(np.arange(modes_y), np.arange(length_y), length_y)
    table = np.stack([by_owner(cos, slabs), by_owner(-sin, slabs)], axis=0)
    return as_bf16(2.0 * table.astype(BF16).astype(np.float32).reshape(2 * modes_y, length_y))


def inverse_y_table(modes_y, length_y, length_x, slabs):
    cos, sin = host_phases(np.arange(modes_y), np.arange(length_y), length_y)
    scale = np.where(np.arange(modes_y) == 0, 1.0, 2.0).astype(np.float32)
    scale = (scale / np.float32(length_x * length_y))[:, None]
    parts = np.stack([scale * cos, -(scale * sin)], axis=0)
    parts = parts.reshape(2, slabs, modes_y // slabs, length_y).transpose(1, 0, 2, 3)
    return as_bf16(parts.reshape(2 * modes_y, length_y))


def forward_x_table(modes_x, length_x, slabs, planes):
    cos, sin = host_phases(first_frequencies(modes_x, length_x), np.arange(length_x), length_x)
    whole = np.array([[cos, -sin], [sin, cos]])
    whole = whole.reshape(2, 2, modes_x, 2, slabs // 2, length_x // slabs)
    table = np.einsum("abqhsx,zw->hsazxwbq", whole, np.eye(planes, dtype=np.float32))
    return as_bf16(table.reshape(2, planes * length_x, planes * 2 * modes_x))


def inverse_x_table(modes_x, length_x, slabs, planes):
    cos, sin = host_phases(first_frequencies(modes_x, length_x), np.arange(length_x), length_x)
    whole = np.array([cos, -sin]).reshape(2, modes_x, slabs, length_x // slabs)
    table = np.einsum("aqsx,zw->zaqswx", whole, np.eye(planes, dtype=np.float32))
    return as_bf16(table.reshape(planes * 2 * modes_x, planes * length_x))


def low_half(shape):
    return lax.broadcasted_iota(jnp.int32, shape, len(shape) - 1) < shape[-1] // 2


def half_turn(values):
    return pltpu.roll(values, values.shape[-1] // 2, values.ndim - 1)


def pair_halves(first, second):
    low = low_half(first.shape)
    return (
        jnp.where(low, first, half_turn(second)),
        jnp.where(low, half_turn(first), second),
    )


def half_field(base, forcing, strength):
    return jnp.tanh(0.5 * (base.astype(F32) + strength * forcing))


def double_gelu(x):
    scale = math.sqrt(2.0 / math.pi)
    return x * (1.0 + jnp.tanh(x * (scale + (0.044715 * scale) * (x * x))))


def cell_layout(cell_rows, length_y):
    y_blocks = length_y // LANES
    planes = SUBLANES // y_blocks
    return planes, y_blocks, cell_rows // SUBLANES


def in_hbm(*arrays):
    return [pltpu.with_memory_space_constraint(a, pltpu.HBM) for a in arrays]


def y_modes_kernel(
    index_any,
    amplitude_hbm,
    load_hbm,
    cells_hbm,
    forcing_hbm,
    table_hbm,
    out_hbm,
    index,
    amplitudes,
    load,
    cells,
    forcing,
    forcing_wide,
    table,
    field,
    rows,
    modes,
    packed,
    arrived,
    sent,
):
    channels, cell_rows, _ = cells.shape
    width = field.shape[1]
    groups = [(c, width) for c in range(0, channels, width)]
    planes, y_blocks, slab_rows = cell_layout(cell_rows, table.shape[1])
    modes_y = table.shape[0] // 2
    span = planes * slab_rows
    owners, block_rows, _ = out_hbm.shape
    part_rows = block_rows // (channels // width)
    small = [
        pltpu.make_async_copy(source, target, arrived.at[n])
        for n, (source, target) in enumerate(
            [
                (index_any, index),
                (amplitude_hbm, amplitudes),
                (load_hbm, load),
                (forcing_hbm, forcing),
                (table_hbm, table),
            ]
        )
    ]
    large = [
        pltpu.make_async_copy(
            cells_hbm.at[pl.ds(first, count)], cells.at[pl.ds(first, count)], arrived.at[len(small) + n]
        )
        for n, (first, count) in enumerate(groups)
    ]
    for copy in small[:4] + large[:1] + small[4:] + large[1:]:
        copy.start()
    for copy in small[:4]:
        copy.wait()
    amplitude = amplitudes[index[0, 0]]
    forcing_wide[...] = forcing[...].astype(F32)
    small[4].wait()
    leaving = [
        pltpu.make_async_copy(packed.at[g], out_hbm.at[:, pl.ds(g * part_rows, part_rows), :], sent.at[g])
        for g in range(channels // width)
    ]
    for step in range(len(groups) + 1):
        if step < len(groups):
            first, count = groups[step]
            large[step].wait()
            strengths = [amplitude * load[first + c] for c in range(count)]
            for start in range(0, cell_rows, FORCING_ROWS):
                some = pl.ds(start, FORCING_ROWS)
                force = forcing_wide[some, :]
                for c in range(count):
                    field[step % 2, c, some, :] = half_field(cells[first + c, some, :], force, strengths[c])
            for c in range(count):
                for z in range(planes):
                    for j in range(y_blocks):
                        picked = field[step % 2, c, pl.ds(j * planes + z, slab_rows, stride=planes * y_blocks), :]
                        rows[
                            step % 2, pl.ds(c * span + z * slab_rows, slab_rows), pl.ds(j * LANES, LANES)
                        ] = picked.astype(BF16)
        if step > 0:
            first, count = groups[step - 1]
            result = lax.dot_general(
                table[...],
                rows[(step - 1) % 2, pl.ds(0, count * span), :],
                (((1,), (1,)), ((), ())),
                preferred_element_type=F32,
            )
            part, place = divmod(first, width)
            for t in range(count // 2):
                tile = slice(t * LANES, (t + 1) * LANES)
                pair = pair_halves(result[:modes_y, tile], result[modes_y:, tile])
                for n in range(2):
                    modes[part % 2, pl.ds(place + 2 * t + n, modes_y, stride=width), :] = pair[n]
            if place + count == width:
                for d in range(owners):
                    packed[part, d] = modes[part % 2, pl.ds(d * part_rows, part_rows), :].astype(BF16)
                leaving[part].start()
    for copy in leaving:
        copy.wait()


def y_modes(amp_index, amplitudes, load, cells, forcing, slabs, modes_y, length_y):
    channels, cell_rows, _ = cells.shape
    width = SUBLANES
    parts = channels // width
    owners = slabs // 2
    block_rows = modes_y // owners * channels
    table = forward_y_table(modes_y, length_y, slabs)
    planes, _, slab_rows = cell_layout(cell_rows, length_y)
    operands = in_hbm(amplitudes, load, cells, forcing, table)
    anywhere = pl.BlockSpec(memory_space=pl.ANY)
    return pl.pallas_call(
        y_modes_kernel,
        in_specs=[anywhere] * (1 + len(operands)),
        out_specs=anywhere,
        out_shape=jax.ShapeDtypeStruct((owners, block_rows, LANES), BF16),
        scratch_shapes=[
            SMEM(amp_index.shape, jnp.int32),
            SMEM(amplitudes.shape, F32),
            SMEM(load.shape, F32),
            pltpu.VMEM(cells.shape, BF16),
            pltpu.VMEM(forcing.shape, BF16),
            pltpu.VMEM(forcing.shape, F32),
            pltpu.VMEM(table.shape, BF16),
            pltpu.VMEM((2, width, cell_rows, LANES), F32),
            pltpu.VMEM((2, width * planes * slab_rows, length_y), BF16),
            pltpu.VMEM((2, modes_y * width, LANES), F32),
            pltpu.VMEM((parts, owners, block_rows // parts, LANES), BF16),
            pltpu.SemaphoreType.DMA((5 + parts,)),
            pltpu.SemaphoreType.DMA((parts,)),
        ],
        compiler_params=pltpu.CompilerParams(vmem_limit_bytes=12 * 1024 * 1024),
        cost_estimate=pl.CostEstimate(
            flops=4 * modes_y * cells.size, bytes_accessed=4 * cells.size, transcendentals=cells.size
        ),
        name="y_modes",
    )(amp_index, *operands)


def prepare_kernel(
    half_ref,
    own_any,
    other_any,
    amplitude_ref,
    load_ref,
    weight_ref,
    forward_hbm,
    inverse_hbm,
    strengths,
    weights,
    forward,
    inverse,
    wide,
    indices,
    arrived,
):
    half, me = half_ref[0], half_ref[1]
    copies = [
        pltpu.make_async_copy(forward_hbm.at[half], forward, arrived.at[0]),
        pltpu.make_async_copy(inverse_hbm, inverse, arrived.at[1]),
        pltpu.make_async_copy(own_any, indices.at[pl.ds(0, 1)], arrived.at[2]),
        pltpu.make_async_copy(other_any, indices.at[pl.ds(1, 1)], arrived.at[3]),
    ]
    for copy in copies:
        copy.start()
    local_modes, parts, channels, _, _ = weight_ref.shape
    for k in range(local_modes // 2):
        for r in range(parts):
            for o in range(channels):
                pair = [weight_ref[2 * k + n, r, o].astype(F32) for n in range(2)]
                wide[k, r, pl.ds(o, channels, stride=channels), :] = jnp.concatenate(pair, axis=1)
    weights[...] = wide[...].astype(BF16)
    for copy in copies:
        copy.wait()
    for m in range(2):
        amplitude = amplitude_ref[indices[lax.rem(me + m, 2), 0]]
        for c in range(channels):
            strengths[m * channels + c] = amplitude * load_ref[c]


def prepare(place, own, other, amplitudes, load, spectral_weight, length_x, slabs, planes):
    local_modes, parts, channels, _, modes_x = spectral_weight.shape
    forward = forward_x_table(modes_x, length_x, slabs, planes)
    inverse = inverse_x_table(modes_x, length_x, slabs, planes)
    wide = (local_modes // 2, parts, channels * channels, 2 * modes_x)
    vmem = pl.BlockSpec(memory_space=pltpu.VMEM)
    smem = pl.BlockSpec(memory_space=SMEM)
    anywhere = pl.BlockSpec(memory_space=pl.ANY)
    return pl.pallas_call(
        prepare_kernel,
        in_specs=[smem] + [anywhere] * 2 + [smem] * 2 + [vmem] + [anywhere] * 2,
        out_specs=[smem] + [vmem] * 3,
        out_shape=[
            jax.ShapeDtypeStruct((2 * channels,), F32),
            pltpu.VMEM(wide, BF16),
            pltpu.VMEM(forward.shape[1:], BF16),
            pltpu.VMEM(inverse.shape, BF16),
        ],
        scratch_shapes=[pltpu.VMEM(wide, F32), SMEM((2, 1), jnp.int32), pltpu.SemaphoreType.DMA((4,))],
        compiler_params=pltpu.CompilerParams(vmem_limit_bytes=16 * 1024 * 1024),
        cost_estimate=pl.CostEstimate(
            flops=4 * spectral_weight.size, bytes_accessed=10 * spectral_weight.size, transcendentals=0
        ),
        name="prepare",
    )(place, own, other, amplitudes, load, *in_hbm(spectral_weight, forward, inverse))


def spectrum_kernel(half_ref, pencil_ref, forward_ref, out_ref):
    sources, block_rows, _ = pencil_ref.shape
    rows = out_ref.shape[0]
    parts = rows // PART_ROWS
    picked = []
    for part in range(parts):
        start = pl.multiple_of((2 * part + half_ref[0]) * PART_ROWS, PART_ROWS)
        picked.append(
            jnp.concatenate([pencil_ref[s, pl.ds(start, PART_ROWS), :] for s in range(sources)], axis=1)
        )
    result = jnp.dot(jnp.concatenate(picked, axis=0), forward_ref[...], preferred_element_type=F32)
    out_ref[...] = result.astype(out_ref.dtype)


def partial_spectrum(half, pencil, forward, dtype):
    _, block_rows, _ = pencil.shape
    vmem = pl.BlockSpec(memory_space=pltpu.VMEM)
    return pl.pallas_call(
        spectrum_kernel,
        in_specs=[pl.BlockSpec(memory_space=SMEM), vmem, vmem],
        out_specs=vmem,
        out_shape=jax.ShapeDtypeStruct((block_rows // 2, forward.shape[1]), dtype),
        compiler_params=pltpu.CompilerParams(vmem_limit_bytes=8 * 1024 * 1024),
        cost_estimate=pl.CostEstimate(
            flops=block_rows * forward.size, bytes_accessed=2 * pencil.size, transcendentals=0
        ),
        name="partial_spectrum",
    )(half, pencil, forward)


def mix_kernel(limit_ref, own_ref, other_ref, weight_ref, inverse_ref, out_hbm, spectrum, mixed, packed, sent):
    block_rows, _ = own_ref.shape
    pairs, _, _, width = weight_ref.shape
    local_modes = 2 * pairs
    channels = block_rows // local_modes
    planes = own_ref.shape[1] // width
    groups = channels // SUBLANES
    block = SUBLANES * 2 * local_modes
    low = low_half((SUBLANES, width))
    result = own_ref[...] + other_ref[...].astype(F32)
    for z in range(planes):
        lanes = slice(z * width, (z + 1) * width)
        for part in range(groups):
            for k in range(pairs):
                start = (part * local_modes + 2 * k) * SUBLANES
                real, imag = pair_halves(
                    result[start : start + SUBLANES, lanes], result[start + SUBLANES : start + 2 * SUBLANES, lanes]
                )
                spectrum[k, z, 0, pl.ds(part * SUBLANES, SUBLANES), :] = real
                spectrum[k, z, 1, pl.ds(part * SUBLANES, SUBLANES), :] = imag
    for k in range(pairs):
        keep = [jnp.where(limit_ref[0] > 2 * k + n, 1.0, 0.0).astype(F32) for n in range(2)]
        sums = [[[None, None] for _ in range(groups)] for _ in range(planes)]
        for i in range(channels):
            values = [
                [jnp.broadcast_to(spectrum[k, z, r, pl.ds(i, 1), :], (SUBLANES, width)) for r in range(2)]
                for z in range(planes)
            ]
            weights = [weight_ref[k, r, pl.ds(i * channels, channels), :].astype(F32) for r in range(2)]
            for g in range(groups):
                real, imag = (w[g * SUBLANES : (g + 1) * SUBLANES] for w in weights)
                for z in range(planes):
                    terms = (
                        real * values[z][0] - imag * values[z][1],
                        real * values[z][1] + imag * values[z][0],
                    )
                    for r in range(2):
                        old = sums[z][g][r]
                        sums[z][g][r] = terms[r] if old is None else old + terms[r]
        for z in range(planes):
            for g in range(groups):
                modes = pair_halves(*sums[z][g])
                for n in range(2):
                    kept = modes[n] * keep[n]
                    swapped = half_turn(kept)
                    start = g * block + 2 * k + n
                    mixed[z, pl.ds(start, SUBLANES, stride=2 * local_modes), :] = kept
                    mixed[z, pl.ds(start + local_modes, SUBLANES, stride=2 * local_modes), :] = jnp.where(
                        low, swapped, -swapped
                    )
    left = jnp.concatenate([mixed[z].astype(BF16) for z in range(planes)], axis=1)
    members = groups // 2
    wide = 2 * LANES
    leaving = []
    for t in range(inverse_ref.shape[1] // wide):
        back = jnp.dot(left, inverse_ref[:, t * wide : (t + 1) * wide], preferred_element_type=F32)
        for u in range(2):
            tile = slice(u * LANES, (u + 1) * LANES)
            for h in range(members):
                start = 2 * h * block
                pair = pair_halves(back[start : start + block, tile], back[start + block : start + 2 * block, tile])
                for n in range(2):
                    packed[(4 * t + 2 * u + n) * members + h] = pair[n].astype(BF16)
        blocks = pl.ds(4 * t * members, 4 * members)
        copy = pltpu.make_async_copy(packed.at[blocks], out_hbm.at[blocks], sent.at[t])
        copy.start()
        leaving.append(copy)
    for copy in leaving:
        copy.wait()


def mix(limit, own, other, weights, inverse, slabs, members):
    block_rows, _ = own.shape
    pairs, _, _, width = weights.shape
    channels = block_rows // (2 * pairs)
    planes = own.shape[1] // width
    rows = channels * 4 * pairs
    blocks = (slabs * members, SUBLANES * 4 * pairs, LANES)
    vmem = pl.BlockSpec(memory_space=pltpu.VMEM)
    return pl.pallas_call(
        mix_kernel,
        in_specs=[pl.BlockSpec(memory_space=SMEM)] + [vmem] * 4,
        out_specs=pl.BlockSpec(memory_space=pl.ANY),
        out_shape=jax.ShapeDtypeStruct(blocks, BF16),
        scratch_shapes=[
            pltpu.VMEM((pairs, planes, 2, channels, width), F32),
            pltpu.VMEM((planes, rows, width), F32),
            pltpu.VMEM(blocks, BF16),
            pltpu.SemaphoreType.DMA((slabs // 4,)),
        ],
        compiler_params=pltpu.CompilerParams(vmem_limit_bytes=8 * 1024 * 1024),
        cost_estimate=pl.CostEstimate(
            flops=2 * rows * inverse.size, bytes_accessed=4 * weights.size, transcendentals=0
        ),
        name="mix",
    )(limit, own, other, weights, inverse)


def pointwise_kernel(
    place_ref, strength_ref, bias_ref, weight_ref, base_ref, forcing_ref, out_ref, spread, native
):
    members, inner, out_rows, length_y = out_ref.shape
    channels, cell_rows, _ = base_ref.shape
    outer = channels // (members * inner)
    planes, y_blocks, slab_rows = cell_layout(cell_rows, length_y)
    depth = 2 * SUBLANES
    out_channels = channels // members
    me = place_ref[1]

    def spread_weight():
        tall = (out_channels * depth, channels)
        wide = (channels, channels * depth)
        row_of = lax.broadcasted_iota(jnp.int32, tall, 0) // depth + me * out_channels
        pick_rows = (row_of == lax.broadcasted_iota(jnp.int32, tall, 1)).astype(BF16)
        column_of = lax.broadcasted_iota(jnp.int32, wide, 1) // depth
        pick_columns = (column_of == lax.broadcasted_iota(jnp.int32, wide, 0)).astype(BF16)
        picked = jnp.dot(pick_rows, weight_ref[...], preferred_element_type=F32).astype(BF16)
        full = jnp.dot(picked, pick_columns, preferred_element_type=F32)
        same = lax.broadcasted_iota(jnp.int32, full.shape, 0) % depth == (
            lax.broadcasted_iota(jnp.int32, full.shape, 1) % depth
        )
        spread[...] = jnp.where(same, 2.0 * full, 0.0).astype(BF16)

    spread_weight()

    def body(step, carry):
        rows = pl.ds(pl.multiple_of(step * depth, depth), depth)
        forcing = forcing_ref[rows, :].astype(F32)
        fields = []
        for m in range(members):
            parts = [
                half_field(base_ref[c, rows, :], forcing, strength_ref[m * channels + c]).astype(BF16)
                for c in range(channels)
            ]
            fields.append(jnp.concatenate(parts, axis=0))
        result = jnp.dot(spread[...], jnp.concatenate(fields, axis=1), preferred_element_type=F32)
        for a in range(outer):
            for b in range(inner):
                o = a * inner + b
                bias = bias_ref[me * out_channels + o]
                for m in range(members):
                    cells = result[o * depth : (o + 1) * depth, m * LANES : (m + 1) * LANES] + bias
                    native[m, a, b, rows, :] = cells
        return carry

    lax.fori_loop(0, cell_rows // depth, body, 0)

    def arrange(b, carry):
        for m in range(members):
            for a in range(outer):
                for z in range(planes):
                    rows = pl.ds((a * planes + z) * slab_rows, slab_rows)
                    for j in range(y_blocks):
                        picked = native[m, a, b, pl.ds(j * planes + z, slab_rows, stride=planes * y_blocks), :]
                        out_ref[m, b, rows, pl.ds(j * LANES, LANES)] = picked.astype(BF16)
        return carry

    lax.fori_loop(0, inner, arrange, 0)


def pointwise(place, strengths, bias, weight, cells, forcing, length_y):
    channels, cell_rows, _ = cells.shape
    members = strengths.shape[0] // channels
    depth = 2 * SUBLANES
    inner = SUBLANES
    outer = channels // members // inner
    spread = (channels // members * depth, channels * depth)
    smem = pl.BlockSpec(memory_space=SMEM)
    vmem = pl.BlockSpec(memory_space=pltpu.VMEM)
    return pl.pallas_call(
        pointwise_kernel,
        in_specs=[smem] * 3 + [vmem] * 3,
        out_specs=vmem,
        out_shape=pltpu.VMEM((members, inner, outer * cell_rows * LANES // length_y, length_y), BF16),
        scratch_shapes=[
            pltpu.VMEM(spread, BF16),
            pltpu.VMEM((members, outer, inner, cell_rows, LANES), F32),
        ],
        compiler_params=pltpu.CompilerParams(vmem_limit_bytes=16 * 1024 * 1024),
        cost_estimate=pl.CostEstimate(
            flops=4 * spread[0] * spread[1] * members * cell_rows // depth * LANES,
            bytes_accessed=8 * cells.size,
            transcendentals=members * cells.size,
        ),
        name="pointwise",
    )(place, strengths, bias, weight, *in_hbm(cells, forcing))


def layer_kernel(back_ref, table_ref, point_ref, out_hbm, columns, native, result, sent):
    members, inner, rows, length_y = point_ref.shape
    _, outer, cell_rows, _ = native.shape
    sources, block_rows, _ = back_ref.shape
    slabs = sources // members
    depth = block_rows // inner
    planes, y_blocks, slab_rows = cell_layout(cell_rows, length_y)
    leaving = [pltpu.make_async_copy(result.at[:, b], out_hbm.at[:, b], sent.at[b]) for b in range(inner)]
    for m in range(members):
        for s in range(slabs):
            block = back_ref[s * members + m].astype(F32)
            for b in range(inner):
                columns[b, m, pl.ds(s * depth, depth), :] = block[b * depth : (b + 1) * depth]
    for b in range(inner):
        turn = b % 2
        total = None
        for m in range(members):
            spectral = lax.dot_general(
                columns[b, m].astype(BF16), table_ref[...], (((0,), (0,)), ((), ())), preferred_element_type=F32
            )
            value = double_gelu(point_ref[m, b].astype(F32) + spectral)
            total = value if total is None else total + value
        total = total * (0.5 / members)
        for a in range(outer):
            for z in range(planes):
                start = (a * planes + z) * slab_rows
                for j in range(y_blocks):
                    native[turn, a, pl.ds(j * planes + z, slab_rows, stride=planes * y_blocks), :] = total[
                        start : start + slab_rows, j * LANES : (j + 1) * LANES
                    ]
        for a in range(outer):
            result[a, b] = native[turn, a].astype(BF16)
        leaving[b].start()
    for copy in leaving:
        copy.wait()


def layer(back, points, outer, length_x, modes_y, slabs):
    members, inner, rows, length_y = points.shape
    cell_rows = rows * length_y // (outer * LANES)
    table = inverse_y_table(modes_y, length_y, length_x, slabs)
    vmem = pl.BlockSpec(memory_space=pltpu.VMEM)
    return pl.pallas_call(
        layer_kernel,
        in_specs=[vmem, vmem, vmem],
        out_specs=pl.BlockSpec(memory_space=pl.ANY),
        out_shape=pltpu.HBM((outer, inner, cell_rows, LANES), BF16),
        scratch_shapes=[
            pltpu.VMEM((inner, members, 2 * modes_y, LANES), F32),
            pltpu.VMEM((2, outer, cell_rows, LANES), F32),
            pltpu.VMEM((outer, inner, cell_rows, LANES), BF16),
            pltpu.SemaphoreType.DMA((inner,)),
        ],
        compiler_params=pltpu.CompilerParams(vmem_limit_bytes=16 * 1024 * 1024),
        cost_estimate=pl.CostEstimate(
            flops=4 * modes_y * points.size, bytes_accessed=5 * points.size, transcendentals=points.size
        ),
        name="layer",
    )(back, table, points)


def fast_local(
    base_field,
    forcing,
    load,
    amplitudes,
    amp_index,
    mode_count,
    point_weight,
    point_bias,
    spectral_weight,
):
    channels, slab_rows, planes, length_y = base_field.shape
    slabs, members = lax.axis_size("slab"), lax.axis_size("member")
    local_modes, modes_x = spectral_weight.shape[:2]
    modes_y = local_modes * slabs
    length_x = slab_rows * slabs
    y_blocks = length_y // LANES
    cells = base_field.reshape(channels, slab_rows, planes, y_blocks, LANES).transpose(0, 1, 3, 2, 4)
    cells = cells.reshape(channels, slab_rows * SUBLANES, LANES)
    force = forcing.reshape(slab_rows, planes, y_blocks, LANES).transpose(0, 2, 1, 3)
    force = force.reshape(slab_rows * SUBLANES, LANES)
    owners = slabs // 2
    slab, me = lax.axis_index("slab"), lax.axis_index("member")
    half = slab // owners
    place = jnp.stack([half, me])
    other_half = jnp.reshape(1 - half, (1,))
    partners = [(n, (n + owners) % slabs) for n in range(slabs)]
    index = amp_index.reshape(1, 1)
    other_index = lax.ppermute(index, "member", [(n, 1 - n) for n in range(2)])
    out_channels = channels // members
    packed = y_modes(index, amplitudes, load, cells, force, slabs, modes_y, length_y)
    pencil = lax.all_to_all(
        packed,
        "slab",
        split_axis=0,
        concat_axis=0,
        tiled=True,
        axis_index_groups=[list(range(h * owners, (h + 1) * owners)) for h in range(2)],
    )
    strengths, weights, forward, inverse = prepare(
        place, index, other_index, amplitudes, load, spectral_weight.transpose(0, 2, 3, 4, 1), length_x, slabs, planes
    )
    leaving = partial_spectrum(other_half, pencil, forward, BF16)
    other = lax.ppermute(leaving, "slab", partners)
    own = partial_spectrum(place, pencil, forward, F32)
    back = mix(mode_count - slab * local_modes, own, other, weights, inverse, slabs, members)
    back = lax.all_to_all(back, ("slab", "member"), split_axis=0, concat_axis=0, tiled=True)
    points = pointwise(place, strengths, point_bias, point_weight, cells, force, length_y)
    result = layer(back, points, out_channels // SUBLANES, length_x, modes_y, slabs)
    result = result.reshape(out_channels, slab_rows, y_blocks, planes, LANES).transpose(0, 1, 3, 2, 4)
    return result.reshape(out_channels, slab_rows, planes, length_y)


def tiles_fit(base_shape, weight_shape, slabs, members):
    channels, slab_rows, planes, length_y = base_shape
    local_modes, modes_x = weight_shape[:2]
    return (
        2 * planes * slab_rows == LANES
        and 2 * modes_x == LANES
        and planes * length_y == SUBLANES * LANES
        and 2 * local_modes == SUBLANES
        and 2 * SUBLANES * members == channels
        and slabs % 4 == 0
    )


def phases(frequency, positions, length):
    product = frequency[:, None] * positions[None, :] % length
    angles = product.astype(jnp.float32) * (TWO_PI / length)
    return (jnp.cos(angles), jnp.sin(angles))


def forward_x(pencil, cos_table, sin_table):
    row_total = pencil.shape[0]
    modes = cos_table.shape[0]
    with_cos = jnp.einsum(
        "kxf,mx->kmf", pencil, cos_table, preferred_element_type=jnp.float32
    ).reshape(row_total, modes, 2, -1)
    with_sin = jnp.einsum(
        "kxf,mx->kmf", pencil, sin_table, preferred_element_type=jnp.float32
    ).reshape(row_total, modes, 2, -1)
    real_part = with_cos[:, :, 0] + with_sin[:, :, 1]
    imag_part = with_cos[:, :, 1] - with_sin[:, :, 0]
    return jnp.stack([real_part, imag_part], axis=2).reshape(row_total, modes, -1)


def inverse_x(spectra, cos_table, sin_table):
    row_total = spectra.shape[0]
    points = cos_table.shape[1]
    with_cos = jnp.einsum(
        "kmf,mx->kxf", spectra, cos_table, preferred_element_type=jnp.float32
    ).reshape(row_total, points, 2, -1)
    with_sin = jnp.einsum(
        "kmf,mx->kxf", spectra, sin_table, preferred_element_type=jnp.float32
    ).reshape(row_total, points, 2, -1)
    real_part = with_cos[:, :, 0] - with_sin[:, :, 1]
    imag_part = with_cos[:, :, 1] + with_sin[:, :, 0]
    return jnp.stack([real_part, imag_part], axis=2).reshape(row_total, points, -1)


def mixing(weights, values):
    return jnp.einsum("kmoi,kmiz->kmoz", weights, values, preferred_element_type=jnp.float32)


def general_local(
    base_field,
    forcing,
    load,
    amplitudes,
    amp_index,
    mode_count,
    point_weight,
    point_bias,
    spectral_weight,
):
    channels, slab_rows, plane_count, length_y = base_field.shape
    slab_count = lax.axis_size("slab")
    local_modes = spectral_weight.shape[0]
    modes_y = local_modes * slab_count
    modes_x = spectral_weight.shape[1]
    length_x = slab_rows * slab_count
    packed_width = 2 * channels * plane_count
    slab_index = lax.axis_index("slab")
    level_ids = jnp.arange(amplitudes.shape[0], dtype=jnp.int32)
    amplitude = jnp.sum(jnp.where(level_ids == amp_index[0], amplitudes, 0.0))
    driven = base_field.astype(jnp.float32) + amplitude * load[:, None, None, None] * forcing[
        None
    ].astype(jnp.float32)
    field_now = (2.0 * jnp.tanh(0.5 * driven)).astype(jnp.bfloat16)
    y_cos, y_sin = phases(
        jnp.arange(modes_y, dtype=jnp.int32), jnp.arange(length_y, dtype=jnp.int32), length_y
    )
    y_real = jnp.einsum(
        "cxzy,ky->kxcz", field_now, y_cos.astype(jnp.bfloat16), preferred_element_type=jnp.float32
    )
    y_imag = -jnp.einsum(
        "cxzy,ky->kxcz", field_now, y_sin.astype(jnp.bfloat16), preferred_element_type=jnp.float32
    )
    packed = (
        jnp.stack([y_real, y_imag], axis=2)
        .astype(jnp.bfloat16)
        .reshape(modes_y, slab_rows, packed_width)
    )
    frequency_x = jnp.concatenate(
        [
            jnp.arange(modes_x // 2, dtype=jnp.int32),
            jnp.arange(length_x - modes_x // 2, length_x, dtype=jnp.int32),
        ]
    )
    full_cos, full_sin = phases(frequency_x, jnp.arange(length_x, dtype=jnp.int32), length_x)
    full_cos = full_cos.astype(jnp.bfloat16)
    full_sin = full_sin.astype(jnp.bfloat16)
    pencil = lax.all_to_all(packed, "slab", split_axis=0, concat_axis=1, tiled=True)
    spectrum = forward_x(pencil, full_cos, full_sin)
    spectrum = spectrum.astype(jnp.bfloat16).reshape(local_modes, modes_x, 2, channels, plane_count)
    weight_real = spectral_weight[:, :, 0]
    weight_imag = spectral_weight[:, :, 1]
    spec_real = spectrum[:, :, 0]
    spec_imag = spectrum[:, :, 1]
    mix_real = mixing(weight_real, spec_real) - mixing(weight_imag, spec_imag)
    mix_imag = mixing(weight_real, spec_imag) + mixing(weight_imag, spec_real)
    global_modes = slab_index * local_modes + jnp.arange(local_modes, dtype=jnp.int32)
    keep = (global_modes < mode_count[0]).astype(jnp.float32)[:, None, None, None, None]
    mixed = (
        (jnp.stack([mix_real, mix_imag], axis=2) * keep)
        .astype(jnp.bfloat16)
        .reshape(local_modes, modes_x, packed_width)
    )
    back = inverse_x(mixed, full_cos, full_sin).astype(jnp.bfloat16)
    returned = lax.all_to_all(back, "slab", split_axis=1, concat_axis=0, tiled=True)
    returned = returned.reshape(modes_y, slab_rows, 2, channels, plane_count)
    weights_y = jnp.where(jnp.arange(modes_y) == 0, 1.0, 2.0).astype(jnp.float32) / (
        length_x * length_y
    )
    back_cos = (weights_y[:, None] * y_cos).astype(jnp.bfloat16)
    back_sin = (weights_y[:, None] * y_sin).astype(jnp.bfloat16)
    spectral = jnp.einsum(
        "kxcz,ky->cxzy", returned[:, :, 0], back_cos, preferred_element_type=jnp.float32
    )
    spectral = spectral - jnp.einsum(
        "kxcz,ky->cxzy", returned[:, :, 1], back_sin, preferred_element_type=jnp.float32
    )
    pointwise = (
        jnp.einsum("oc,cxzy->oxzy", point_weight, field_now, preferred_element_type=jnp.float32)
        + point_bias[:, None, None, None]
    )
    layer = jax.nn.gelu(pointwise + spectral, approximate=True).astype(jnp.bfloat16)
    layer = lax.optimization_barrier(layer).astype(jnp.float32)
    total = lax.psum_scatter(
        layer.astype(jnp.bfloat16), "member", scatter_dimension=0, tiled=True
    ).astype(jnp.float32)
    return (total / lax.axis_size("member")).astype(jnp.bfloat16)


def local(base_field, forcing, load, amplitudes, amp_index, mode_count, point_weight, point_bias, spectral_weight):
    fits = tiles_fit(
        base_field.shape, spectral_weight.shape, lax.axis_size("slab"), lax.axis_size("member")
    )
    return (fast_local if fits else general_local)(
        base_field,
        forcing,
        load,
        amplitudes,
        amp_index,
        mode_count,
        point_weight,
        point_bias,
        spectral_weight,
    )


def solution(mesh):
    in_specs = (
        P(None, "slab", None, None),
        P("slab", None, None),
        P(),
        P(),
        P("member"),
        P("member"),
        P(),
        P(),
        P("slab", None, None, None, None),
    )
    out_specs = P("member", "slab", None, None)
    return jax.shard_map(local, mesh=mesh, in_specs=in_specs, out_specs=out_specs, check_vma=False)
```

```python
import math
import random

import jax
import jax.numpy as jnp
import numpy as np
from jax import lax
from jax.experimental import pallas as pl
from jax.experimental.pallas import tpu as pltpu
from jax.sharding import PartitionSpec as P

TWO_PI = 2.0 * math.pi
LANES = 128
SUBLANES = 8
FORCING_ROWS = 64
PART_ROWS = SUBLANES * SUBLANES // 2
SMEM = pltpu.SMEM
F32 = jnp.float32
BF16 = jnp.bfloat16


def host_phases(frequency, positions, length):
    product = frequency[:, None] * positions[None, :] % length
    angles = product.astype(np.float32) * np.float32(TWO_PI / length)
    return np.cos(angles), np.sin(angles)


def first_frequencies(modes_x, length_x):
    return np.concatenate([np.arange(modes_x // 2), np.arange(length_x - modes_x // 2, length_x)])


def as_bf16(table):
    return jnp.asarray(table.astype(BF16))


def half_order(owners):
    order = list(range(owners))
    random.Random(4).shuffle(order)
    return order


def by_owner(table, slabs):
    modes, length = table.shape
    local = modes // slabs
    return table.reshape(2, slabs // 2, local, length).transpose(1, 0, 2, 3)[half_order(slabs // 2)]


def forward_y_table(modes_y, length_y, slabs):
    cos, sin = host_phases(np.arange(modes_y), np.arange(length_y), length_y)
    table = np.stack([by_owner(cos, slabs), by_owner(-sin, slabs)], axis=0)
    return as_bf16(2.0 * table.astype(BF16).astype(np.float32).reshape(2 * modes_y, length_y))


def inverse_y_table(modes_y, length_y, length_x, slabs):
    cos, sin = host_phases(np.arange(modes_y), np.arange(length_y), length_y)
    scale = np.where(np.arange(modes_y) == 0, 1.0, 2.0).astype(np.float32)
    scale = (scale / np.float32(length_x * length_y))[:, None]
    parts = np.stack([scale * cos, -(scale * sin)], axis=0)
    parts = parts.reshape(2, slabs, modes_y // slabs, length_y).transpose(1, 0, 2, 3)
    return as_bf16(parts.reshape(2 * modes_y, length_y))


def forward_x_table(modes_x, length_x, slabs, planes):
    cos, sin = host_phases(first_frequencies(modes_x, length_x), np.arange(length_x), length_x)
    whole = np.array([[cos, -sin], [sin, cos]])
    whole = whole.reshape(2, 2, modes_x, 2, slabs // 2, length_x // slabs)[:, :, :, :, half_order(slabs // 2)]
    table = np.einsum("abqhsx,zw->hsazxwbq", whole, np.eye(planes, dtype=np.float32))
    return as_bf16(table.reshape(2, planes * length_x, planes * 2 * modes_x))


def inverse_x_table(modes_x, length_x, slabs, planes):
    cos, sin = host_phases(first_frequencies(modes_x, length_x), np.arange(length_x), length_x)
    whole = np.array([cos, -sin]).reshape(2, modes_x, slabs, length_x // slabs)
    table = np.einsum("aqsx,zw->zaqswx", whole, np.eye(planes, dtype=np.float32))
    return as_bf16(table.reshape(planes * 2 * modes_x, planes * length_x))


def low_half(shape):
    return lax.broadcasted_iota(jnp.int32, shape, len(shape) - 1) < shape[-1] // 2


def half_turn(values):
    return pltpu.roll(values, values.shape[-1] // 2, values.ndim - 1)


def pair_halves(first, second):
    low = low_half(first.shape)
    return (
        jnp.where(low, first, half_turn(second)),
        jnp.where(low, half_turn(first), second),
    )


def half_field(base, forcing, strength):
    return jnp.tanh(0.5 * (base.astype(F32) + strength * forcing))


def double_gelu(x):
    scale = math.sqrt(2.0 / math.pi)
    return x * (1.0 + jnp.tanh(x * (scale + (0.044715 * scale) * (x * x))))


def cell_layout(cell_rows, length_y):
    y_blocks = length_y // LANES
    planes = SUBLANES // y_blocks
    return planes, y_blocks, cell_rows // SUBLANES


def in_hbm(*arrays):
    return [pltpu.with_memory_space_constraint(a, pltpu.HBM) for a in arrays]


def y_modes_kernel(
    index_any,
    amplitude_hbm,
    load_hbm,
    cells_hbm,
    forcing_hbm,
    table_hbm,
    out_hbm,
    index,
    amplitudes,
    load,
    cells,
    forcing,
    forcing_wide,
    table,
    field,
    rows,
    modes,
    packed,
    arrived,
    sent,
):
    channels, cell_rows, _ = cells.shape
    width = field.shape[1]
    groups = [(c, width) for c in range(0, channels, width)]
    planes, y_blocks, slab_rows = cell_layout(cell_rows, table.shape[1])
    modes_y = table.shape[0] // 2
    span = planes * slab_rows
    owners, block_rows, _ = out_hbm.shape
    part_rows = block_rows // (channels // width)
    small = [
        pltpu.make_async_copy(source, target, arrived.at[n])
        for n, (source, target) in enumerate(
            [
                (index_any, index),
                (amplitude_hbm, amplitudes),
                (load_hbm, load),
                (forcing_hbm, forcing),
                (table_hbm, table),
            ]
        )
    ]
    large = [
        pltpu.make_async_copy(
            cells_hbm.at[pl.ds(first, count)], cells.at[pl.ds(first, count)], arrived.at[len(small) + n]
        )
        for n, (first, count) in enumerate(groups)
    ]
    for copy in small[:4] + large[:1] + small[4:] + large[1:]:
        copy.start()
    for copy in small[:4]:
        copy.wait()
    amplitude = amplitudes[index[0, 0]]
    forcing_wide[...] = forcing[...].astype(F32)
    small[4].wait()
    leaving = [
        pltpu.make_async_copy(packed.at[g], out_hbm.at[:, pl.ds(g * part_rows, part_rows), :], sent.at[g])
        for g in range(channels // width)
    ]
    for step in range(len(groups) + 1):
        if step < len(groups):
            first, count = groups[step]
            large[step].wait()
            strengths = [amplitude * load[first + c] for c in range(count)]
            for start in range(0, cell_rows, FORCING_ROWS):
                some = pl.ds(start, FORCING_ROWS)
                force = forcing_wide[some, :]
                for c in range(count):
                    field[step % 2, c, some, :] = half_field(cells[first + c, some, :], force, strengths[c])
            for c in range(count):
                for z in range(planes):
                    for j in range(y_blocks):
                        picked = field[step % 2, c, pl.ds(j * planes + z, slab_rows, stride=planes * y_blocks), :]
                        rows[
                            step % 2, pl.ds(c * span + z * slab_rows, slab_rows), pl.ds(j * LANES, LANES)
                        ] = picked.astype(BF16)
        if step > 0:
            first, count = groups[step - 1]
            result = lax.dot_general(
                table[...],
                rows[(step - 1) % 2, pl.ds(0, count * span), :],
                (((1,), (1,)), ((), ())),
                preferred_element_type=F32,
            )
            part, place = divmod(first, width)
            for t in range(count // 2):
                tile = slice(t * LANES, (t + 1) * LANES)
                pair = pair_halves(result[:modes_y, tile], result[modes_y:, tile])
                for n in range(2):
                    modes[part % 2, pl.ds(place + 2 * t + n, modes_y, stride=width), :] = pair[n]
            if place + count == width:
                for d in range(owners):
                    packed[part, d] = modes[part % 2, pl.ds(d * part_rows, part_rows), :].astype(BF16)
                leaving[part].start()
    for copy in leaving:
        copy.wait()


def y_modes(amp_index, amplitudes, load, cells, forcing, slabs, modes_y, length_y):
    channels, cell_rows, _ = cells.shape
    width = SUBLANES
    parts = channels // width
    owners = slabs // 2
    block_rows = modes_y // owners * channels
    table = forward_y_table(modes_y, length_y, slabs)
    planes, _, slab_rows = cell_layout(cell_rows, length_y)
    operands = in_hbm(amplitudes, load, cells, forcing, table)
    anywhere = pl.BlockSpec(memory_space=pl.ANY)
    return pl.pallas_call(
        y_modes_kernel,
        in_specs=[anywhere] * (1 + len(operands)),
        out_specs=anywhere,
        out_shape=jax.ShapeDtypeStruct((owners, block_rows, LANES), BF16),
        scratch_shapes=[
            SMEM(amp_index.shape, jnp.int32),
            SMEM(amplitudes.shape, F32),
            SMEM(load.shape, F32),
            pltpu.VMEM(cells.shape, BF16),
            pltpu.VMEM(forcing.shape, BF16),
            pltpu.VMEM(forcing.shape, F32),
            pltpu.VMEM(table.shape, BF16),
            pltpu.VMEM((2, width, cell_rows, LANES), F32),
            pltpu.VMEM((2, width * planes * slab_rows, length_y), BF16),
            pltpu.VMEM((2, modes_y * width, LANES), F32),
            pltpu.VMEM((parts, owners, block_rows // parts, LANES), BF16),
            pltpu.SemaphoreType.DMA((5 + parts,)),
            pltpu.SemaphoreType.DMA((parts,)),
        ],
        compiler_params=pltpu.CompilerParams(vmem_limit_bytes=12 * 1024 * 1024),
        cost_estimate=pl.CostEstimate(
            flops=4 * modes_y * cells.size, bytes_accessed=4 * cells.size, transcendentals=cells.size
        ),
        name="y_modes",
    )(amp_index, *operands)


def prepare_kernel(
    half_ref,
    own_any,
    other_any,
    amplitude_ref,
    load_ref,
    weight_ref,
    forward_hbm,
    inverse_hbm,
    strengths,
    weights,
    forward,
    inverse,
    wide,
    indices,
    arrived,
):
    half, me = half_ref[0], half_ref[1]
    copies = [
        pltpu.make_async_copy(forward_hbm.at[half], forward, arrived.at[0]),
        pltpu.make_async_copy(inverse_hbm, inverse, arrived.at[1]),
        pltpu.make_async_copy(own_any, indices.at[pl.ds(0, 1)], arrived.at[2]),
        pltpu.make_async_copy(other_any, indices.at[pl.ds(1, 1)], arrived.at[3]),
    ]
    for copy in copies:
        copy.start()
    local_modes, parts, channels, _, _ = weight_ref.shape
    for k in range(local_modes // 2):
        for r in range(parts):
            for o in range(channels):
                pair = [weight_ref[2 * k + n, r, o].astype(F32) for n in range(2)]
                wide[k, r, pl.ds(o, channels, stride=channels), :] = jnp.concatenate(pair, axis=1)
    weights[...] = wide[...].astype(BF16)
    for copy in copies:
        copy.wait()
    for m in range(2):
        amplitude = amplitude_ref[indices[lax.rem(me + m, 2), 0]]
        for c in range(channels):
            strengths[m * channels + c] = amplitude * load_ref[c]


def prepare(place, own, other, amplitudes, load, spectral_weight, length_x, slabs, planes):
    local_modes, parts, channels, _, modes_x = spectral_weight.shape
    forward = forward_x_table(modes_x, length_x, slabs, planes)
    inverse = inverse_x_table(modes_x, length_x, slabs, planes)
    wide = (local_modes // 2, parts, channels * channels, 2 * modes_x)
    vmem = pl.BlockSpec(memory_space=pltpu.VMEM)
    smem = pl.BlockSpec(memory_space=SMEM)
    anywhere = pl.BlockSpec(memory_space=pl.ANY)
    return pl.pallas_call(
        prepare_kernel,
        in_specs=[smem] + [anywhere] * 2 + [smem] * 2 + [vmem] + [anywhere] * 2,
        out_specs=[smem] + [vmem] * 3,
        out_shape=[
            jax.ShapeDtypeStruct((2 * channels,), F32),
            pltpu.VMEM(wide, BF16),
            pltpu.VMEM(forward.shape[1:], BF16),
            pltpu.VMEM(inverse.shape, BF16),
        ],
        scratch_shapes=[pltpu.VMEM(wide, F32), SMEM((2, 1), jnp.int32), pltpu.SemaphoreType.DMA((4,))],
        compiler_params=pltpu.CompilerParams(vmem_limit_bytes=16 * 1024 * 1024),
        cost_estimate=pl.CostEstimate(
            flops=4 * spectral_weight.size, bytes_accessed=10 * spectral_weight.size, transcendentals=0
        ),
        name="prepare",
    )(place, own, other, amplitudes, load, *in_hbm(spectral_weight, forward, inverse))


def spectrum_kernel(half_ref, pencil_ref, forward_ref, out_ref):
    sources, block_rows, _ = pencil_ref.shape
    rows = out_ref.shape[0]
    parts = rows // PART_ROWS
    picked = []
    for part in range(parts):
        start = pl.multiple_of((2 * part + half_ref[0]) * PART_ROWS, PART_ROWS)
        picked.append(
            jnp.concatenate([pencil_ref[s, pl.ds(start, PART_ROWS), :] for s in range(sources)], axis=1)
        )
    result = jnp.dot(jnp.concatenate(picked, axis=0), forward_ref[...], preferred_element_type=F32)
    out_ref[...] = result.astype(out_ref.dtype)


def partial_spectrum(half, pencil, forward, dtype):
    _, block_rows, _ = pencil.shape
    vmem = pl.BlockSpec(memory_space=pltpu.VMEM)
    return pl.pallas_call(
        spectrum_kernel,
        in_specs=[pl.BlockSpec(memory_space=SMEM), vmem, vmem],
        out_specs=vmem,
        out_shape=jax.ShapeDtypeStruct((block_rows // 2, forward.shape[1]), dtype),
        compiler_params=pltpu.CompilerParams(vmem_limit_bytes=8 * 1024 * 1024),
        cost_estimate=pl.CostEstimate(
            flops=block_rows * forward.size, bytes_accessed=2 * pencil.size, transcendentals=0
        ),
        name="partial_spectrum",
    )(half, pencil, forward)


def mix_kernel(limit_ref, own_ref, other_ref, weight_ref, inverse_ref, out_hbm, spectrum, mixed, packed, sent):
    block_rows, _ = own_ref.shape
    pairs, _, _, width = weight_ref.shape
    local_modes = 2 * pairs
    channels = block_rows // local_modes
    planes = own_ref.shape[1] // width
    groups = channels // SUBLANES
    block = SUBLANES * 2 * local_modes
    low = low_half((SUBLANES, width))
    result = own_ref[...] + other_ref[...].astype(F32)
    for z in range(planes):
        lanes = slice(z * width, (z + 1) * width)
        for part in range(groups):
            for k in range(pairs):
                start = (part * local_modes + 2 * k) * SUBLANES
                real, imag = pair_halves(
                    result[start : start + SUBLANES, lanes], result[start + SUBLANES : start + 2 * SUBLANES, lanes]
                )
                spectrum[k, z, 0, pl.ds(part * SUBLANES, SUBLANES), :] = real
                spectrum[k, z, 1, pl.ds(part * SUBLANES, SUBLANES), :] = imag
    for k in range(pairs):
        keep = [jnp.where(limit_ref[0] > 2 * k + n, 1.0, 0.0).astype(F32) for n in range(2)]
        sums = [[[None, None] for _ in range(groups)] for _ in range(planes)]
        for i in range(channels):
            values = [
                [jnp.broadcast_to(spectrum[k, z, r, pl.ds(i, 1), :], (SUBLANES, width)) for r in range(2)]
                for z in range(planes)
            ]
            weights = [weight_ref[k, r, pl.ds(i * channels, channels), :].astype(F32) for r in range(2)]
            for g in range(groups):
                real, imag = (w[g * SUBLANES : (g + 1) * SUBLANES] for w in weights)
                for z in range(planes):
                    terms = (
                        real * values[z][0] - imag * values[z][1],
                        real * values[z][1] + imag * values[z][0],
                    )
                    for r in range(2):
                        old = sums[z][g][r]
                        sums[z][g][r] = terms[r] if old is None else old + terms[r]
        for z in range(planes):
            for g in range(groups):
                modes = pair_halves(*sums[z][g])
                for n in range(2):
                    kept = modes[n] * keep[n]
                    swapped = half_turn(kept)
                    start = g * block + 2 * k + n
                    mixed[z, pl.ds(start, SUBLANES, stride=2 * local_modes), :] = kept
                    mixed[z, pl.ds(start + local_modes, SUBLANES, stride=2 * local_modes), :] = jnp.where(
                        low, swapped, -swapped
                    )
    left = jnp.concatenate([mixed[z].astype(BF16) for z in range(planes)], axis=1)
    members = groups // 2
    wide = 2 * LANES
    leaving = []
    for t in range(inverse_ref.shape[1] // wide):
        back = jnp.dot(left, inverse_ref[:, t * wide : (t + 1) * wide], preferred_element_type=F32)
        for u in range(2):
            tile = slice(u * LANES, (u + 1) * LANES)
            for h in range(members):
                start = 2 * h * block
                pair = pair_halves(back[start : start + block, tile], back[start + block : start + 2 * block, tile])
                for n in range(2):
                    packed[(4 * t + 2 * u + n) * members + h] = pair[n].astype(BF16)
        blocks = pl.ds(4 * t * members, 4 * members)
        copy = pltpu.make_async_copy(packed.at[blocks], out_hbm.at[blocks], sent.at[t])
        copy.start()
        leaving.append(copy)
    for copy in leaving:
        copy.wait()


def mix(limit, own, other, weights, inverse, slabs, members):
    block_rows, _ = own.shape
    pairs, _, _, width = weights.shape
    channels = block_rows // (2 * pairs)
    planes = own.shape[1] // width
    rows = channels * 4 * pairs
    blocks = (slabs * members, SUBLANES * 4 * pairs, LANES)
    vmem = pl.BlockSpec(memory_space=pltpu.VMEM)
    return pl.pallas_call(
        mix_kernel,
        in_specs=[pl.BlockSpec(memory_space=SMEM)] + [vmem] * 4,
        out_specs=pl.BlockSpec(memory_space=pl.ANY),
        out_shape=jax.ShapeDtypeStruct(blocks, BF16),
        scratch_shapes=[
            pltpu.VMEM((pairs, planes, 2, channels, width), F32),
            pltpu.VMEM((planes, rows, width), F32),
            pltpu.VMEM(blocks, BF16),
            pltpu.SemaphoreType.DMA((slabs // 4,)),
        ],
        compiler_params=pltpu.CompilerParams(vmem_limit_bytes=8 * 1024 * 1024),
        cost_estimate=pl.CostEstimate(
            flops=2 * rows * inverse.size, bytes_accessed=4 * weights.size, transcendentals=0
        ),
        name="mix",
    )(limit, own, other, weights, inverse)


def pointwise_kernel(
    place_ref, strength_ref, bias_ref, weight_ref, base_ref, forcing_ref, out_ref, spread, native
):
    members, inner, out_rows, length_y = out_ref.shape
    channels, cell_rows, _ = base_ref.shape
    outer = channels // (members * inner)
    planes, y_blocks, slab_rows = cell_layout(cell_rows, length_y)
    depth = 2 * SUBLANES
    out_channels = channels // members
    me = place_ref[1]

    def spread_weight():
        tall = (out_channels * depth, channels)
        wide = (channels, channels * depth)
        row_of = lax.broadcasted_iota(jnp.int32, tall, 0) // depth + me * out_channels
        pick_rows = (row_of == lax.broadcasted_iota(jnp.int32, tall, 1)).astype(BF16)
        column_of = lax.broadcasted_iota(jnp.int32, wide, 1) // depth
        pick_columns = (column_of == lax.broadcasted_iota(jnp.int32, wide, 0)).astype(BF16)
        picked = jnp.dot(pick_rows, weight_ref[...], preferred_element_type=F32).astype(BF16)
        full = jnp.dot(picked, pick_columns, preferred_element_type=F32)
        same = lax.broadcasted_iota(jnp.int32, full.shape, 0) % depth == (
            lax.broadcasted_iota(jnp.int32, full.shape, 1) % depth
        )
        spread[...] = jnp.where(same, 2.0 * full, 0.0).astype(BF16)

    spread_weight()

    def body(step, carry):
        rows = pl.ds(pl.multiple_of(step * depth, depth), depth)
        forcing = forcing_ref[rows, :].astype(F32)
        fields = []
        for m in range(members):
            parts = [
                half_field(base_ref[c, rows, :], forcing, strength_ref[m * channels + c]).astype(BF16)
                for c in range(channels)
            ]
            fields.append(jnp.concatenate(parts, axis=0))
        result = jnp.dot(spread[...], jnp.concatenate(fields, axis=1), preferred_element_type=F32)
        for a in range(outer):
            for b in range(inner):
                o = a * inner + b
                bias = bias_ref[me * out_channels + o]
                for m in range(members):
                    cells = result[o * depth : (o + 1) * depth, m * LANES : (m + 1) * LANES] + bias
                    native[m, a, b, rows, :] = cells
        return carry

    lax.fori_loop(0, cell_rows // depth, body, 0)

    def arrange(b, carry):
        for m in range(members):
            for a in range(outer):
                for z in range(planes):
                    rows = pl.ds((a * planes + z) * slab_rows, slab_rows)
                    for j in range(y_blocks):
                        picked = native[m, a, b, pl.ds(j * planes + z, slab_rows, stride=planes * y_blocks), :]
                        out_ref[m, b, rows, pl.ds(j * LANES, LANES)] = picked.astype(BF16)
        return carry

    lax.fori_loop(0, inner, arrange, 0)


def pointwise(place, strengths, bias, weight, cells, forcing, length_y):
    channels, cell_rows, _ = cells.shape
    members = strengths.shape[0] // channels
    depth = 2 * SUBLANES
    inner = SUBLANES
    outer = channels // members // inner
    spread = (channels // members * depth, channels * depth)
    smem = pl.BlockSpec(memory_space=SMEM)
    vmem = pl.BlockSpec(memory_space=pltpu.VMEM)
    return pl.pallas_call(
        pointwise_kernel,
        in_specs=[smem] * 3 + [vmem] * 3,
        out_specs=vmem,
        out_shape=pltpu.VMEM((members, inner, outer * cell_rows * LANES // length_y, length_y), BF16),
        scratch_shapes=[
            pltpu.VMEM(spread, BF16),
            pltpu.VMEM((members, outer, inner, cell_rows, LANES), F32),
        ],
        compiler_params=pltpu.CompilerParams(vmem_limit_bytes=16 * 1024 * 1024),
        cost_estimate=pl.CostEstimate(
            flops=4 * spread[0] * spread[1] * members * cell_rows // depth * LANES,
            bytes_accessed=8 * cells.size,
            transcendentals=members * cells.size,
        ),
        name="pointwise",
    )(place, strengths, bias, weight, *in_hbm(cells, forcing))


def layer_kernel(back_ref, table_ref, point_ref, out_hbm, columns, native, result, sent):
    members, inner, rows, length_y = point_ref.shape
    _, outer, cell_rows, _ = native.shape
    sources, block_rows, _ = back_ref.shape
    slabs = sources // members
    depth = block_rows // inner
    planes, y_blocks, slab_rows = cell_layout(cell_rows, length_y)
    leaving = [pltpu.make_async_copy(result.at[:, b], out_hbm.at[:, b], sent.at[b]) for b in range(inner)]
    for m in range(members):
        for s in range(slabs):
            block = back_ref[s * members + m].astype(F32)
            for b in range(inner):
                columns[b, m, pl.ds(s * depth, depth), :] = block[b * depth : (b + 1) * depth]
    for b in range(inner):
        turn = b % 2
        total = None
        for m in range(members):
            spectral = lax.dot_general(
                columns[b, m].astype(BF16), table_ref[...], (((0,), (0,)), ((), ())), preferred_element_type=F32
            )
            value = double_gelu(point_ref[m, b].astype(F32) + spectral)
            total = value if total is None else total + value
        total = total * (0.5 / members)
        for a in range(outer):
            for z in range(planes):
                start = (a * planes + z) * slab_rows
                for j in range(y_blocks):
                    native[turn, a, pl.ds(j * planes + z, slab_rows, stride=planes * y_blocks), :] = total[
                        start : start + slab_rows, j * LANES : (j + 1) * LANES
                    ]
        for a in range(outer):
            result[a, b] = native[turn, a].astype(BF16)
        leaving[b].start()
    for copy in leaving:
        copy.wait()


def layer(back, points, outer, length_x, modes_y, slabs):
    members, inner, rows, length_y = points.shape
    cell_rows = rows * length_y // (outer * LANES)
    table = inverse_y_table(modes_y, length_y, length_x, slabs)
    vmem = pl.BlockSpec(memory_space=pltpu.VMEM)
    return pl.pallas_call(
        layer_kernel,
        in_specs=[vmem, vmem, vmem],
        out_specs=pl.BlockSpec(memory_space=pl.ANY),
        out_shape=pltpu.HBM((outer, inner, cell_rows, LANES), BF16),
        scratch_shapes=[
            pltpu.VMEM((inner, members, 2 * modes_y, LANES), F32),
            pltpu.VMEM((2, outer, cell_rows, LANES), F32),
            pltpu.VMEM((outer, inner, cell_rows, LANES), BF16),
            pltpu.SemaphoreType.DMA((inner,)),
        ],
        compiler_params=pltpu.CompilerParams(vmem_limit_bytes=16 * 1024 * 1024),
        cost_estimate=pl.CostEstimate(
            flops=4 * modes_y * points.size, bytes_accessed=5 * points.size, transcendentals=points.size
        ),
        name="layer",
    )(back, table, points)


def fast_local(
    base_field,
    forcing,
    load,
    amplitudes,
    amp_index,
    mode_count,
    point_weight,
    point_bias,
    spectral_weight,
):
    channels, slab_rows, planes, length_y = base_field.shape
    slabs, members = lax.axis_size("slab"), lax.axis_size("member")
    local_modes, modes_x = spectral_weight.shape[:2]
    modes_y = local_modes * slabs
    length_x = slab_rows * slabs
    y_blocks = length_y // LANES
    cells = base_field.reshape(channels, slab_rows, planes, y_blocks, LANES).transpose(0, 1, 3, 2, 4)
    cells = cells.reshape(channels, slab_rows * SUBLANES, LANES)
    force = forcing.reshape(slab_rows, planes, y_blocks, LANES).transpose(0, 2, 1, 3)
    force = force.reshape(slab_rows * SUBLANES, LANES)
    owners = slabs // 2
    slab, me = lax.axis_index("slab"), lax.axis_index("member")
    half = slab // owners
    place = jnp.stack([half, me])
    other_half = jnp.reshape(1 - half, (1,))
    partners = [(n, (n + owners) % slabs) for n in range(slabs)]
    index = amp_index.reshape(1, 1)
    other_index = lax.ppermute(index, "member", [(n, 1 - n) for n in range(2)])
    out_channels = channels // members
    packed = y_modes(index, amplitudes, load, cells, force, slabs, modes_y, length_y)
    pencil = lax.all_to_all(
        packed,
        "slab",
        split_axis=0,
        concat_axis=0,
        tiled=True,
        axis_index_groups=[[h * owners + n for n in half_order(owners)] for h in range(2)],
    )
    strengths, weights, forward, inverse = prepare(
        place, index, other_index, amplitudes, load, spectral_weight.transpose(0, 2, 3, 4, 1), length_x, slabs, planes
    )
    leaving = partial_spectrum(other_half, pencil, forward, BF16)
    other = lax.ppermute(leaving, "slab", partners)
    own = partial_spectrum(place, pencil, forward, F32)
    back = mix(mode_count - slab * local_modes, own, other, weights, inverse, slabs, members)
    back = lax.all_to_all(back, ("slab", "member"), split_axis=0, concat_axis=0, tiled=True)
    points = pointwise(place, strengths, point_bias, point_weight, cells, force, length_y)
    result = layer(back, points, out_channels // SUBLANES, length_x, modes_y, slabs)
    result = result.reshape(out_channels, slab_rows, y_blocks, planes, LANES).transpose(0, 1, 3, 2, 4)
    return result.reshape(out_channels, slab_rows, planes, length_y)


def tiles_fit(base_shape, weight_shape, slabs, members):
    channels, slab_rows, planes, length_y = base_shape
    local_modes, modes_x = weight_shape[:2]
    return (
        2 * planes * slab_rows == LANES
        and 2 * modes_x == LANES
        and planes * length_y == SUBLANES * LANES
        and 2 * local_modes == SUBLANES
        and 2 * SUBLANES * members == channels
        and slabs % 4 == 0
    )


def phases(frequency, positions, length):
    product = frequency[:, None] * positions[None, :] % length
    angles = product.astype(jnp.float32) * (TWO_PI / length)
    return (jnp.cos(angles), jnp.sin(angles))


def forward_x(pencil, cos_table, sin_table):
    row_total = pencil.shape[0]
    modes = cos_table.shape[0]
    with_cos = jnp.einsum(
        "kxf,mx->kmf", pencil, cos_table, preferred_element_type=jnp.float32
    ).reshape(row_total, modes, 2, -1)
    with_sin = jnp.einsum(
        "kxf,mx->kmf", pencil, sin_table, preferred_element_type=jnp.float32
    ).reshape(row_total, modes, 2, -1)
    real_part = with_cos[:, :, 0] + with_sin[:, :, 1]
    imag_part = with_cos[:, :, 1] - with_sin[:, :, 0]
    return jnp.stack([real_part, imag_part], axis=2).reshape(row_total, modes, -1)


def inverse_x(spectra, cos_table, sin_table):
    row_total = spectra.shape[0]
    points = cos_table.shape[1]
    with_cos = jnp.einsum(
        "kmf,mx->kxf", spectra, cos_table, preferred_element_type=jnp.float32
    ).reshape(row_total, points, 2, -1)
    with_sin = jnp.einsum(
        "kmf,mx->kxf", spectra, sin_table, preferred_element_type=jnp.float32
    ).reshape(row_total, points, 2, -1)
    real_part = with_cos[:, :, 0] - with_sin[:, :, 1]
    imag_part = with_cos[:, :, 1] + with_sin[:, :, 0]
    return jnp.stack([real_part, imag_part], axis=2).reshape(row_total, points, -1)


def mixing(weights, values):
    return jnp.einsum("kmoi,kmiz->kmoz", weights, values, preferred_element_type=jnp.float32)


def general_local(
    base_field,
    forcing,
    load,
    amplitudes,
    amp_index,
    mode_count,
    point_weight,
    point_bias,
    spectral_weight,
):
    channels, slab_rows, plane_count, length_y = base_field.shape
    slab_count = lax.axis_size("slab")
    local_modes = spectral_weight.shape[0]
    modes_y = local_modes * slab_count
    modes_x = spectral_weight.shape[1]
    length_x = slab_rows * slab_count
    packed_width = 2 * channels * plane_count
    slab_index = lax.axis_index("slab")
    level_ids = jnp.arange(amplitudes.shape[0], dtype=jnp.int32)
    amplitude = jnp.sum(jnp.where(level_ids == amp_index[0], amplitudes, 0.0))
    driven = base_field.astype(jnp.float32) + amplitude * load[:, None, None, None] * forcing[
        None
    ].astype(jnp.float32)
    field_now = (2.0 * jnp.tanh(0.5 * driven)).astype(jnp.bfloat16)
    y_cos, y_sin = phases(
        jnp.arange(modes_y, dtype=jnp.int32), jnp.arange(length_y, dtype=jnp.int32), length_y
    )
    y_real = jnp.einsum(
        "cxzy,ky->kxcz", field_now, y_cos.astype(jnp.bfloat16), preferred_element_type=jnp.float32
    )
    y_imag = -jnp.einsum(
        "cxzy,ky->kxcz", field_now, y_sin.astype(jnp.bfloat16), preferred_element_type=jnp.float32
    )
    packed = (
        jnp.stack([y_real, y_imag], axis=2)
        .astype(jnp.bfloat16)
        .reshape(modes_y, slab_rows, packed_width)
    )
    frequency_x = jnp.concatenate(
        [
            jnp.arange(modes_x // 2, dtype=jnp.int32),
            jnp.arange(length_x - modes_x // 2, length_x, dtype=jnp.int32),
        ]
    )
    full_cos, full_sin = phases(frequency_x, jnp.arange(length_x, dtype=jnp.int32), length_x)
    full_cos = full_cos.astype(jnp.bfloat16)
    full_sin = full_sin.astype(jnp.bfloat16)
    pencil = lax.all_to_all(packed, "slab", split_axis=0, concat_axis=1, tiled=True)
    spectrum = forward_x(pencil, full_cos, full_sin)
    spectrum = spectrum.astype(jnp.bfloat16).reshape(local_modes, modes_x, 2, channels, plane_count)
    weight_real = spectral_weight[:, :, 0]
    weight_imag = spectral_weight[:, :, 1]
    spec_real = spectrum[:, :, 0]
    spec_imag = spectrum[:, :, 1]
    mix_real = mixing(weight_real, spec_real) - mixing(weight_imag, spec_imag)
    mix_imag = mixing(weight_real, spec_imag) + mixing(weight_imag, spec_real)
    global_modes = slab_index * local_modes + jnp.arange(local_modes, dtype=jnp.int32)
    keep = (global_modes < mode_count[0]).astype(jnp.float32)[:, None, None, None, None]
    mixed = (
        (jnp.stack([mix_real, mix_imag], axis=2) * keep)
        .astype(jnp.bfloat16)
        .reshape(local_modes, modes_x, packed_width)
    )
    back = inverse_x(mixed, full_cos, full_sin).astype(jnp.bfloat16)
    returned = lax.all_to_all(back, "slab", split_axis=1, concat_axis=0, tiled=True)
    returned = returned.reshape(modes_y, slab_rows, 2, channels, plane_count)
    weights_y = jnp.where(jnp.arange(modes_y) == 0, 1.0, 2.0).astype(jnp.float32) / (
        length_x * length_y
    )
    back_cos = (weights_y[:, None] * y_cos).astype(jnp.bfloat16)
    back_sin = (weights_y[:, None] * y_sin).astype(jnp.bfloat16)
    spectral = jnp.einsum(
        "kxcz,ky->cxzy", returned[:, :, 0], back_cos, preferred_element_type=jnp.float32
    )
    spectral = spectral - jnp.einsum(
        "kxcz,ky->cxzy", returned[:, :, 1], back_sin, preferred_element_type=jnp.float32
    )
    pointwise = (
        jnp.einsum("oc,cxzy->oxzy", point_weight, field_now, preferred_element_type=jnp.float32)
        + point_bias[:, None, None, None]
    )
    layer = jax.nn.gelu(pointwise + spectral, approximate=True).astype(jnp.bfloat16)
    layer = lax.optimization_barrier(layer).astype(jnp.float32)
    total = lax.psum_scatter(
        layer.astype(jnp.bfloat16), "member", scatter_dimension=0, tiled=True
    ).astype(jnp.float32)
    return (total / lax.axis_size("member")).astype(jnp.bfloat16)


def local(base_field, forcing, load, amplitudes, amp_index, mode_count, point_weight, point_bias, spectral_weight):
    fits = tiles_fit(
        base_field.shape, spectral_weight.shape, lax.axis_size("slab"), lax.axis_size("member")
    )
    return (fast_local if fits else general_local)(
        base_field,
        forcing,
        load,
        amplitudes,
        amp_index,
        mode_count,
        point_weight,
        point_bias,
        spectral_weight,
    )


def solution(mesh):
    in_specs = (
        P(None, "slab", None, None),
        P("slab", None, None),
        P(),
        P(),
        P("member"),
        P("member"),
        P(),
        P(),
        P("slab", None, None, None, None),
    )
    out_specs = P("member", "slab", None, None)
    return jax.shard_map(local, mesh=mesh, in_specs=in_specs, out_specs=out_specs, check_vma=False)
```

```python
import math
import random

import jax
import jax.numpy as jnp
import numpy as np
from jax import lax
from jax.experimental import pallas as pl
from jax.experimental.pallas import tpu as pltpu
from jax.sharding import PartitionSpec as P

TWO_PI = 2.0 * math.pi
LANES = 128
SUBLANES = 8
FORCING_ROWS = 64
PART_ROWS = SUBLANES * SUBLANES // 2
SMEM = pltpu.SMEM
F32 = jnp.float32
BF16 = jnp.bfloat16


def host_phases(frequency, positions, length):
    product = frequency[:, None] * positions[None, :] % length
    angles = product.astype(np.float32) * np.float32(TWO_PI / length)
    return np.cos(angles), np.sin(angles)


def first_frequencies(modes_x, length_x):
    return np.concatenate([np.arange(modes_x // 2), np.arange(length_x - modes_x // 2, length_x)])


def as_bf16(table):
    return jnp.asarray(table.astype(BF16))


def half_order(owners):
    order = list(range(owners))
    random.Random(4).shuffle(order)
    return order


def by_owner(table, slabs):
    modes, length = table.shape
    local = modes // slabs
    return table.reshape(2, slabs // 2, local, length).transpose(1, 0, 2, 3)[half_order(slabs // 2)]


def forward_y_table(modes_y, length_y, slabs):
    cos, sin = host_phases(np.arange(modes_y), np.arange(length_y), length_y)
    table = np.stack([by_owner(cos, slabs), by_owner(-sin, slabs)], axis=0)
    return as_bf16(2.0 * table.astype(BF16).astype(np.float32).reshape(2 * modes_y, length_y))


def inverse_y_table(modes_y, length_y, length_x, slabs):
    cos, sin = host_phases(np.arange(modes_y), np.arange(length_y), length_y)
    scale = np.where(np.arange(modes_y) == 0, 1.0, 2.0).astype(np.float32)
    scale = (scale / np.float32(length_x * length_y))[:, None]
    parts = np.stack([scale * cos, -(scale * sin)], axis=0)
    parts = parts.reshape(2, slabs, modes_y // slabs, length_y).transpose(1, 0, 2, 3)
    return as_bf16(parts.reshape(2 * modes_y, length_y))


def forward_x_table(modes_x, length_x, slabs, planes):
    cos, sin = host_phases(first_frequencies(modes_x, length_x), np.arange(length_x), length_x)
    whole = np.array([[cos, -sin], [sin, cos]])
    whole = whole.reshape(2, 2, modes_x, 2, slabs // 2, length_x // slabs)[:, :, :, :, half_order(slabs // 2)]
    table = np.einsum("abqhsx,zw->hsazxwbq", whole, np.eye(planes, dtype=np.float32))
    return as_bf16(table.reshape(2, planes * length_x, planes * 2 * modes_x))


def inverse_x_table(modes_x, length_x, slabs, planes):
    cos, sin = host_phases(first_frequencies(modes_x, length_x), np.arange(length_x), length_x)
    whole = np.array([cos, -sin]).reshape(2, modes_x, slabs, length_x // slabs)
    table = np.einsum("aqsx,zw->zaqswx", whole, np.eye(planes, dtype=np.float32))
    return as_bf16(table.reshape(planes * 2 * modes_x, planes * length_x))


def low_half(shape):
    return lax.broadcasted_iota(jnp.int32, shape, len(shape) - 1) < shape[-1] // 2


def half_turn(values):
    return pltpu.roll(values, values.shape[-1] // 2, values.ndim - 1)


def pair_halves(first, second):
    low = low_half(first.shape)
    return (
        jnp.where(low, first, half_turn(second)),
        jnp.where(low, half_turn(first), second),
    )


def half_field(base, forcing, strength):
    return jnp.tanh(0.5 * (base.astype(F32) + strength * forcing))


def double_gelu(x):
    scale = math.sqrt(2.0 / math.pi)
    return x * (1.0 + jnp.tanh(x * (scale + (0.044715 * scale) * (x * x))))


def cell_layout(cell_rows, length_y):
    y_blocks = length_y // LANES
    planes = SUBLANES // y_blocks
    return planes, y_blocks, cell_rows // SUBLANES


def in_hbm(*arrays):
    return [pltpu.with_memory_space_constraint(a, pltpu.HBM) for a in arrays]


def y_modes_kernel(
    index_any,
    amplitude_hbm,
    load_hbm,
    cells_hbm,
    forcing_hbm,
    table_hbm,
    out_hbm,
    index,
    amplitudes,
    load,
    cells,
    forcing,
    forcing_wide,
    table,
    field,
    rows,
    modes,
    packed,
    arrived,
    sent,
):
    channels, cell_rows, _ = cells.shape
    width = field.shape[1]
    groups = [(c, width) for c in range(0, channels, width)]
    planes, y_blocks, slab_rows = cell_layout(cell_rows, table.shape[1])
    modes_y = table.shape[0] // 2
    span = planes * slab_rows
    owners, block_rows, _ = out_hbm.shape
    part_rows = block_rows // (channels // width)
    small = [
        pltpu.make_async_copy(source, target, arrived.at[n])
        for n, (source, target) in enumerate(
            [
                (index_any, index),
                (amplitude_hbm, amplitudes),
                (load_hbm, load),
                (forcing_hbm, forcing),
                (table_hbm, table),
            ]
        )
    ]
    large = [
        pltpu.make_async_copy(
            cells_hbm.at[pl.ds(first, count)], cells.at[pl.ds(first, count)], arrived.at[len(small) + n]
        )
        for n, (first, count) in enumerate(groups)
    ]
    for copy in small[:4] + large[:1] + small[4:] + large[1:]:
        copy.start()
    for copy in small[:4]:
        copy.wait()
    amplitude = amplitudes[index[0, 0]]
    forcing_wide[...] = forcing[...].astype(F32)
    small[4].wait()
    leaving = [
        pltpu.make_async_copy(packed.at[g], out_hbm.at[:, pl.ds(g * part_rows, part_rows), :], sent.at[g])
        for g in range(channels // width)
    ]
    for step in range(len(groups) + 1):
        if step < len(groups):
            first, count = groups[step]
            large[step].wait()
            strengths = [amplitude * load[first + c] for c in range(count)]
            for start in range(0, cell_rows, FORCING_ROWS):
                some = pl.ds(start, FORCING_ROWS)
                force = forcing_wide[some, :]
                for c in range(count):
                    field[step % 2, c, some, :] = half_field(cells[first + c, some, :], force, strengths[c])
            for c in range(count):
                for z in range(planes):
                    for j in range(y_blocks):
                        picked = field[step % 2, c, pl.ds(j * planes + z, slab_rows, stride=planes * y_blocks), :]
                        rows[
                            step % 2, pl.ds(c * span + z * slab_rows, slab_rows), pl.ds(j * LANES, LANES)
                        ] = picked.astype(BF16)
        if step > 0:
            first, count = groups[step - 1]
            result = lax.dot_general(
                table[...],
                rows[(step - 1) % 2, pl.ds(0, count * span), :],
                (((1,), (1,)), ((), ())),
                preferred_element_type=F32,
            )
            part, place = divmod(first, width)
            for t in range(count // 2):
                tile = slice(t * LANES, (t + 1) * LANES)
                pair = pair_halves(result[:modes_y, tile], result[modes_y:, tile])
                for n in range(2):
                    modes[part % 2, pl.ds(place + 2 * t + n, modes_y, stride=width), :] = pair[n]
            if place + count == width:
                for d in range(owners):
                    packed[part, d] = modes[part % 2, pl.ds(d * part_rows, part_rows), :].astype(BF16)
                leaving[part].start()
    for copy in leaving:
        copy.wait()


def y_modes(amp_index, amplitudes, load, cells, forcing, slabs, modes_y, length_y):
    channels, cell_rows, _ = cells.shape
    width = SUBLANES
    parts = channels // width
    owners = slabs // 2
    block_rows = modes_y // owners * channels
    table = forward_y_table(modes_y, length_y, slabs)
    planes, _, slab_rows = cell_layout(cell_rows, length_y)
    operands = in_hbm(amplitudes, load, cells, forcing, table)
    anywhere = pl.BlockSpec(memory_space=pl.ANY)
    return pl.pallas_call(
        y_modes_kernel,
        in_specs=[anywhere] * (1 + len(operands)),
        out_specs=anywhere,
        out_shape=jax.ShapeDtypeStruct((owners, block_rows, LANES), BF16),
        scratch_shapes=[
            SMEM(amp_index.shape, jnp.int32),
            SMEM(amplitudes.shape, F32),
            SMEM(load.shape, F32),
            pltpu.VMEM(cells.shape, BF16),
            pltpu.VMEM(forcing.shape, BF16),
            pltpu.VMEM(forcing.shape, F32),
            pltpu.VMEM(table.shape, BF16),
            pltpu.VMEM((2, width, cell_rows, LANES), F32),
            pltpu.VMEM((2, width * planes * slab_rows, length_y), BF16),
            pltpu.VMEM((2, modes_y * width, LANES), F32),
            pltpu.VMEM((parts, owners, block_rows // parts, LANES), BF16),
            pltpu.SemaphoreType.DMA((5 + parts,)),
            pltpu.SemaphoreType.DMA((parts,)),
        ],
        compiler_params=pltpu.CompilerParams(vmem_limit_bytes=12 * 1024 * 1024),
        cost_estimate=pl.CostEstimate(
            flops=4 * modes_y * cells.size, bytes_accessed=4 * cells.size, transcendentals=cells.size
        ),
        name="y_modes",
    )(amp_index, *operands)


def prepare_kernel(
    half_ref,
    own_any,
    other_any,
    amplitude_ref,
    load_ref,
    weight_ref,
    forward_hbm,
    inverse_hbm,
    strengths,
    weights,
    forward,
    inverse,
    wide,
    indices,
    arrived,
):
    half, me = half_ref[0], half_ref[1]
    copies = [
        pltpu.make_async_copy(forward_hbm.at[half], forward, arrived.at[0]),
        pltpu.make_async_copy(inverse_hbm, inverse, arrived.at[1]),
        pltpu.make_async_copy(own_any, indices.at[pl.ds(0, 1)], arrived.at[2]),
        pltpu.make_async_copy(other_any, indices.at[pl.ds(1, 1)], arrived.at[3]),
    ]
    for copy in copies:
        copy.start()
    local_modes, parts, channels, _, _ = weight_ref.shape
    for k in range(local_modes // 2):
        for r in range(parts):
            for o in range(channels):
                pair = [weight_ref[2 * k + n, r, o].astype(F32) for n in range(2)]
                wide[k, r, pl.ds(o, channels, stride=channels), :] = jnp.concatenate(pair, axis=1)
    weights[...] = wide[...].astype(BF16)
    for copy in copies:
        copy.wait()
    for m in range(2):
        amplitude = amplitude_ref[indices[lax.rem(me + m, 2), 0]]
        for c in range(channels):
            strengths[m * channels + c] = amplitude * load_ref[c]


def prepare(place, own, other, amplitudes, load, spectral_weight, length_x, slabs, planes):
    local_modes, parts, channels, _, modes_x = spectral_weight.shape
    forward = forward_x_table(modes_x, length_x, slabs, planes)
    inverse = inverse_x_table(modes_x, length_x, slabs, planes)
    wide = (local_modes // 2, parts, channels * channels, 2 * modes_x)
    vmem = pl.BlockSpec(memory_space=pltpu.VMEM)
    smem = pl.BlockSpec(memory_space=SMEM)
    anywhere = pl.BlockSpec(memory_space=pl.ANY)
    return pl.pallas_call(
        prepare_kernel,
        in_specs=[smem] + [anywhere] * 2 + [smem] * 2 + [vmem] + [anywhere] * 2,
        out_specs=[smem] + [vmem] * 3,
        out_shape=[
            jax.ShapeDtypeStruct((2 * channels,), F32),
            pltpu.VMEM(wide, BF16),
            pltpu.VMEM(forward.shape[1:], BF16),
            pltpu.VMEM(inverse.shape, BF16),
        ],
        scratch_shapes=[pltpu.VMEM(wide, F32), SMEM((2, 1), jnp.int32), pltpu.SemaphoreType.DMA((4,))],
        compiler_params=pltpu.CompilerParams(vmem_limit_bytes=16 * 1024 * 1024),
        cost_estimate=pl.CostEstimate(
            flops=4 * spectral_weight.size, bytes_accessed=10 * spectral_weight.size, transcendentals=0
        ),
        name="prepare",
    )(place, own, other, amplitudes, load, *in_hbm(spectral_weight, forward, inverse))


def spectrum_kernel(half_ref, pencil_ref, forward_ref, out_ref):
    sources, block_rows, _ = pencil_ref.shape
    rows = out_ref.shape[0]
    parts = rows // PART_ROWS
    picked = []
    for part in range(parts):
        start = pl.multiple_of((2 * part + half_ref[0]) * PART_ROWS, PART_ROWS)
        picked.append(
            jnp.concatenate([pencil_ref[s, pl.ds(start, PART_ROWS), :] for s in range(sources)], axis=1)
        )
    result = jnp.dot(jnp.concatenate(picked, axis=0), forward_ref[...], preferred_element_type=F32)
    out_ref[...] = result.astype(out_ref.dtype)


def partial_spectrum(half, pencil, forward, dtype):
    _, block_rows, _ = pencil.shape
    vmem = pl.BlockSpec(memory_space=pltpu.VMEM)
    return pl.pallas_call(
        spectrum_kernel,
        in_specs=[pl.BlockSpec(memory_space=SMEM), vmem, vmem],
        out_specs=vmem,
        out_shape=jax.ShapeDtypeStruct((block_rows // 2, forward.shape[1]), dtype),
        compiler_params=pltpu.CompilerParams(vmem_limit_bytes=8 * 1024 * 1024),
        cost_estimate=pl.CostEstimate(
            flops=block_rows * forward.size, bytes_accessed=2 * pencil.size, transcendentals=0
        ),
        name="partial_spectrum",
    )(half, pencil, forward)


def mix_kernel(limit_ref, own_ref, other_ref, weight_ref, inverse_ref, out_hbm, spectrum, mixed, packed, sent):
    block_rows, _ = own_ref.shape
    pairs, _, _, width = weight_ref.shape
    local_modes = 2 * pairs
    channels = block_rows // local_modes
    planes = own_ref.shape[1] // width
    groups = channels // SUBLANES
    block = SUBLANES * 2 * local_modes
    low = low_half((SUBLANES, width))
    result = own_ref[...] + other_ref[...].astype(F32)
    for z in range(planes):
        lanes = slice(z * width, (z + 1) * width)
        for part in range(groups):
            for k in range(pairs):
                start = (part * local_modes + 2 * k) * SUBLANES
                real, imag = pair_halves(
                    result[start : start + SUBLANES, lanes], result[start + SUBLANES : start + 2 * SUBLANES, lanes]
                )
                spectrum[k, z, 0, pl.ds(part * SUBLANES, SUBLANES), :] = real
                spectrum[k, z, 1, pl.ds(part * SUBLANES, SUBLANES), :] = imag
    for k in range(pairs):
        keep = [jnp.where(limit_ref[0] > 2 * k + n, 1.0, 0.0).astype(F32) for n in range(2)]
        sums = [[[None, None] for _ in range(groups)] for _ in range(planes)]
        for i in range(channels):
            values = [
                [jnp.broadcast_to(spectrum[k, z, r, pl.ds(i, 1), :], (SUBLANES, width)) for r in range(2)]
                for z in range(planes)
            ]
            weights = [weight_ref[k, r, pl.ds(i * channels, channels), :].astype(F32) for r in range(2)]
            for g in range(groups):
                real, imag = (w[g * SUBLANES : (g + 1) * SUBLANES] for w in weights)
                for z in range(planes):
                    terms = (
                        real * values[z][0] - imag * values[z][1],
                        real * values[z][1] + imag * values[z][0],
                    )
                    for r in range(2):
                        old = sums[z][g][r]
                        sums[z][g][r] = terms[r] if old is None else old + terms[r]
        for z in range(planes):
            for g in range(groups):
                modes = pair_halves(*sums[z][g])
                for n in range(2):
                    kept = modes[n] * keep[n]
                    swapped = half_turn(kept)
                    start = g * block + 2 * k + n
                    mixed[z, pl.ds(start, SUBLANES, stride=2 * local_modes), :] = kept
                    mixed[z, pl.ds(start + local_modes, SUBLANES, stride=2 * local_modes), :] = jnp.where(
                        low, swapped, -swapped
                    )
    left = jnp.concatenate([mixed[z].astype(BF16) for z in range(planes)], axis=1)
    members = groups // 2
    leaving = []
    for t in range(inverse_ref.shape[1] // LANES):
        if t % 2 == 0:
            pair_of = slice(t * LANES, (t + 2) * LANES)
            wide = jnp.dot(left, inverse_ref[:, pair_of], preferred_element_type=F32)
        back = wide[:, (t % 2) * LANES : (t % 2 + 1) * LANES]
        for h in range(members):
            start = 2 * h * block
            pair = pair_halves(back[start : start + block], back[start + block : start + 2 * block])
            for n in range(2):
                packed[(2 * t + n) * members + h] = pair[n].astype(BF16)
        blocks = pl.ds(2 * t * members, 2 * members)
        copy = pltpu.make_async_copy(packed.at[blocks], out_hbm.at[blocks], sent.at[t])
        copy.start()
        leaving.append(copy)
    for copy in leaving:
        copy.wait()


def mix(limit, own, other, weights, inverse, slabs, members):
    block_rows, _ = own.shape
    pairs, _, _, width = weights.shape
    channels = block_rows // (2 * pairs)
    planes = own.shape[1] // width
    rows = channels * 4 * pairs
    blocks = (slabs * members, SUBLANES * 4 * pairs, LANES)
    vmem = pl.BlockSpec(memory_space=pltpu.VMEM)
    return pl.pallas_call(
        mix_kernel,
        in_specs=[pl.BlockSpec(memory_space=SMEM)] + [vmem] * 4,
        out_specs=pl.BlockSpec(memory_space=pl.ANY),
        out_shape=jax.ShapeDtypeStruct(blocks, BF16),
        scratch_shapes=[
            pltpu.VMEM((pairs, planes, 2, channels, width), F32),
            pltpu.VMEM((planes, rows, width), F32),
            pltpu.VMEM(blocks, BF16),
            pltpu.SemaphoreType.DMA((slabs // 2,)),
        ],
        compiler_params=pltpu.CompilerParams(vmem_limit_bytes=8 * 1024 * 1024),
        cost_estimate=pl.CostEstimate(
            flops=2 * rows * inverse.size, bytes_accessed=4 * weights.size, transcendentals=0
        ),
        name="mix",
    )(limit, own, other, weights, inverse)


def pointwise_kernel(
    place_ref, strength_ref, bias_ref, weight_ref, base_ref, forcing_ref, out_ref, spread, native
):
    members, inner, out_rows, length_y = out_ref.shape
    channels, cell_rows, _ = base_ref.shape
    outer = channels // (members * inner)
    planes, y_blocks, slab_rows = cell_layout(cell_rows, length_y)
    depth = 2 * SUBLANES
    out_channels = channels // members
    me = place_ref[1]

    def spread_weight():
        tall = (out_channels * depth, channels)
        wide = (channels, channels * depth)
        row_of = lax.broadcasted_iota(jnp.int32, tall, 0) // depth + me * out_channels
        pick_rows = (row_of == lax.broadcasted_iota(jnp.int32, tall, 1)).astype(BF16)
        column_of = lax.broadcasted_iota(jnp.int32, wide, 1) // depth
        pick_columns = (column_of == lax.broadcasted_iota(jnp.int32, wide, 0)).astype(BF16)
        picked = jnp.dot(pick_rows, weight_ref[...], preferred_element_type=F32).astype(BF16)
        full = jnp.dot(picked, pick_columns, preferred_element_type=F32)
        same = lax.broadcasted_iota(jnp.int32, full.shape, 0) % depth == (
            lax.broadcasted_iota(jnp.int32, full.shape, 1) % depth
        )
        spread[...] = jnp.where(same, 2.0 * full, 0.0).astype(BF16)

    spread_weight()

    def body(step, carry):
        rows = pl.ds(pl.multiple_of(step * depth, depth), depth)
        forcing = forcing_ref[rows, :].astype(F32)
        fields = []
        for m in range(members):
            parts = [
                half_field(base_ref[c, rows, :], forcing, strength_ref[m * channels + c]).astype(BF16)
                for c in range(channels)
            ]
            fields.append(jnp.concatenate(parts, axis=0))
        result = jnp.dot(spread[...], jnp.concatenate(fields, axis=1), preferred_element_type=F32)
        for a in range(outer):
            for b in range(inner):
                o = a * inner + b
                bias = bias_ref[me * out_channels + o]
                for m in range(members):
                    cells = result[o * depth : (o + 1) * depth, m * LANES : (m + 1) * LANES] + bias
                    native[m, a, b, rows, :] = cells
        return carry

    lax.fori_loop(0, cell_rows // depth, body, 0)

    def arrange(b, carry):
        for m in range(members):
            for a in range(outer):
                for z in range(planes):
                    rows = pl.ds((a * planes + z) * slab_rows, slab_rows)
                    for j in range(y_blocks):
                        picked = native[m, a, b, pl.ds(j * planes + z, slab_rows, stride=planes * y_blocks), :]
                        out_ref[m, b, rows, pl.ds(j * LANES, LANES)] = picked.astype(BF16)
        return carry

    lax.fori_loop(0, inner, arrange, 0)


def pointwise(place, strengths, bias, weight, cells, forcing, length_y):
    channels, cell_rows, _ = cells.shape
    members = strengths.shape[0] // channels
    depth = 2 * SUBLANES
    inner = SUBLANES
    outer = channels // members // inner
    spread = (channels // members * depth, channels * depth)
    smem = pl.BlockSpec(memory_space=SMEM)
    vmem = pl.BlockSpec(memory_space=pltpu.VMEM)
    return pl.pallas_call(
        pointwise_kernel,
        in_specs=[smem] * 3 + [vmem] * 3,
        out_specs=vmem,
        out_shape=pltpu.VMEM((members, inner, outer * cell_rows * LANES // length_y, length_y), BF16),
        scratch_shapes=[
            pltpu.VMEM(spread, BF16),
            pltpu.VMEM((members, outer, inner, cell_rows, LANES), F32),
        ],
        compiler_params=pltpu.CompilerParams(vmem_limit_bytes=16 * 1024 * 1024),
        cost_estimate=pl.CostEstimate(
            flops=4 * spread[0] * spread[1] * members * cell_rows // depth * LANES,
            bytes_accessed=8 * cells.size,
            transcendentals=members * cells.size,
        ),
        name="pointwise",
    )(place, strengths, bias, weight, *in_hbm(cells, forcing))


def layer_kernel(back_ref, table_ref, point_ref, out_hbm, columns, native, result, sent):
    members, inner, rows, length_y = point_ref.shape
    _, outer, cell_rows, _ = native.shape
    sources, block_rows, _ = back_ref.shape
    slabs = sources // members
    depth = block_rows // inner
    planes, y_blocks, slab_rows = cell_layout(cell_rows, length_y)
    leaving = [pltpu.make_async_copy(result.at[:, b], out_hbm.at[:, b], sent.at[b]) for b in range(inner)]
    for m in range(members):
        for s in range(slabs):
            block = back_ref[s * members + m].astype(F32)
            for b in range(inner):
                columns[b, m, pl.ds(s * depth, depth), :] = block[b * depth : (b + 1) * depth]
    for b in range(inner):
        turn = b % 2
        total = None
        for m in range(members):
            spectral = lax.dot_general(
                columns[b, m].astype(BF16), table_ref[...], (((0,), (0,)), ((), ())), preferred_element_type=F32
            )
            value = double_gelu(point_ref[m, b].astype(F32) + spectral)
            total = value if total is None else total + value
        total = total * (0.5 / members)
        for a in range(outer):
            for z in range(planes):
                start = (a * planes + z) * slab_rows
                for j in range(y_blocks):
                    native[turn, a, pl.ds(j * planes + z, slab_rows, stride=planes * y_blocks), :] = total[
                        start : start + slab_rows, j * LANES : (j + 1) * LANES
                    ]
        for a in range(outer):
            result[a, b] = native[turn, a].astype(BF16)
        leaving[b].start()
    for copy in leaving:
        copy.wait()


def layer(back, points, outer, length_x, modes_y, slabs):
    members, inner, rows, length_y = points.shape
    cell_rows = rows * length_y // (outer * LANES)
    table = inverse_y_table(modes_y, length_y, length_x, slabs)
    vmem = pl.BlockSpec(memory_space=pltpu.VMEM)
    return pl.pallas_call(
        layer_kernel,
        in_specs=[vmem, vmem, vmem],
        out_specs=pl.BlockSpec(memory_space=pl.ANY),
        out_shape=pltpu.HBM((outer, inner, cell_rows, LANES), BF16),
        scratch_shapes=[
            pltpu.VMEM((inner, members, 2 * modes_y, LANES), F32),
            pltpu.VMEM((2, outer, cell_rows, LANES), F32),
            pltpu.VMEM((outer, inner, cell_rows, LANES), BF16),
            pltpu.SemaphoreType.DMA((inner,)),
        ],
        compiler_params=pltpu.CompilerParams(vmem_limit_bytes=16 * 1024 * 1024),
        cost_estimate=pl.CostEstimate(
            flops=4 * modes_y * points.size, bytes_accessed=5 * points.size, transcendentals=points.size
        ),
        name="layer",
    )(back, table, points)


def fast_local(
    base_field,
    forcing,
    load,
    amplitudes,
    amp_index,
    mode_count,
    point_weight,
    point_bias,
    spectral_weight,
):
    channels, slab_rows, planes, length_y = base_field.shape
    slabs, members = lax.axis_size("slab"), lax.axis_size("member")
    local_modes, modes_x = spectral_weight.shape[:2]
    modes_y = local_modes * slabs
    length_x = slab_rows * slabs
    y_blocks = length_y // LANES
    cells = base_field.reshape(channels, slab_rows, planes, y_blocks, LANES).transpose(0, 1, 3, 2, 4)
    cells = cells.reshape(channels, slab_rows * SUBLANES, LANES)
    force = forcing.reshape(slab_rows, planes, y_blocks, LANES).transpose(0, 2, 1, 3)
    force = force.reshape(slab_rows * SUBLANES, LANES)
    owners = slabs // 2
    slab, me = lax.axis_index("slab"), lax.axis_index("member")
    half = slab // owners
    place = jnp.stack([half, me])
    other_half = jnp.reshape(1 - half, (1,))
    partners = [(n, (n + owners) % slabs) for n in range(slabs)]
    index = amp_index.reshape(1, 1)
    other_index = lax.ppermute(index, "member", [(n, 1 - n) for n in range(2)])
    out_channels = channels // members
    packed = y_modes(index, amplitudes, load, cells, force, slabs, modes_y, length_y)
    pencil = lax.all_to_all(
        packed,
        "slab",
        split_axis=0,
        concat_axis=0,
        tiled=True,
        axis_index_groups=[[h * owners + n for n in half_order(owners)] for h in range(2)],
    )
    strengths, weights, forward, inverse = prepare(
        place, index, other_index, amplitudes, load, spectral_weight.transpose(0, 2, 3, 4, 1), length_x, slabs, planes
    )
    leaving = partial_spectrum(other_half, pencil, forward, BF16)
    other = lax.ppermute(leaving, "slab", partners)
    own = partial_spectrum(place, pencil, forward, F32)
    back = mix(mode_count - slab * local_modes, own, other, weights, inverse, slabs, members)
    back = lax.all_to_all(back, ("slab", "member"), split_axis=0, concat_axis=0, tiled=True)
    points = pointwise(place, strengths, point_bias, point_weight, cells, force, length_y)
    result = layer(back, points, out_channels // SUBLANES, length_x, modes_y, slabs)
    result = result.reshape(out_channels, slab_rows, y_blocks, planes, LANES).transpose(0, 1, 3, 2, 4)
    return result.reshape(out_channels, slab_rows, planes, length_y)


def tiles_fit(base_shape, weight_shape, slabs, members):
    channels, slab_rows, planes, length_y = base_shape
    local_modes, modes_x = weight_shape[:2]
    return (
        2 * planes * slab_rows == LANES
        and 2 * modes_x == LANES
        and planes * length_y == SUBLANES * LANES
        and 2 * local_modes == SUBLANES
        and 2 * SUBLANES * members == channels
        and slabs % 4 == 0
    )


def phases(frequency, positions, length):
    product = frequency[:, None] * positions[None, :] % length
    angles = product.astype(jnp.float32) * (TWO_PI / length)
    return (jnp.cos(angles), jnp.sin(angles))


def forward_x(pencil, cos_table, sin_table):
    row_total = pencil.shape[0]
    modes = cos_table.shape[0]
    with_cos = jnp.einsum(
        "kxf,mx->kmf", pencil, cos_table, preferred_element_type=jnp.float32
    ).reshape(row_total, modes, 2, -1)
    with_sin = jnp.einsum(
        "kxf,mx->kmf", pencil, sin_table, preferred_element_type=jnp.float32
    ).reshape(row_total, modes, 2, -1)
    real_part = with_cos[:, :, 0] + with_sin[:, :, 1]
    imag_part = with_cos[:, :, 1] - with_sin[:, :, 0]
    return jnp.stack([real_part, imag_part], axis=2).reshape(row_total, modes, -1)


def inverse_x(spectra, cos_table, sin_table):
    row_total = spectra.shape[0]
    points = cos_table.shape[1]
    with_cos = jnp.einsum(
        "kmf,mx->kxf", spectra, cos_table, preferred_element_type=jnp.float32
    ).reshape(row_total, points, 2, -1)
    with_sin = jnp.einsum(
        "kmf,mx->kxf", spectra, sin_table, preferred_element_type=jnp.float32
    ).reshape(row_total, points, 2, -1)
    real_part = with_cos[:, :, 0] - with_sin[:, :, 1]
    imag_part = with_cos[:, :, 1] + with_sin[:, :, 0]
    return jnp.stack([real_part, imag_part], axis=2).reshape(row_total, points, -1)


def mixing(weights, values):
    return jnp.einsum("kmoi,kmiz->kmoz", weights, values, preferred_element_type=jnp.float32)


def general_local(
    base_field,
    forcing,
    load,
    amplitudes,
    amp_index,
    mode_count,
    point_weight,
    point_bias,
    spectral_weight,
):
    channels, slab_rows, plane_count, length_y = base_field.shape
    slab_count = lax.axis_size("slab")
    local_modes = spectral_weight.shape[0]
    modes_y = local_modes * slab_count
    modes_x = spectral_weight.shape[1]
    length_x = slab_rows * slab_count
    packed_width = 2 * channels * plane_count
    slab_index = lax.axis_index("slab")
    level_ids = jnp.arange(amplitudes.shape[0], dtype=jnp.int32)
    amplitude = jnp.sum(jnp.where(level_ids == amp_index[0], amplitudes, 0.0))
    driven = base_field.astype(jnp.float32) + amplitude * load[:, None, None, None] * forcing[
        None
    ].astype(jnp.float32)
    field_now = (2.0 * jnp.tanh(0.5 * driven)).astype(jnp.bfloat16)
    y_cos, y_sin = phases(
        jnp.arange(modes_y, dtype=jnp.int32), jnp.arange(length_y, dtype=jnp.int32), length_y
    )
    y_real = jnp.einsum(
        "cxzy,ky->kxcz", field_now, y_cos.astype(jnp.bfloat16), preferred_element_type=jnp.float32
    )
    y_imag = -jnp.einsum(
        "cxzy,ky->kxcz", field_now, y_sin.astype(jnp.bfloat16), preferred_element_type=jnp.float32
    )
    packed = (
        jnp.stack([y_real, y_imag], axis=2)
        .astype(jnp.bfloat16)
        .reshape(modes_y, slab_rows, packed_width)
    )
    frequency_x = jnp.concatenate(
        [
            jnp.arange(modes_x // 2, dtype=jnp.int32),
            jnp.arange(length_x - modes_x // 2, length_x, dtype=jnp.int32),
        ]
    )
    full_cos, full_sin = phases(frequency_x, jnp.arange(length_x, dtype=jnp.int32), length_x)
    full_cos = full_cos.astype(jnp.bfloat16)
    full_sin = full_sin.astype(jnp.bfloat16)
    pencil = lax.all_to_all(packed, "slab", split_axis=0, concat_axis=1, tiled=True)
    spectrum = forward_x(pencil, full_cos, full_sin)
    spectrum = spectrum.astype(jnp.bfloat16).reshape(local_modes, modes_x, 2, channels, plane_count)
    weight_real = spectral_weight[:, :, 0]
    weight_imag = spectral_weight[:, :, 1]
    spec_real = spectrum[:, :, 0]
    spec_imag = spectrum[:, :, 1]
    mix_real = mixing(weight_real, spec_real) - mixing(weight_imag, spec_imag)
    mix_imag = mixing(weight_real, spec_imag) + mixing(weight_imag, spec_real)
    global_modes = slab_index * local_modes + jnp.arange(local_modes, dtype=jnp.int32)
    keep = (global_modes < mode_count[0]).astype(jnp.float32)[:, None, None, None, None]
    mixed = (
        (jnp.stack([mix_real, mix_imag], axis=2) * keep)
        .astype(jnp.bfloat16)
        .reshape(local_modes, modes_x, packed_width)
    )
    back = inverse_x(mixed, full_cos, full_sin).astype(jnp.bfloat16)
    returned = lax.all_to_all(back, "slab", split_axis=1, concat_axis=0, tiled=True)
    returned = returned.reshape(modes_y, slab_rows, 2, channels, plane_count)
    weights_y = jnp.where(jnp.arange(modes_y) == 0, 1.0, 2.0).astype(jnp.float32) / (
        length_x * length_y
    )
    back_cos = (weights_y[:, None] * y_cos).astype(jnp.bfloat16)
    back_sin = (weights_y[:, None] * y_sin).astype(jnp.bfloat16)
    spectral = jnp.einsum(
        "kxcz,ky->cxzy", returned[:, :, 0], back_cos, preferred_element_type=jnp.float32
    )
    spectral = spectral - jnp.einsum(
        "kxcz,ky->cxzy", returned[:, :, 1], back_sin, preferred_element_type=jnp.float32
    )
    pointwise = (
        jnp.einsum("oc,cxzy->oxzy", point_weight, field_now, preferred_element_type=jnp.float32)
        + point_bias[:, None, None, None]
    )
    layer = jax.nn.gelu(pointwise + spectral, approximate=True).astype(jnp.bfloat16)
    layer = lax.optimization_barrier(layer).astype(jnp.float32)
    total = lax.psum_scatter(
        layer.astype(jnp.bfloat16), "member", scatter_dimension=0, tiled=True
    ).astype(jnp.float32)
    return (total / lax.axis_size("member")).astype(jnp.bfloat16)


def local(base_field, forcing, load, amplitudes, amp_index, mode_count, point_weight, point_bias, spectral_weight):
    fits = tiles_fit(
        base_field.shape, spectral_weight.shape, lax.axis_size("slab"), lax.axis_size("member")
    )
    return (fast_local if fits else general_local)(
        base_field,
        forcing,
        load,
        amplitudes,
        amp_index,
        mode_count,
        point_weight,
        point_bias,
        spectral_weight,
    )


def solution(mesh):
    in_specs = (
        P(None, "slab", None, None),
        P("slab", None, None),
        P(),
        P(),
        P("member"),
        P("member"),
        P(),
        P(),
        P("slab", None, None, None, None),
    )
    out_specs = P("member", "slab", None, None)
    return jax.shard_map(local, mesh=mesh, in_specs=in_specs, out_specs=out_specs, check_vma=False)
```
